32 devices in a mesh: dp: 8 (over z, x), ffn: 4 (over y, core).
Axes of the slice: x: 2, y: 2, z: 4, core: 2. Of those that a mesh axis runs over, the one named last changes fastest.
Arguments:
- inputs: bfloat16 [4, 32, 512, 768], P(None, ('dp', 'ffn')), may hold values from -6 to 6
- doc_ids: int32 [4, 32, 512], P(None, ('dp', 'ffn')), may hold values from 0 to 3, never falling along the last dimension, each value on 1 to 192 neighbouring positions
- cotangent: bfloat16 [4, 32, 512, 768], P(None, ('dp', 'ffn')), may hold values from -6 to 6
- query_weight: bfloat16 [4, 192, 192], replicated, may hold values from -0.875 to 0.875
- query_bias: bfloat16 [768], replicated, may hold values from -3 to 3
- key_weight: bfloat16 [4, 192, 192], replicated, may hold values from -0.4375 to 0.4375
- value_weight: bfloat16 [4, 192, 192], replicated, may hold values from -0.4375 to 0.4375
- value_bias: bfloat16 [768], replicated, may hold values from -3 to 3
- out_weight: bfloat16 [768, 768], replicated, may hold values from -0.875 to 0.875
- out_bias: bfloat16 [768], replicated, may hold values from -3 to 3
- mixed_gain: float32 [768], replicated, may hold values from 0.5 to 1.5
- mixed_bias: float32 [768], replicated, may hold values from -2 to 2
- expand_weight: bfloat16 [4, 192, 768], P(None, None, 'ffn'), may hold values from -0.4375 to 0.4375
- expand_bias: bfloat16 [4, 768], P(None, 'ffn'), may hold values from -3 to 3
- shrink_weight: bfloat16 [4, 768, 192], P(None, 'ffn'), may hold values from -0.21875 to 0.21875
- shrink_bias: bfloat16 [768], replicated, may hold values from -3 to 3
- final_gain: float32 [768], replicated, may hold values from 0.5 to 1.5
- final_bias: float32 [768], replicated, may hold values from -2 to 2
Outputs:
- result: bfloat16 [4, 32, 512, 768], P(None, ('dp', 'ffn'))
- input_grad: bfloat16 [4, 32, 512, 768], P(None, ('dp', 'ffn'))
- grad_query_weight: float32 [4, 192, 192], replicated
- grad_query_bias: float32 [768], replicated
- grad_key_weight: float32 [4, 192, 192], replicated
- grad_value_weight: float32 [4, 192, 192], replicated
- grad_value_bias: float32 [768], replicated
- grad_out_weight: float32 [768, 768], replicated
- grad_out_bias: float32 [768], replicated
- grad_mixed_gain: float32 [768], replicated
- grad_mixed_bias: float32 [768], replicated
- grad_expand_weight: float32 [4, 192, 768], P(None, None, 'ffn')
- grad_expand_bias: float32 [4, 768], P(None, 'ffn')
- grad_shrink_weight: float32 [4, 768, 192], P(None, 'ffn')
- grad_shrink_bias: float32 [768], replicated
- grad_final_gain: float32 [768], replicated
- grad_final_bias: float32 [768], replicated
The draws below stay inside these ranges and needn't reach their ends.
Inputs may be any that keep to these rules, and one draw needn't show every extreme that they name: `doc_ids`: within each batch row the document numbers never fall; each row has 4 documents, each of 1 to 192 tokens, one of exactly that many.
All inputs are finite; a program needn't handle non-finite values.
Results may differ from the reference program's by a relative error of at most 0.015.
The reference program's roundings to bfloat16 on the way count: a program that leaves them out, or rounds other values in their place, can miss the bound.
Values may be sent and summed in bfloat16 or wider, within the bound.
No kernel may reach another device: no remote copies, remote signals or barrier semaphores. Data moves between devices by JAX's collectives and lax.ppermute only.
A program may use at most 384 MiB of HBM per device.

```python
import math
import jax
import jax.numpy as jnp
import numpy as np
from jax import lax

D = 768
FF = 3072
HEADS = 12
HEAD = 64
GROUPS = 4
LEN = 512
MB = 4
SEQS = 32


def block_levels(own_key, dims, pieces, smallest, largest):
    loudness = 1.0
    for dim, parts in pieces:
        draws = jax.random.uniform(jax.random.fold_in(jax.random.fold_in(own_key, 6), dim), (parts,), jnp.float32, smallest / len(pieces), largest / len(pieces))
        loudness = loudness * jnp.repeat(jnp.exp(draws), dims[dim] // parts).reshape((-1,) + (1,) * (len(dims) - 1 - dim))
    return loudness


def split_up(count, total, limit, skew):
    weights = [(1 << 20) // math.isqrt(standing ** skew) + 1 for standing in range(2, count + 1)]
    surplus, counts = total - limit - (count - 1), [1] * (count - 1)
    while surplus > 0:
        candidates = [i for i in range(count - 1) if counts[i] < limit]
        pool, left = sum([weights[i] for i in candidates]), surplus
        for i in candidates:
            addition = min(limit - counts[i], max(1, left * weights[i] // pool), surplus)
            counts[i] = counts[i] + addition
            surplus = surplus - addition
    return np.array([limit] + counts)


def uneven_parts(rng, number_of, total, reach, lean):
    if number_of == 2:
        one = jax.random.randint(rng, (), max(1, total - reach), min(reach, total - 1) + 1)
        return jnp.stack([one, total - one])
    lengths = jnp.asarray(split_up(number_of, total, reach, lean), jnp.int32)
    twos = (number_of - 1) // 2
    giver, taker = lengths[1:1 + 2 * twos:2], lengths[2:2 + 2 * twos:2]
    room = jnp.minimum(giver - 1, reach - taker)
    shifted = jax.random.randint(jax.random.fold_in(rng, 1), (twos,), 0, 1 << 20) % (room + 1)
    lengths = lengths.at[1:1 + 2 * twos:2].set(giver - shifted).at[2:2 + 2 * twos:2].set(taker + shifted)
    return lengths[jax.random.permutation(jax.random.fold_in(rng, 2), number_of)]


def bell_draw(own_key, extent, scale, most, cuts=(), dtype=jnp.bfloat16):
    level = block_levels(own_key, extent, cuts, -0.22, 0.18) if cuts else 1.0
    entries = jax.random.normal(own_key, extent, jnp.float32) * scale * level
    return jnp.minimum(jnp.maximum(entries, -most), most).astype(dtype)


def setup_inputs(seed: int = 0) -> dict:
    key_list = jax.random.split(jax.random.key(seed), 19)
    inputs = bell_draw(key_list[0], (MB, SEQS, LEN, D), 1.0, 6.0, ((1, 32),))
    doc_ids = jax.vmap(lambda own: jnp.searchsorted(jnp.cumsum(uneven_parts(own, 4, LEN, LEN * 3 // 8, 1)), jnp.arange(LEN), side="right"))(jax.random.split(key_list[1], MB * SEQS)).reshape((MB, SEQS, LEN)).astype(jnp.int32)
    cotangent = bell_draw(key_list[2], (MB, SEQS, LEN, D), 1.0, 6.0, ((1, 32),))
    query_weight = bell_draw(key_list[3], (GROUPS, D // GROUPS, D // GROUPS), (D // 16) ** -0.5, 0.875)
    query_bias = bell_draw(key_list[4], (D,), 0.5, 3.0)
    key_weight = bell_draw(key_list[5], (GROUPS, D // GROUPS, D // GROUPS), (D // GROUPS) ** -0.5, 0.4375)
    value_weight = bell_draw(key_list[6], (GROUPS, D // GROUPS, D // GROUPS), (D // GROUPS) ** -0.5, 0.4375)
    value_bias = bell_draw(key_list[7], (D,), 0.5, 3.0)
    out_weight = bell_draw(key_list[8], (D, D), (D // 16) ** -0.5, 0.875)
    out_bias = bell_draw(key_list[9], (D,), 0.5, 3.0)
    mixed_gain = jnp.clip(1.0 + 0.1 * jax.random.normal(key_list[10], (D,), jnp.float32), 0.5, 1.5)
    mixed_bias = bell_draw(key_list[11], (D,), 0.3, 2.0, (), jnp.float32)
    expand_weight = bell_draw(key_list[12], (GROUPS, D // GROUPS, FF // GROUPS), (D // GROUPS) ** -0.5, 0.4375, ((2, 4),))
    expand_bias = bell_draw(key_list[13], (GROUPS, FF // GROUPS), 0.5, 3.0, ((1, 4),))
    shrink_weight = bell_draw(key_list[14], (GROUPS, FF // GROUPS, D // GROUPS), (FF // GROUPS) ** -0.5, 0.21875, ((1, 4),))
    shrink_bias = bell_draw(key_list[15], (D,), 0.5, 3.0)
    final_gain = jnp.clip(1.0 + 0.1 * jax.random.normal(key_list[16], (D,), jnp.float32), 0.5, 1.5)
    final_bias = bell_draw(key_list[17], (D,), 0.3, 2.0, (), jnp.float32)
    return dict(inputs=inputs, doc_ids=doc_ids, cotangent=cotangent, query_weight=query_weight, query_bias=query_bias, key_weight=key_weight, value_weight=value_weight, value_bias=value_bias, out_weight=out_weight, out_bias=out_bias, mixed_gain=mixed_gain, mixed_bias=mixed_bias, expand_weight=expand_weight, expand_bias=expand_bias, shrink_weight=shrink_weight, shrink_bias=shrink_bias, final_gain=final_gain, final_bias=final_bias)


epsilon = 1e-05
masked_score = -1e+30
highest = lax.Precision.HIGHEST

@jax.custom_vjp
def low(v):
    return lax.optimization_barrier(v.astype(jnp.bfloat16)).astype(jnp.float32)

@jax.custom_vjp
def low_back(v):
    return v

def low_keep(v):
    return (low(v), None)

def low_pass(kept, grad):
    return (grad,)

def back_keep(v):
    return (v, None)

def back_low(kept, grad):
    return (low(grad),)
low.defvjp(low_keep, low_pass)
low_back.defvjp(back_keep, back_low)

def layer_norm(value, gain, offset):
    centered = value - lax.optimization_barrier(jnp.mean(value, axis=-1, keepdims=True))
    variance = lax.optimization_barrier(jnp.mean(centered * centered, axis=-1, keepdims=True))
    return centered * lax.rsqrt(variance + epsilon) * gain + offset

def grouped(inputs, weight):
    groups, width_in, width_out = weight.shape
    parted = inputs.reshape(inputs.shape[0], groups, width_in)
    result = jnp.einsum('tgi,gio->tgo', parted, weight, precision=highest)
    return result.reshape(inputs.shape[0], groups * width_out)

def block_forward(params, inputs, docs):
    query_weight, query_bias, key_weight, value_weight, value_bias, out_weight, out_bias, mixed_gain, mixed_bias, expand_weight, expand_bias, shrink_weight, shrink_bias, final_gain, final_bias = params
    count = inputs.shape[0]
    tokens = inputs.reshape(count * LEN, D)
    query = low(low_back(grouped(tokens, query_weight) + query_bias))
    keys = low(low_back(grouped(tokens, key_weight)))
    values = low(low_back(grouped(tokens, value_weight) + value_bias))
    shape = (count, LEN, HEADS, HEAD)
    scores = jnp.einsum('bqhd,bkhd->bhqk', query.reshape(shape), keys.reshape(shape), precision=highest) * HEAD ** (-0.5)
    scores = low_back(scores)
    same = docs[:, :, None] == docs[:, None, :]
    probs = low(jax.nn.softmax(jnp.where(same[:, None], scores, masked_score), axis=-1))
    context = jnp.einsum('bhqk,bkhd->bqhd', probs, values.reshape(shape), precision=highest)
    context = low(low_back(context.reshape(count * LEN, D)))
    hidden_one = tokens + low_back(jnp.dot(context, out_weight, precision=highest)) + out_bias
    normed = layer_norm(hidden_one, mixed_gain, mixed_bias)
    normed_low = low(normed)
    upper = low_back(grouped(normed_low, expand_weight) + expand_bias.reshape(-1))
    active = low(jax.nn.gelu(upper, approximate=False))
    hidden_two = normed + low_back(grouped(active, shrink_weight)) + shrink_bias
    return layer_norm(hidden_two, final_gain, final_bias).reshape(count, LEN, D)

def reference(inputs, doc_ids, cotangent, query_weight, query_bias, key_weight, value_weight, value_bias, out_weight, out_bias, mixed_gain, mixed_bias, expand_weight, expand_bias, shrink_weight, shrink_bias, final_gain, final_bias):
    params = tuple((weight.astype(jnp.float32) for weight in (query_weight, query_bias, key_weight, value_weight, value_bias, out_weight, out_bias, mixed_gain, mixed_bias, expand_weight, expand_bias, shrink_weight, shrink_bias, final_gain, final_bias)))
    rows = inputs.astype(jnp.float32).reshape(-1, 8, LEN, D)
    doc_rows = doc_ids.reshape(-1, 8, LEN)

    def forward(weights, blocks):

        def single(pair):
            return block_forward(weights, pair[0], pair[1])
        return lax.map(jax.checkpoint(single), (blocks, doc_rows))
    result, backward = jax.vjp(forward, params, rows)
    grads, grad_rows = backward(cotangent.astype(jnp.float32).reshape(rows.shape))
    return (result.reshape(inputs.shape).astype(jnp.bfloat16), grad_rows.reshape(inputs.shape).astype(jnp.bfloat16), grads[0], grads[1], grads[2], grads[3], grads[4], grads[5], grads[6], grads[7], grads[8], grads[9], grads[10], grads[11], grads[12], grads[13], grads[14])
```

```python
import functools

import jax
import jax.numpy as jnp
from jax import lax
from jax.experimental import pallas as pl
from jax.experimental.pallas import tpu as pltpu
from jax.sharding import PartitionSpec as P

HEADS = 12
HEAD = 64
epsilon = 1e-05
masked_score = -1e30
bf16 = jnp.bfloat16
f32 = jnp.float32
VMEM_LIMIT = 60 * 1024 * 1024

NN = (((1,), (0,)), ((), ()))
NT = (((1,), (1,)), ((), ()))
TN = (((0,), (0,)), ((), ()))


def dot(a, b, dims=NN):
    return lax.dot_general(a, b, dims, preferred_element_type=f32)


def window(group, width):
    start = group * width
    base = start // 128 * 128
    return base, start - base


def shift_matrix(rows, cols, offset):
    r = lax.broadcasted_iota(jnp.int32, (rows, cols), 0)
    c = lax.broadcasted_iota(jnp.int32, (rows, cols), 1)
    return jnp.where(c == r + offset, 1.0, 0.0).astype(bf16)


def pad_cols(w, offset):
    return dot(w, shift_matrix(w.shape[1], 256, offset)).astype(bf16)


def pad_rows(w, offset):
    rows = w.shape[0]
    parts = []
    if offset:
        parts.append(jnp.zeros((offset, w.shape[1]), bf16))
    parts.append(w)
    if 256 - offset - rows:
        parts.append(jnp.zeros((256 - offset - rows, w.shape[1]), bf16))
    return jnp.concatenate(parts, axis=0)


def join_windows(parts):
    out = []
    for i in range(0, len(parts), 2):
        a, b = parts[i], parts[i + 1]
        out += [a[:, :128], a[:, 128:] + b[:, :128], b[:, 128:]]
    return out


def attend_kernel(x_ref, docs_ref, wq_ref, qb_ref, wk_ref, wv_ref, vb_ref,
                  q_ref, k_ref, v_ref, c_ref, p_ref, wpad, bias_ref):
    length = x_ref.shape[1]
    width = x_ref.shape[2]
    groups = wq_ref.shape[0]
    per = width // groups

    @pl.when(pl.program_id(0) == 0)
    def _():
        for j, w_ref in enumerate((wq_ref, wk_ref, wv_ref)):
            for g in range(groups):
                _, off = window(g, per)
                wpad[j, g] = pad_rows(pad_cols(w_ref[g], off), off)

    for j, (out, b_ref) in enumerate(((q_ref, qb_ref), (k_ref, None), (v_ref, vb_ref))):
        parts = []
        for g in range(groups):
            base, _ = window(g, per)
            parts.append(dot(x_ref[0, :, base:base + 256], wpad[j, g]))
        for n, col in enumerate(join_windows(parts)):
            if b_ref is not None:
                col = col + b_ref[:, 128 * n:128 * n + 128].astype(f32)
            out[0, :, 128 * n:128 * n + 128] = col.astype(bf16)

    docs = docs_ref[0].astype(f32)
    down = jnp.transpose(jnp.broadcast_to(docs, (128, length)))[:, :1]
    bias_ref[...] = jnp.where(down == docs, 0.0, masked_score)
    low = lax.broadcasted_iota(jnp.int32, (1, 128), 1) < HEAD
    for pair in range(HEADS // 2):
        lanes = slice(128 * pair, 128 * pair + 128)
        q2 = q_ref[0, :, lanes] * bf16(HEAD ** -0.5)
        k2 = k_ref[0, :, lanes]
        v2 = v_ref[0, :, lanes]
        acc = None
        for h in range(2):
            half = low if h == 0 else jnp.logical_not(low)
            km = jnp.where(half, k2, bf16(0))
            vm = jnp.where(half, v2, bf16(0))
            s = dot(q2, km, NT) + bias_ref[...]
            top = jnp.max(s, axis=-1, keepdims=True)
            e = jnp.exp(s - top)
            total = jnp.sum(e, axis=-1, keepdims=True)
            pr = (e * (1.0 / total)).astype(bf16)
            p_ref[0, 2 * pair + h] = pr
            c = dot(pr, vm)
            acc = c if acc is None else acc + c
        c_ref[0, :, lanes] = acc.astype(bf16)


def full(shape):
    return pl.BlockSpec(shape, lambda *_: (0,) * len(shape))


def row_spec(shape):
    return pl.BlockSpec((1,) + shape, lambda r: (r,) + (0,) * len(shape))


def attend(x, docs, wq, qb, wk, wv, vb):
    rows, length, width = x.shape
    wide = row_spec((length, width))
    low = jax.ShapeDtypeStruct((rows, length, width), bf16)
    return pl.pallas_call(
        attend_kernel,
        grid=(rows,),
        in_specs=[wide, row_spec((1, length)), full(wq.shape), full(qb.shape), full(wk.shape),
                  full(wv.shape), full(vb.shape)],
        out_specs=[wide, wide, wide, wide, row_spec((HEADS, length, length))],
        out_shape=[low, low, low, low, jax.ShapeDtypeStruct((rows, HEADS, length, length), bf16)],
        scratch_shapes=[pltpu.VMEM((3, wq.shape[0], 256, 256), bf16), pltpu.VMEM((length, length), f32)],
        compiler_params=pltpu.CompilerParams(vmem_limit_bytes=VMEM_LIMIT),
        cost_estimate=pl.CostEstimate(flops=int(2e10), bytes_accessed=int(5e7), transcendentals=0),
        name="attend",
    )(x, docs, wq, qb, wk, wv, vb)


def gelu_both(u):
    cdf = 0.5 * (1.0 + lax.erf(u * 0.7071067811865476))
    pdf = jnp.exp(-0.5 * u * u) * 0.3989422804014327
    return u * cdf, cdf + u * pdf


def feed_kernel(x_ref, c_ref, e_ref, wo_ref, we_ref, be_ref, ws_ref, vec_ref,
                result_ref, dh1_ref, dc_ref, gwo_ref, gwe_ref, gws_ref, gbe_ref, gvec_ref,
                wepad, wspad, act, slope, pre_low, df_low, wo_t):
    step = pl.program_id(0)
    shards = we_ref.shape[0]
    groups = we_ref.shape[1]
    part = we_ref.shape[3]
    per = we_ref.shape[2]
    hidden = shards * part
    width = x_ref.shape[2]

    @pl.when(step == 0)
    def _():
        gwo_ref[...] = jnp.zeros(gwo_ref.shape, f32)
        gwe_ref[...] = jnp.zeros(gwe_ref.shape, f32)
        gws_ref[...] = jnp.zeros(gws_ref.shape, f32)
        gbe_ref[...] = jnp.zeros(gbe_ref.shape, f32)
        gvec_ref[...] = jnp.zeros(gvec_ref.shape, f32)
        for g in range(groups):
            _, off = window(g, per)
            w = jnp.concatenate([we_ref[s, g].astype(f32) for s in range(shards)], axis=1).astype(bf16)
            wepad[g] = pad_rows(w, off)
            wspad[g] = jnp.concatenate([pad_cols(ws_ref[s, g], off) for s in range(shards)], axis=0)

    out_bias, mixed_gain, mixed_bias = vec_ref[0:1], vec_ref[1:2], vec_ref[2:3]
    shrink_bias, final_gain, final_bias = vec_ref[3:4], vec_ref[4:5], vec_ref[5:6]
    h1 = x_ref[0].astype(f32) + dot(c_ref[0], wo_ref[...]) + out_bias
    cen = h1 - jnp.mean(h1, axis=-1, keepdims=True)
    rstd1 = lax.rsqrt(jnp.mean(cen * cen, axis=-1, keepdims=True) + epsilon)
    xhat1 = cen * rstd1
    a = xhat1 * mixed_gain + mixed_bias
    a_low = a.astype(bf16)
    pre_low[...] = a_low

    parts = []
    for g in range(groups):
        base, _ = window(g, per)
        for n in range(hidden // 256):
            cols = slice(256 * n, 256 * n + 256)
            u = dot(pre_low[:, base:base + 256], wepad[g, :, cols]) + be_ref[g:g + 1, cols]
            val, slp = gelu_both(u)
            act[g, :, cols] = val.astype(bf16)
            slope[g, :, cols] = slp
        parts.append(dot(act[g], wspad[g]))
    f = jnp.concatenate(join_windows(parts), axis=1)
    h2 = a + f + shrink_bias
    cen = h2 - jnp.mean(h2, axis=-1, keepdims=True)
    rstd2 = lax.rsqrt(jnp.mean(cen * cen, axis=-1, keepdims=True) + epsilon)
    xhat2 = cen * rstd2
    result_ref[0] = (xhat2 * final_gain + final_bias).astype(bf16)

    up = e_ref[0].astype(f32)
    gvec_ref[4:5] += jnp.sum(up * xhat2, axis=0, keepdims=True)
    gvec_ref[5:6] += jnp.sum(up, axis=0, keepdims=True)
    dx = up * final_gain
    dh2 = rstd2 * (dx - jnp.mean(dx, axis=-1, keepdims=True) - xhat2 * jnp.mean(dx * xhat2, axis=-1, keepdims=True))
    gvec_ref[3:4] += jnp.sum(dh2, axis=0, keepdims=True)
    df_low[...] = dh2.astype(bf16)
    a_t = jnp.transpose(a_low)
    df_t = jnp.transpose(df_low[...])
    parts = []
    for g in range(groups):
        base, _ = window(g, per)
        rows = slice(per * g, per * g + per)
        gws_ref[g] += dot(df_t[rows], act[g])
        acc = None
        for n in range(hidden // 256):
            cols = slice(256 * n, 256 * n + 256)
            dg = dot(df_low[:, base:base + 256], wspad[g, cols, :], NT)
            du = (dg * slope[g, :, cols]).astype(bf16)
            gbe_ref[g:g + 1, cols] += jnp.sum(du.astype(f32), axis=0, keepdims=True)
            gwe_ref[g, :, cols] += dot(a_t[rows], du)
            da = dot(du, wepad[g, :, cols], NT)
            acc = da if acc is None else acc + da
        parts.append(acc)
    da = dh2 + jnp.concatenate(join_windows(parts), axis=1)
    gvec_ref[1:2] += jnp.sum(da * xhat1, axis=0, keepdims=True)
    gvec_ref[2:3] += jnp.sum(da, axis=0, keepdims=True)
    dx = da * mixed_gain
    dh1 = rstd1 * (dx - jnp.mean(dx, axis=-1, keepdims=True) - xhat1 * jnp.mean(dx * xhat1, axis=-1, keepdims=True))
    gvec_ref[0:1] += jnp.sum(dh1, axis=0, keepdims=True)
    dh1_ref[0] = dh1
    dy = dh1.astype(bf16)
    gwo_ref[...] += dot(jnp.transpose(c_ref[0]), dy)
    dc_ref[0] = dot(dy, wo_ref[...], NT).astype(bf16)


def feed(x, c, e, wo, we, be, ws, vec):
    rows, length, width = x.shape
    shards, groups, per, part = we.shape
    hidden = shards * part
    wide = row_spec((length, width))
    low = jax.ShapeDtypeStruct((rows, length, width), bf16)
    grads = [(width, width), (groups, per, hidden), (groups, per, hidden), (groups, hidden), (8, width)]
    return pl.pallas_call(
        feed_kernel,
        grid=(rows,),
        in_specs=[wide, wide, wide] + [full(t.shape) for t in (wo, we, be, ws, vec)],
        out_specs=[wide, wide, wide] + [full(s) for s in grads],
        out_shape=[low, jax.ShapeDtypeStruct((rows, length, width), f32), low]
        + [jax.ShapeDtypeStruct(s, f32) for s in grads],
        scratch_shapes=[
            pltpu.VMEM((groups, 256, hidden), bf16),
            pltpu.VMEM((groups, hidden, 256), bf16),
            pltpu.VMEM((groups, length, hidden), bf16),
            pltpu.VMEM((groups, length, hidden), f32),
            pltpu.VMEM((length, width), bf16),
            pltpu.VMEM((length, width), bf16),
            pltpu.VMEM((8, 128), bf16),
        ],
        compiler_params=pltpu.CompilerParams(vmem_limit_bytes=VMEM_LIMIT),
        cost_estimate=pl.CostEstimate(flops=int(4e10), bytes_accessed=int(5e7), transcendentals=0),
        name="feed",
    )(x, c, e, wo, we, be, ws, vec)


def attend_back_kernel(x_ref, q_ref, k_ref, v_ref, c_ref, dc_ref, p_ref, dh1_ref, wq_ref, wk_ref, wv_ref,
                       dx_ref, gw_ref, gvec_ref, wpad, dqkv, gacc):
    step = pl.program_id(0)
    groups, per = wq_ref.shape[0], wq_ref.shape[1]
    lanes_in = x_ref.shape[2]

    @pl.when(step == 0)
    def _():
        gacc[...] = jnp.zeros(gacc.shape, f32)
        gvec_ref[...] = jnp.zeros(gvec_ref.shape, f32)
        for j, w_ref in enumerate((wq_ref, wk_ref, wv_ref)):
            for g in range(groups):
                _, off = window(g, per)
                wpad[j, g] = pad_rows(pad_cols(w_ref[g], off), off)

    low = lax.broadcasted_iota(jnp.int32, (1, 128), 1) < HEAD
    for pair in range(lanes_in // 128):
        lanes = slice(128 * pair, 128 * pair + 128)
        q2 = q_ref[0, :, lanes] * bf16(HEAD ** -0.5)
        k2 = k_ref[0, :, lanes]
        v2 = v_ref[0, :, lanes]
        dc2 = dc_ref[0, :, lanes]
        prod = dc2.astype(f32) * c_ref[0, :, lanes].astype(f32)
        dq = dk = dv = None
        for h in range(2):
            half = low if h == 0 else jnp.logical_not(low)
            km = jnp.where(half, k2, bf16(0))
            qm = jnp.where(half, q2, bf16(0))
            dcm = jnp.where(half, dc2, bf16(0))
            delta = jnp.sum(jnp.where(half, prod, 0.0), axis=-1, keepdims=True)
            pr = p_ref[0, 2 * pair + h]
            dp = dot(dcm, v2, NT)
            ds = (pr.astype(f32) * (dp - delta)).astype(bf16)
            a = dot(ds, km)
            b = dot(ds, qm, TN)
            c = dot(pr, dcm, TN)
            dq = a if dq is None else dq + a
            dk = b if dk is None else dk + b
            dv = c if dv is None else dv + c
        dq = (dq * (HEAD ** -0.5)).astype(bf16)
        dk = dk.astype(bf16)
        dv = dv.astype(bf16)
        dqkv[0, :, lanes] = dq
        dqkv[1, :, lanes] = dk
        dqkv[2, :, lanes] = dv
        gvec_ref[0:1, lanes] += jnp.sum(dq.astype(f32), axis=0, keepdims=True)
        gvec_ref[1:2, lanes] += jnp.sum(dv.astype(f32), axis=0, keepdims=True)

    x_t = jnp.transpose(x_ref[0])
    parts = []
    for g in range(groups):
        base, off = window(g, per)
        acc = None
        for j in range(3):
            d = dqkv[j, :, base:base + 256]
            gacc[j, g] += dot(x_t[per * g:per * g + per], d)
            t = dot(d, wpad[j, g], NT)
            acc = t if acc is None else acc + t
        parts.append(acc)
    for n, col in enumerate(join_windows(parts)):
        lanes = slice(128 * n, 128 * n + 128)
        dx_ref[0, :, lanes] = (col + dh1_ref[0, :, lanes]).astype(bf16)

    @pl.when(step == pl.num_programs(0) - 1)
    def _():
        gw_ref[...] = gacc[...]


def attend_back(x, q, k, v, c, dc, p, dh1, wq, wk, wv, part, parts, prev=None):
    rows, length, width = x.shape
    groups, per, _ = wq.shape
    mine = groups // parts
    lanes = width // parts
    heads = HEADS // parts
    wide = pl.BlockSpec((1, length, lanes), lambda r: (r, 0, part))
    wspec = pl.BlockSpec((mine, per, per), lambda r: (part, 0, 0))
    args = [x, q, k, v, c, dc, p, dh1, wq, wk, wv]
    specs = [wide] * 6 + [pl.BlockSpec((1, heads, length, length), lambda r: (r, part, 0, 0)), wide] + [wspec] * 3
    kernel = attend_back_kernel
    aliases = {}
    if prev is not None:
        args.append(prev)
        specs.append(pl.BlockSpec(memory_space=pl.ANY))
        aliases = {len(args) - 1: 0}
        kernel = lambda *refs: attend_back_kernel(*refs[:11], *refs[12:])
    return pl.pallas_call(
        kernel,
        grid=(rows,),
        in_specs=specs,
        out_specs=[wide, full((3, mine, per, 256)), full((8, lanes))],
        out_shape=[jax.ShapeDtypeStruct((rows, length, width), bf16),
                   jax.ShapeDtypeStruct((3, mine, per, 256), f32), jax.ShapeDtypeStruct((8, lanes), f32)],
        input_output_aliases=aliases,
        scratch_shapes=[
            pltpu.VMEM((3, mine, 256, 256), bf16),
            pltpu.VMEM((3, length, lanes), bf16),
            pltpu.VMEM((3, mine, per, 256), f32),
        ],
        compiler_params=pltpu.CompilerParams(vmem_limit_bytes=VMEM_LIMIT),
        cost_estimate=pl.CostEstimate(flops=int(2e10), bytes_accessed=int(3e7), transcendentals=0),
        name="attend_back",
    )(*args)


def gather_shards(shard):
    count = lax.axis_size("ffn")
    return [shard] + [
        lax.ppermute(shard, "ffn", [(i, (i + d) % count) for i in range(count)]) for d in range(1, count)
    ]


def order_shards(got):
    count = len(got)
    me = lax.axis_index("ffn")
    stacked = jnp.stack(got)
    return stacked[(me - jnp.arange(count)) % count]


def reduce_all(x, axes, count):
    got = lax.all_to_all(x, axes, 0, 0, tiled=True)
    return jnp.sum(got.astype(f32), axis=0)


def spread(x, axes, count):
    return lax.all_to_all(jnp.broadcast_to(x[None], (count,) + x.shape), axes, 0, 0, tiled=True)


def on_device(
    inputs,
    doc_ids,
    cotangent,
    query_weight,
    query_bias,
    key_weight,
    value_weight,
    value_bias,
    out_weight,
    out_bias,
    mixed_gain,
    mixed_bias,
    expand_weight,
    expand_bias,
    shrink_weight,
    shrink_bias,
    final_gain,
    final_bias,
):
    micro, rows_dev, length, width = inputs.shape
    rows = micro * rows_dev
    groups, per, part = expand_weight.shape
    x = inputs.reshape(rows, length, width)
    docs = doc_ids.reshape(rows, 1, length)
    cot = cotangent.reshape(rows, length, width)
    ffn = lax.axis_size("ffn")
    devices = ffn * lax.axis_size("dp")
    hidden = part * ffn

    expand_got = gather_shards(expand_weight)
    shrink_got = gather_shards(shrink_weight)
    bias_all = lax.all_gather(expand_bias, "ffn", axis=1, tiled=True).astype(f32)
    q, k, v, c, p = attend(
        x, docs, query_weight, query_bias[None], key_weight, value_weight, value_bias[None]
    )
    expand_all = order_shards(expand_got)
    shrink_all = order_shards(shrink_got)
    vec = jnp.stack(
        [out_bias.astype(f32), mixed_gain, mixed_bias, shrink_bias.astype(f32), final_gain, final_bias]
        + [jnp.zeros(width, f32)] * 2
    )
    result, dh1, dc, gwo, gwe, gws, gbe, gvec = feed(
        x, c, cot, out_weight, expand_all, bias_all, shrink_all, vec
    )
    dx, gw0, gv0 = attend_back(x, q, k, v, c, dc, p, dh1, query_weight, key_weight, value_weight, 0, 2)
    dx, gw1, gv1 = attend_back(x, q, k, v, c, dc, p, dh1, query_weight, key_weight, value_weight, 1, 2, dx)

    everything = ("dp", "ffn")
    dp = devices // ffn
    shard = jnp.stack([gwe.reshape(groups, per, ffn, part).transpose(2, 0, 1, 3),
                       gws.reshape(groups, per, ffn, part).transpose(2, 0, 1, 3)], axis=1).astype(bf16)
    n = 2 * groups * per * part
    shard = shard.reshape(ffn, dp, n // dp // 128, 128).transpose(1, 0, 2, 3).reshape(devices, n // dp // 128, 128)
    mine = reduce_all(shard, everything, devices)
    ffn_grads = spread(mine.astype(bf16), "dp", dp).reshape(2, groups, per, part).astype(f32)
    grad_expand = ffn_grads[0]
    grad_shrink = ffn_grads[1].transpose(0, 2, 1)

    gw = jnp.concatenate([gw0, gw1], axis=1)
    gw = jnp.stack([gw[:, g, :, window(g, per)[1]:window(g, per)[1] + per] for g in range(groups)], axis=1)
    flat = jnp.concatenate([gwo.reshape(-1), gw.reshape(-1)]).astype(bf16)
    mine = reduce_all(flat.reshape(devices, -1), everything, devices)
    flat = spread(mine.astype(bf16), everything, devices).reshape(-1).astype(f32)
    grad_out = flat[: width * width].reshape(width, width)
    gqkv = flat[width * width :].reshape(3, groups, per, per)

    gvec2 = jnp.concatenate([gv0[:2], gv1[:2]], axis=1)
    vecs = lax.psum((gvec[:6], gvec2), everything)
    gbe = lax.psum(gbe.reshape(groups, ffn, part), "dp")
    gbe = lax.psum_scatter(gbe.transpose(1, 0, 2), "ffn", scatter_dimension=0, tiled=False)
    v6, v2 = vecs
    return (
        result.reshape(inputs.shape),
        dx.reshape(inputs.shape),
        gqkv[0],
        v2[0],
        gqkv[1],
        gqkv[2],
        v2[1],
        grad_out,
        v6[0],
        v6[1],
        v6[2],
        grad_expand,
        gbe,
        grad_shrink,
        v6[3],
        v6[4],
        v6[5],
    )


def solution(mesh):
    in_specs = (
        P(None, ("dp", "ffn"), None, None),
        P(None, ("dp", "ffn"), None),
        P(None, ("dp", "ffn"), None, None),
        P(),
        P(),
        P(),
        P(),
        P(),
        P(),
        P(),
        P(),
        P(),
        P(None, None, "ffn"),
        P(None, "ffn"),
        P(None, "ffn", None),
        P(),
        P(),
        P(),
    )
    out_specs = (
        P(None, ("dp", "ffn"), None, None),
        P(None, ("dp", "ffn"), None, None),
        P(),
        P(),
        P(),
        P(),
        P(),
        P(),
        P(),
        P(),
        P(),
        P(None, None, "ffn"),
        P(None, "ffn"),
        P(None, "ffn", None),
        P(),
        P(),
        P(),
    )
    return jax.shard_map(
        on_device, mesh=mesh, in_specs=in_specs, out_specs=out_specs, check_vma=False
    )
```

```python
import functools

import jax
import jax.numpy as jnp
from jax import lax
from jax.experimental import pallas as pl
from jax.experimental.pallas import tpu as pltpu
from jax.sharding import PartitionSpec as P

HEADS = 12
HEAD = 64
epsilon = 1e-05
masked_score = -1e30
bf16 = jnp.bfloat16
f32 = jnp.float32
VMEM_LIMIT = 60 * 1024 * 1024

OUT_BIAS, MIXED_GAIN, MIXED_BIAS, SHRINK_BIAS, FINAL_GAIN, FINAL_BIAS, QUERY_BIAS, VALUE_BIAS = range(8)

NN = (((1,), (0,)), ((), ()))
NT = (((1,), (1,)), ((), ()))
TN = (((0,), (0,)), ((), ()))


def dot(a, b, dims=NN):
    return lax.dot_general(a, b, dims, preferred_element_type=f32)


def window(group, width):
    start = group * width
    base = start // 128 * 128
    return base, start - base


def shift_matrix(rows, cols, offset, low=0):
    r = lax.broadcasted_iota(jnp.int32, (rows, cols), 0) + offset
    c = lax.broadcasted_iota(jnp.int32, (rows, cols), 1)
    return jnp.where((c == r) & (c >= low), 1.0, 0.0).astype(bf16)


def as_row(ref):
    return ref[...].astype(f32).reshape(1, ref.shape[0])


def pad_cols(w, offset):
    return dot(w, shift_matrix(w.shape[1], 256, offset)).astype(bf16)


def pad_rows(w, offset):
    rows = w.shape[0]
    parts = []
    if offset:
        parts.append(jnp.zeros((offset, w.shape[1]), bf16))
    parts.append(w)
    if 256 - offset - rows:
        parts.append(jnp.zeros((256 - offset - rows, w.shape[1]), bf16))
    return jnp.concatenate(parts, axis=0)


def join_windows(parts):
    out = []
    for i in range(0, len(parts), 2):
        a, b = parts[i], parts[i + 1]
        out += [a[:, :128], a[:, 128:] + b[:, :128], b[:, 128:]]
    return out


def attend_kernel(x_ref, docs_ref, wq_ref, wk_ref, wv_ref, qb_ref, vb_ref,
                  q_ref, k_ref, v_ref, c_ref, p_ref, wpad, bias_ref):
    length = x_ref.shape[1]
    width = x_ref.shape[2]
    groups = wq_ref.shape[0]
    per = width // groups

    @pl.when(pl.program_id(0) == 0)
    def _():
        for j, w_ref in enumerate((wq_ref, wk_ref, wv_ref)):
            for g in range(groups):
                _, off = window(g, per)
                wpad[j, g] = pad_rows(pad_cols(w_ref[g], off), off)

    for j, (out, b_ref) in enumerate(((q_ref, qb_ref), (k_ref, None), (v_ref, vb_ref))):
        bias = None if b_ref is None else as_row(b_ref)
        parts = []
        for g in range(groups):
            base, _ = window(g, per)
            parts.append(dot(x_ref[0, :, base:base + 256], wpad[j, g]))
        for n, col in enumerate(join_windows(parts)):
            if bias is not None:
                col = col + bias[:, 128 * n:128 * n + 128]
            out[0, :, 128 * n:128 * n + 128] = col.astype(bf16)

    docs = docs_ref[0].astype(f32)
    down = jnp.transpose(jnp.broadcast_to(docs, (128, length)))[:, :1]
    bias_ref[...] = jnp.where(down == docs, 0.0, masked_score)
    low = lax.broadcasted_iota(jnp.int32, (1, 128), 1) < HEAD
    for pair in range(HEADS // 2):
        lanes = slice(128 * pair, 128 * pair + 128)
        q2 = q_ref[0, :, lanes] * bf16(HEAD ** -0.5)
        k2 = k_ref[0, :, lanes]
        v2 = v_ref[0, :, lanes]
        acc = None
        for h in range(2):
            half = low if h == 0 else jnp.logical_not(low)
            km = jnp.where(half, k2, bf16(0))
            vm = jnp.where(half, v2, bf16(0))
            s = dot(q2, km, NT) + bias_ref[...]
            top = jnp.max(s, axis=-1, keepdims=True)
            e = jnp.exp(s - top)
            total = jnp.sum(e, axis=-1, keepdims=True)
            pr = (e * (1.0 / total)).astype(bf16)
            p_ref[0, 2 * pair + h] = pr
            c = dot(pr, vm)
            acc = c if acc is None else acc + c
        c_ref[0, :, lanes] = acc.astype(bf16)


def full(shape):
    return pl.BlockSpec(shape, lambda *_: (0,) * len(shape))


def row_spec(shape):
    return pl.BlockSpec((1,) + shape, lambda r: (r,) + (0,) * len(shape))


def attend(x, docs, wq, wk, wv, qb, vb):
    rows, length, width = x.shape
    wide = row_spec((length, width))
    low = jax.ShapeDtypeStruct((rows, length, width), bf16)
    return pl.pallas_call(
        attend_kernel,
        grid=(rows,),
        in_specs=[wide, row_spec((1, length)), full(wq.shape), full(wk.shape), full(wv.shape),
                  whole(), whole()],
        out_specs=[wide, wide, wide, wide, row_spec((HEADS, length, length))],
        out_shape=[low, low, low, low, jax.ShapeDtypeStruct((rows, HEADS, length, length), bf16)],
        scratch_shapes=[pltpu.VMEM((3, wq.shape[0], 256, 256), bf16), pltpu.VMEM((length, length), f32)],
        compiler_params=pltpu.CompilerParams(vmem_limit_bytes=VMEM_LIMIT),
        cost_estimate=pl.CostEstimate(flops=int(2e10), bytes_accessed=int(5e7), transcendentals=0),
        name="attend",
    )(x, docs, wq, wk, wv, qb, vb)


def gelu_both(u):
    cdf = 0.5 * (1.0 + lax.erf(u * 0.7071067811865476))
    pdf = jnp.exp(-0.5 * u * u) * 0.3989422804014327
    return u * cdf, cdf + u * pdf


def low_half():
    return lax.broadcasted_iota(jnp.int32, (1, 128), 1) < 64


def shard_lanes(pos, part):
    start = pos * part
    if start % 128 == 0:
        return start, start + 128
    return start + 64, start - 64


def both_halves(a, b, odd):
    if odd:
        return jnp.where(low_half(), pltpu.roll(a, 64, 1), b)
    return jnp.where(low_half(), a, pltpu.roll(b, 64, 1))


def feed_kernel(me_ref, x_ref, c_ref, e_ref, wo_ref, w0_ref, w1_ref, w2_ref, w3_ref, ob_ref, mg_ref, mb_ref, sb_ref, fg_ref, fb_ref,
                result_ref, dh1_ref, dc_ref, near_e, far_e, send_e, keep_w, send_w, gvec_ref, gbe_ref,
                wepad, wspad, be_s, act, slope, pre_low, df_low, gwo_ref, gwe_ref, gws_ref):
    step = pl.program_id(0)
    groups, width = w0_ref.shape[0], x_ref.shape[2]
    per = width // groups
    part = w0_ref.shape[2] // 2
    hidden = 4 * part
    mine_y = me_ref[0] // 2
    mine_c = me_ref[0] % 2

    @pl.when(step == 0)
    def _():
        gwo_ref[...] = jnp.zeros(gwo_ref.shape, f32)
        gwe_ref[...] = jnp.zeros(gwe_ref.shape, f32)
        gws_ref[...] = jnp.zeros(gws_ref.shape, f32)
        gbe_ref[...] = jnp.zeros(gbe_ref.shape, f32)
        gvec_ref[...] = jnp.zeros(gvec_ref.shape, f32)
        for g in range(groups):
            _, off = window(g, per)
            wide, tall, bias = [], [], []
            for pos in range(4):
                y, dc = pos % 2, pos // 2
                near, far = ((w0_ref, w2_ref), (w1_ref, w3_ref))[dc]
                own = mine_y == y
                blk = jnp.where(own, near[g], far[g])
                e = blk[:per, :256].astype(f32)[:, :part]
                s_ = dot(blk[:part, 128:], shift_matrix(256, 256, off - 64, off)).astype(bf16)
                b = blk[per:, :256].astype(f32)[:1, :part]
                if pos % 2:
                    wide += [e[:, 128:], e[:, :128]]
                    tall += [s_[128:], s_[:128]]
                    bias += [b[:, 128:], b[:, :128]]
                else:
                    wide.append(e)
                    tall.append(s_)
                    bias.append(b)
            wepad[g] = pad_rows(jnp.concatenate(wide, axis=1).astype(bf16), off)
            wspad[g] = jnp.concatenate(tall, axis=0)
            be_s[g:g + 1] = jnp.concatenate(bias, axis=1)

    out_bias, mixed_gain, mixed_bias = as_row(ob_ref), as_row(mg_ref), as_row(mb_ref)
    shrink_bias, final_gain, final_bias = as_row(sb_ref), as_row(fg_ref), as_row(fb_ref)
    h1 = x_ref[0].astype(f32) + dot(c_ref[0], wo_ref[...]) + out_bias
    cen = h1 - jnp.mean(h1, axis=-1, keepdims=True)
    rstd1 = lax.rsqrt(jnp.mean(cen * cen, axis=-1, keepdims=True) + epsilon)
    xhat1 = cen * rstd1
    a = xhat1 * mixed_gain + mixed_bias
    a_low = a.astype(bf16)
    pre_low[...] = a_low

    parts = []
    for g in range(groups):
        base, _ = window(g, per)
        for n in range(hidden // 256):
            cols = slice(256 * n, 256 * n + 256)
            u = dot(pre_low[:, base:base + 256], wepad[g, :, cols]) + be_s[g:g + 1, cols]
            val, slp = gelu_both(u)
            act[g, :, cols] = val.astype(bf16)
            slope[g, :, cols] = slp
        parts.append(dot(act[g], wspad[g]))
    f = jnp.concatenate(join_windows(parts), axis=1)
    h2 = a + f + shrink_bias
    cen = h2 - jnp.mean(h2, axis=-1, keepdims=True)
    rstd2 = lax.rsqrt(jnp.mean(cen * cen, axis=-1, keepdims=True) + epsilon)
    xhat2 = cen * rstd2
    result_ref[0] = (xhat2 * final_gain + final_bias).astype(bf16)

    up = e_ref[0].astype(f32)
    gvec_ref[4:5] += jnp.sum(up * xhat2, axis=0, keepdims=True)
    gvec_ref[5:6] += jnp.sum(up, axis=0, keepdims=True)
    dx = up * final_gain
    dh2 = rstd2 * (dx - jnp.mean(dx, axis=-1, keepdims=True) - xhat2 * jnp.mean(dx * xhat2, axis=-1, keepdims=True))
    gvec_ref[3:4] += jnp.sum(dh2, axis=0, keepdims=True)
    df_low[...] = dh2.astype(bf16)
    a_t = jnp.transpose(a_low)
    df_t = jnp.transpose(df_low[...])
    parts = []
    for g in range(groups):
        base, _ = window(g, per)
        rows = slice(per * g, per * g + per)
        gws_ref[g] += dot(df_t[rows], act[g])
        acc = None
        for n in range(hidden // 256):
            cols = slice(256 * n, 256 * n + 256)
            dg = dot(df_low[:, base:base + 256], wspad[g, cols, :], NT)
            du = (dg * slope[g, :, cols]).astype(bf16)
            gbe_ref[g:g + 1, cols] += jnp.sum(du.astype(f32), axis=0, keepdims=True)
            gwe_ref[g, :, cols] += dot(a_t[rows], du)
            da = dot(du, wepad[g, :, cols], NT)
            acc = da if acc is None else acc + da
        parts.append(acc)
    da = dh2 + jnp.concatenate(join_windows(parts), axis=1)
    gvec_ref[1:2] += jnp.sum(da * xhat1, axis=0, keepdims=True)
    gvec_ref[2:3] += jnp.sum(da, axis=0, keepdims=True)
    dx = da * mixed_gain
    dh1 = rstd1 * (dx - jnp.mean(dx, axis=-1, keepdims=True) - xhat1 * jnp.mean(dx * xhat1, axis=-1, keepdims=True))
    gvec_ref[0:1] += jnp.sum(dh1, axis=0, keepdims=True)
    dh1_ref[0] = dh1
    dy = dh1.astype(bf16)
    gwo_ref[...] += dot(jnp.transpose(c_ref[0]), dy)
    dc_ref[0] = dot(dy, wo_ref[...], NT).astype(bf16)

    @pl.when(step == pl.num_programs(0) - 1)
    def _():
        half = width // 2
        for n in range(3):
            a = gwo_ref[:, 128 * n:128 * n + 128].astype(bf16)
            b = gwo_ref[:, half + 128 * n:half + 128 * n + 128].astype(bf16)
            first = mine_c == 0
            keep_w[width * n:width * n + width] = jnp.where(first, a, b)
            send_w[width * n:width * n + width] = jnp.where(first, b, a)
        for pos in range(4):
            near = mine_y == pos % 2
            base = jnp.where(near, 0, send_e.shape[0] // 2)
            most, rest = shard_lanes(pos, part)
            for i in range(groups):
                acc, g = ((gwe_ref, 2 * i) if 2 * i < groups else (gws_ref, 2 * i - groups))
                tiles = (acc[g, :, most:most + 128], acc[g + 1, :, most:most + 128], both_halves(
                    acc[g, :, rest:rest + 128], acc[g + 1, :, rest:rest + 128], pos % 2))
                for n, tile in enumerate(tiles):
                    first = per * (3 * i + n)
                    tile = tile.astype(bf16)
                    if pos // 2:
                        send_e[pl.ds(pl.multiple_of(base + first, 16), per)] = tile
                    else:
                        @pl.when(near)
                        def _():
                            near_e[first:first + per] = tile

                        @pl.when(jnp.logical_not(near))
                        def _():
                            far_e[first:first + per] = tile


def whole():
    return pl.BlockSpec(memory_space=pltpu.VMEM)


def feed(me, x, c, e, wo, shards, vectors):
    rows, length, width = x.shape
    groups = shards[0].shape[0]
    part = shards[0].shape[2] // 2
    hidden = 4 * part
    per = width // groups
    wide = row_spec((length, width))
    low = jax.ShapeDtypeStruct((rows, length, width), bf16)
    half_e = jax.ShapeDtypeStruct((groups * 3 * per, 128), bf16)
    flat_e = jax.ShapeDtypeStruct((2 * groups * 3 * per, 128), bf16)
    flat_w = jax.ShapeDtypeStruct((3 * width, 128), bf16)
    return pl.pallas_call(
        feed_kernel,
        grid=(rows,),
        in_specs=[pl.BlockSpec(memory_space=pltpu.SMEM), wide, wide, wide] + [whole()] * 11,
        out_specs=[wide, wide, wide] + [whole()] * 7,
        out_shape=[low, jax.ShapeDtypeStruct((rows, length, width), f32), low, half_e, half_e, flat_e, flat_w, flat_w,
                   jax.ShapeDtypeStruct((8, width), f32), jax.ShapeDtypeStruct((8, hidden), f32)],
        scratch_shapes=[
            pltpu.VMEM((groups, 256, hidden), bf16),
            pltpu.VMEM((groups, hidden, 256), bf16),
            pltpu.VMEM((8, hidden), f32),
            pltpu.VMEM((groups, length, hidden), bf16),
            pltpu.VMEM((groups, length, hidden), f32),
            pltpu.VMEM((length, width), bf16),
            pltpu.VMEM((length, width), bf16),
            pltpu.VMEM((width, width), f32),
            pltpu.VMEM((groups, per, hidden), f32),
            pltpu.VMEM((groups, per, hidden), f32),
        ],
        compiler_params=pltpu.CompilerParams(vmem_limit_bytes=VMEM_LIMIT),
        cost_estimate=pl.CostEstimate(flops=int(4e10), bytes_accessed=int(5e7), transcendentals=0),
        name="feed",
    )(me, x, c, e, wo, *shards, *vectors)


def attend_back_kernel(lanes_in, per, x_ref, q_ref, k_ref, v_ref, c_ref, dc_ref, p_ref, me_ref, vec_ref, gbe_ref,
                       prev_ref, dqkv_ref, out_ref, send_ref, gacc, gvec_ref, flat_ref):
    step = pl.program_id(0)
    groups = lanes_in // per

    @pl.when(step == 0)
    def _():
        gacc[...] = jnp.zeros(gacc.shape, f32)
        gvec_ref[...] = jnp.zeros(gvec_ref.shape, f32)

    low = lax.broadcasted_iota(jnp.int32, (1, 128), 1) < HEAD
    for pair in range(lanes_in // 128):
        lanes = slice(128 * pair, 128 * pair + 128)
        q2 = q_ref[0, :, lanes] * bf16(HEAD ** -0.5)
        k2 = k_ref[0, :, lanes]
        v2 = v_ref[0, :, lanes]
        dc2 = dc_ref[0, :, lanes]
        prod = dc2.astype(f32) * c_ref[0, :, lanes].astype(f32)
        dq = dk = dv = None
        for h in range(2):
            half = low if h == 0 else jnp.logical_not(low)
            km = jnp.where(half, k2, bf16(0))
            qm = jnp.where(half, q2, bf16(0))
            dcm = jnp.where(half, dc2, bf16(0))
            delta = jnp.sum(jnp.where(half, prod, 0.0), axis=-1, keepdims=True)
            pr = p_ref[0, 2 * pair + h]
            dp = dot(dcm, v2, NT)
            ds = (pr.astype(f32) * (dp - delta)).astype(bf16)
            a = dot(ds, km)
            b = dot(ds, qm, TN)
            c = dot(pr, dcm, TN)
            dq = a if dq is None else dq + a
            dk = b if dk is None else dk + b
            dv = c if dv is None else dv + c
        dq = (dq * (HEAD ** -0.5)).astype(bf16)
        dk = dk.astype(bf16)
        dv = dv.astype(bf16)
        dqkv_ref[0, 0, :, lanes] = dq
        dqkv_ref[0, 1, :, lanes] = dk
        dqkv_ref[0, 2, :, lanes] = dv
        gvec_ref[0:1, lanes] += jnp.sum(dq.astype(f32), axis=0, keepdims=True)
        gvec_ref[1:2, lanes] += jnp.sum(dv.astype(f32), axis=0, keepdims=True)

    x_t = jnp.transpose(x_ref[0])
    for g in range(groups):
        base, _ = window(g, per)
        for j in range(3):
            gacc[j, g] += dot(x_t[per * g:per * g + per], dqkv_ref[0, j, :, base:base + 256])

    @pl.when(step == pl.num_programs(0) - 1)
    def _():
        base = 0
        if prev_ref is not None:
            base = prev_ref.shape[0]
            flat_ref[:base] = prev_ref[...]
        for j in range(3):
            a, b = gacc[j, 0], gacc[j, 1]
            cols = (a[:, :128], jnp.where(low, a[:, 128:], b[:, :128]), b[:, 128:])
            for n, col in enumerate(cols):
                first = base + per * (3 * j + n)
                flat_ref[first:first + per] = col.astype(bf16)
        first = base + 9 * per
        bits = [gvec_ref[:, 128 * n:128 * n + 128] for n in range(3)] + [jnp.zeros((8, 128), f32)]
        if vec_ref is not None:
            bits += [vec_ref[:, 128 * n:128 * n + 128] for n in range(vec_ref.shape[1] // 128)]
            part = gbe_ref.shape[1] // 4
            same = me_ref[0] % 2 == 0
            for f in range(4):
                y, core = f // 2, f % 2
                near = [gbe_ref[:, lane:lane + 128] for lane in shard_lanes(y + 2 * core, part)]
                far = [gbe_ref[:, lane:lane + 128] for lane in shard_lanes(y + 2 * (1 - core), part)]
                most, rest = (jnp.where(same, a, b) for a, b in zip(near, far))
                bits += [most, pltpu.roll(rest, 64, 1) if y else rest]
        left = flat_ref.shape[0] - first - 8 * len(bits)
        if left:
            bits.append(jnp.zeros((left, 128), f32))
        flat_ref[first:] = jnp.concatenate(bits, axis=0).astype(bf16)
        if send_ref is None:
            out_ref[...] = flat_ref[...]
        else:
            half = out_ref.shape[0]
            core = me_ref[0] % 2
            out_ref[...] = flat_ref[pl.ds(pl.multiple_of(core * half, 16), half)]
            send_ref[...] = flat_ref[pl.ds(pl.multiple_of((1 - core) * half, 16), half)]


def unused():
    return pl.BlockSpec(memory_space=pl.ANY)


def call_sum(kernel, args, shape, after):
    count = len(args)
    return pl.pallas_call(
        lambda *refs: kernel(*refs[:count], *refs[count + len(after):]),
        in_specs=[whole()] * count + [unused()] * len(after),
        out_specs=whole(),
        out_shape=jax.ShapeDtypeStruct(shape, bf16),
        compiler_params=pltpu.CompilerParams(vmem_limit_bytes=VMEM_LIMIT),
        name="add_up",
    )(*args, *after)


def add(arrays, halves=None, after=()):
    shape = arrays[0].shape
    starts = [(n or 0) * shape[0] for n in halves or [0] * len(arrays)]

    def kernel(*refs):
        acc = None
        for first, ref in zip(starts, refs):
            term = ref[first:first + shape[0]].astype(f32)
            acc = term if acc is None else acc + term
        refs[-1][...] = acc.astype(bf16)

    return call_sum(kernel, arrays, shape, after)


def total(x, after=(), copies=0):
    shape = x.shape[1:]

    def kernel(x_ref, o_ref):
        acc = x_ref[0].astype(f32)
        for n in range(1, x_ref.shape[0]):
            acc = acc + x_ref[n].astype(f32)
        acc = acc.astype(bf16)
        if copies:
            for n in range(copies):
                o_ref[n] = acc
        else:
            o_ref[...] = acc

    return call_sum(kernel, (x,), (copies,) + shape if copies else shape, after)


def attend_back(x, q, k, v, c, dc, p, part, me, per, vec=None, gbe=None, prev=None, devices=1, after=()):
    rows, length, width = x.shape
    lanes = width // 2
    heads = HEADS // 2
    wide = pl.BlockSpec((1, length, lanes), lambda r: (r, 0, part))
    args = [x, q, k, v, c, dc, p, me]
    specs = [wide] * 6 + [pl.BlockSpec((1, heads, length, length), lambda r: (r, part, 0, 0)),
                          pl.BlockSpec(memory_space=pltpu.SMEM)]
    flat = 9 * per + 32
    dqkv = jax.ShapeDtypeStruct((rows, 3, length, lanes), bf16)
    if prev is None:
        args += [vec, gbe]
        specs += [whole(), whole()]
        flat += 8 * (width // 128) + 64
        outs = [jax.ShapeDtypeStruct((flat, 128), bf16)]
        pick = lambda refs: (refs[8], refs[9], None) + refs[10:12] + (None,) + refs[12:]
    else:
        args.append(prev)
        specs.append(whole())
        flat = -(-(prev.shape[0] + flat) // (8 * devices)) * 8 * devices
        outs = [jax.ShapeDtypeStruct((flat // 2, 128), bf16)] * 2
        pick = lambda refs: (None, None, refs[8]) + refs[9:]
    return pl.pallas_call(
        lambda *refs: attend_back_kernel(lanes, per, *refs[:8], *pick(refs[:len(args)] + refs[len(args) + len(after):])),
        grid=(rows,),
        in_specs=specs + [unused()] * len(after),
        out_specs=[pl.BlockSpec((1, 3, length, lanes), lambda r: (r, 0, 0, 0))] + [whole()] * len(outs),
        out_shape=[dqkv] + outs,
        scratch_shapes=[
            pltpu.VMEM((3, lanes // per, per, 256), f32),
            pltpu.VMEM((8, lanes), f32),
            pltpu.VMEM((flat, 128), bf16),
        ],
        compiler_params=pltpu.CompilerParams(vmem_limit_bytes=VMEM_LIMIT),
        cost_estimate=pl.CostEstimate(flops=int(2e10), bytes_accessed=int(3e7), transcendentals=0),
        name="attend_back",
    )(*args, *after)


def input_grad_kernel(dh1_ref, d0_ref, d1_ref, wq_ref, wk_ref, wv_ref, dx_ref, wpad):
    groups, per = wq_ref.shape[0], wq_ref.shape[1]

    @pl.when(pl.program_id(0) == 0)
    def _():
        for j, w_ref in enumerate((wq_ref, wk_ref, wv_ref)):
            for g in range(groups):
                _, off = window(g, per)
                wpad[j, g] = pad_rows(pad_cols(w_ref[g], off), off)

    half = d0_ref.shape[3]
    parts = []
    for g in range(groups):
        base, _ = window(g, per)
        d_ref = (d0_ref, d1_ref)[base // half]
        acc = None
        for j in range(3):
            t = dot(d_ref[0, j, :, base % half:base % half + 256], wpad[j, g], NT)
            acc = t if acc is None else acc + t
        parts.append(acc)
    for n, col in enumerate(join_windows(parts)):
        lanes = slice(128 * n, 128 * n + 128)
        dx_ref[0, :, lanes] = (col + dh1_ref[0, :, lanes]).astype(bf16)


def input_grad(dh1, d0, d1, wq, wk, wv, after=()):
    rows, length, width = dh1.shape
    wide = row_spec((length, width))
    back = pl.BlockSpec((1, 3, length, width // 2), lambda r: (r, 0, 0, 0))
    count = 6
    return pl.pallas_call(
        lambda *refs: input_grad_kernel(*refs[:count], *refs[count + len(after):]),
        grid=(rows,),
        in_specs=[wide, back, back] + [full(wq.shape)] * 3 + [unused()] * len(after),
        out_specs=wide,
        out_shape=jax.ShapeDtypeStruct((rows, length, width), bf16),
        scratch_shapes=[pltpu.VMEM((3, wq.shape[0], 256, 256), bf16)],
        compiler_params=pltpu.CompilerParams(vmem_limit_bytes=VMEM_LIMIT),
        cost_estimate=pl.CostEstimate(flops=int(1e10), bytes_accessed=int(2e7), transcendentals=0),
        name="input_grad",
    )(dh1, d0, d1, wq, wk, wv, *after)


def unpack_kernel(order, me_ref, *refs):
    count = len(order)
    pieces, w_ref, own_ref, other_ref = refs[:count], *refs[count:count + 3]
    refs = refs[1:]
    gexp_ref, gshr_ref, gout_ref, gq_ref, gk_ref, gv_ref, gbe_ref = refs[count + 2:count + 9]
    vecs, (e_ref, flat_w, q_ref) = refs[count + 9:count + 17], refs[count + 17:]
    groups, per = gq_ref.shape[0], gq_ref.shape[1]
    width = gout_ref.shape[0]
    part = gexp_ref.shape[2]
    size = pieces[0].shape[0]
    for bit, piece in zip(order, pieces):
        place = pl.multiple_of((me_ref[1] ^ bit) * size, 8)
        e_ref[pl.ds(place, size)] = piece[...].astype(f32)
    size = w_ref.shape[1]
    for i in range(w_ref.shape[0]):
        place = i % 2 * (flat_w.shape[0] // 2) + i // 2 * size
        flat_w[place:place + size] = w_ref[i].astype(f32)
    for i in range(groups):
        first = 3 * per * i
        a = e_ref[first:first + per]
        b = e_ref[first + per:first + 2 * per]
        mix = e_ref[first + 2 * per:first + 3 * per]
        one = jnp.concatenate([a, mix], axis=1)
        two = jnp.concatenate([b, pltpu.roll(mix, 64, 1)], axis=1)
        if 2 * i < groups:
            gexp_ref[2 * i] = one[:, :part]
            gexp_ref[2 * i + 1] = two[:, :part]
        else:
            gshr_ref[2 * i - groups] = jnp.transpose(one)[:part]
            gshr_ref[2 * i - groups + 1] = jnp.transpose(two)[:part]
    half = own_ref.shape[0]
    core = me_ref[0] % 2
    q_ref[pl.ds(pl.multiple_of(core * half, 16), half)] = own_ref[...]
    q_ref[pl.ds(pl.multiple_of((1 - core) * half, 16), half)] = other_ref[...]
    for n in range(width // 128):
        gout_ref[:, 128 * n:128 * n + 128] = flat_w[width * n:width * n + width]
    tiles = width // 128
    used = 9 * per + 32
    start = used + 8 * tiles + 64
    got = {n: [] for n in range(8)}
    for half, flat in enumerate((q_ref[:start], q_ref[start:start + used])):
        for j, out in enumerate((gq_ref, gk_ref, gv_ref)):
            cols = [flat[per * (3 * j + n):per * (3 * j + n) + per].astype(f32) for n in range(3)]
            out[2 * half] = jnp.concatenate(cols[:2], axis=1)[:, :per]
            out[2 * half + 1] = pltpu.roll(jnp.concatenate(cols[1:], axis=1), 192, 1)[:, :per]
        ends = flat[9 * per:9 * per + 32].astype(f32)
        for m, bias in enumerate((QUERY_BIAS, VALUE_BIAS)):
            got[bias] += [ends[8 * n + m:8 * n + m + 1] for n in range(3)]
    rows = q_ref[used:used + 8 * tiles].astype(f32)
    for m in range(6):
        got[m] = [rows[8 * n + m:8 * n + m + 1] for n in range(tiles)]
    for m, vec in enumerate(vecs):
        vec[...] = jnp.concatenate(got[m], axis=1).reshape(width)
    blocks = q_ref[used + 8 * tiles:start].astype(f32)
    pick = blocks[:16]
    for f in range(1, 4):
        pick = jnp.where(me_ref[0] == f, blocks[16 * f:16 * f + 16], pick)
    gbe_ref[...] = jnp.concatenate([pick[:8], pick[8:]], axis=1)[:groups, :part]


def unpack(place, order, pieces, w, own, other, groups, per, width, part):
    shapes = [(groups, per, part), (groups, part, per), (width, width)] + [(groups, per, per)] * 3 + [
        (groups, part)] + [(width,)] * 8
    return pl.pallas_call(
        functools.partial(unpack_kernel, order),
        in_specs=[pl.BlockSpec(memory_space=pltpu.SMEM)] + [whole()] * (len(pieces) + 3),
        out_specs=[whole()] * len(shapes),
        out_shape=[jax.ShapeDtypeStruct(t, f32) for t in shapes],
        scratch_shapes=[pltpu.VMEM((len(pieces) * pieces[0].shape[0], 128), f32),
                        pltpu.VMEM((w.shape[0] * w.shape[1], 128), f32),
                        pltpu.VMEM((2 * own.shape[0], 128), bf16)],
        compiler_params=pltpu.CompilerParams(vmem_limit_bytes=VMEM_LIMIT),
        name="unpack",
    )(place, *pieces, w, own, other)


def exchange(x, axes, groups=None):
    return lax.all_to_all(x, axes, 0, 0, axis_index_groups=groups, tiled=True)


def on_device(
    inputs,
    doc_ids,
    cotangent,
    query_weight,
    query_bias,
    key_weight,
    value_weight,
    value_bias,
    out_weight,
    out_bias,
    mixed_gain,
    mixed_bias,
    expand_weight,
    expand_bias,
    shrink_weight,
    shrink_bias,
    final_gain,
    final_bias,
):
    micro, rows_dev, length, width = inputs.shape
    rows = micro * rows_dev
    groups, per, part = expand_weight.shape
    x = inputs.reshape(rows, length, width)
    docs = doc_ids.reshape(rows, 1, length)
    cot = cotangent.reshape(rows, length, width)
    dp = lax.axis_size("dp")
    everyone = ("dp", "ffn")
    count = 4 * dp
    me = lax.axis_index("ffn").astype(jnp.int32).reshape(1)
    like = [[4 * d + 2 * y + core for d in range(dp) for y in range(2)] for core in range(2)]

    def swap(array, bit):
        return lax.ppermute(array, "ffn", [(f, f ^ bit) for f in range(4)])

    bias = jnp.pad(expand_bias[:, None], ((0, 0), (0, 15), (0, part)))
    shard = jnp.concatenate([jnp.concatenate([expand_weight, shrink_weight], axis=2), bias], axis=1)
    shards = [shard] + [swap(shard, bit) for bit in (1, 2, 3)]
    q, k, v, c, p = attend(x, docs, query_weight, key_weight, value_weight, query_bias, value_bias)
    result, dh1, dc, near_e, far_e, send_e, keep_w, send_w, gvec, gbe = feed(
        me, x, c, cot, out_weight, shards, (out_bias, mixed_gain, mixed_bias, shrink_bias, final_gain, final_bias)
    )

    core_w = swap(send_w, 1)
    core_e = swap(send_e, 1)
    sum_w = add((keep_w, core_w))
    far = add((far_e, core_e), (None, 1))
    got_w = exchange(sum_w.reshape(2 * dp, -1, 128), everyone, like)
    far_got = swap(far, 2)
    back = functools.partial(attend_back, x, q, k, v, c, dc, p, me=me, per=per)
    d0, flat0 = back(part=0, vec=gvec, gbe=gbe, after=(far, sum_w))
    piece_w = total(got_w, after=(flat0,))
    sum_e = add((near_e, core_e, far_got), (None, 0, None), after=(flat0,))
    got_e = exchange(sum_e.reshape(dp, -1, 128), "dp")
    all_w = lax.all_gather(piece_w, everyone)
    d1, keep_q, send_q = back(part=1, prev=flat0, devices=count, after=(sum_e, piece_w))
    piece_e = total(got_e, after=(d1,))
    order, pieces = [0], [piece_e]
    bit = dp // 2
    while bit:
        pieces = pieces + [lax.ppermute(t, "dp", [(d, d ^ bit) for d in range(dp)]) for t in pieces]
        order = order + [n ^ bit for n in order]
        bit //= 2
    sum_q = add((keep_q, swap(send_q, 1)), after=(piece_e, pieces[1]))
    got_q = exchange(sum_q.reshape(2 * dp, -1, 128), everyone, like)
    dx = input_grad(dh1, d0, d1, query_weight, key_weight, value_weight, after=(sum_q,))
    piece_q = total(got_q, after=(dx, all_w, *pieces[2:]), copies=2 * dp)
    own_q = exchange(piece_q, everyone, like).reshape(-1, 128)
    other_q = swap(own_q, 1)
    place = jnp.stack([lax.axis_index("ffn"), lax.axis_index("dp")]).astype(jnp.int32)
    gexp, gshr, gout, gq, gk, gv, gbe, *vecs = unpack(
        place, order, pieces, all_w, own_q, other_q, groups, per, width, part
    )
    return (
        result.reshape(inputs.shape),
        dx.reshape(inputs.shape),
        gq,
        vecs[QUERY_BIAS],
        gk,
        gv,
        vecs[VALUE_BIAS],
        gout,
        vecs[OUT_BIAS],
        vecs[MIXED_GAIN],
        vecs[MIXED_BIAS],
        gexp,
        gbe,
        gshr,
        vecs[SHRINK_BIAS],
        vecs[FINAL_GAIN],
        vecs[FINAL_BIAS],
    )


def solution(mesh):
    in_specs = (
        P(None, ("dp", "ffn"), None, None),
        P(None, ("dp", "ffn"), None),
        P(None, ("dp", "ffn"), None, None),
        P(),
        P(),
        P(),
        P(),
        P(),
        P(),
        P(),
        P(),
        P(),
        P(None, None, "ffn"),
        P(None, "ffn"),
        P(None, "ffn", None),
        P(),
        P(),
        P(),
    )
    out_specs = (
        P(None, ("dp", "ffn"), None, None),
        P(None, ("dp", "ffn"), None, None),
        P(),
        P(),
        P(),
        P(),
        P(),
        P(),
        P(),
        P(),
        P(),
        P(None, None, "ffn"),
        P(None, "ffn"),
        P(None, "ffn", None),
        P(),
        P(),
        P(),
    )
    return jax.shard_map(
        on_device, mesh=mesh, in_specs=in_specs, out_specs=out_specs, check_vma=False
    )
```

```python
import functools

import jax
import jax.numpy as jnp
from jax import lax
from jax.experimental import pallas as pl
from jax.experimental.pallas import tpu as pltpu
from jax.sharding import PartitionSpec as P

HEADS = 12
HEAD = 64
DOCS = 4
CHUNK = 256
epsilon = 1e-05
masked_score = -1e30
bf16 = jnp.bfloat16
f32 = jnp.float32
VMEM_LIMIT = 60 * 1024 * 1024

OUT_BIAS, MIXED_GAIN, MIXED_BIAS, SHRINK_BIAS, FINAL_GAIN, FINAL_BIAS, QUERY_BIAS, VALUE_BIAS = range(8)

NN = (((1,), (0,)), ((), ()))
NT = (((1,), (1,)), ((), ()))
TN = (((0,), (0,)), ((), ()))


def dot(a, b, dims=NN):
    return lax.dot_general(a, b, dims, preferred_element_type=f32)


def window(group, width):
    start = group * width
    base = start // 128 * 128
    return base, start - base


def shift_matrix(rows, cols, offset, low=0):
    r = lax.broadcasted_iota(jnp.int32, (rows, cols), 0) + offset
    c = lax.broadcasted_iota(jnp.int32, (rows, cols), 1)
    return jnp.where((c == r) & (c >= low), 1.0, 0.0).astype(bf16)


def as_row(ref):
    return ref[...].astype(f32).reshape(1, ref.shape[0])


def pad_cols(w, offset):
    return dot(w, shift_matrix(w.shape[1], 256, offset)).astype(bf16)


def pad_rows(w, offset):
    rows = w.shape[0]
    parts = []
    if offset:
        parts.append(jnp.zeros((offset, w.shape[1]), bf16))
    parts.append(w)
    if 256 - offset - rows:
        parts.append(jnp.zeros((256 - offset - rows, w.shape[1]), bf16))
    return jnp.concatenate(parts, axis=0)


def join_windows(parts):
    out = []
    for i in range(0, len(parts), 2):
        a, b = parts[i], parts[i + 1]
        out += [a[:, :128], a[:, 128:] + b[:, :128], b[:, 128:]]
    return out


def attend_kernel(x_ref, docs_ref, wq_ref, wk_ref, wv_ref, qb_ref, vb_ref,
                  q_ref, k_ref, v_ref, c_ref, r_ref, p_ref, wpad):
    length = x_ref.shape[1]
    width = x_ref.shape[2]
    groups = wq_ref.shape[0]
    per = width // groups

    @pl.when(pl.program_id(0) == 0)
    def _():
        for j, w_ref in enumerate((wq_ref, wk_ref, wv_ref)):
            for g in range(groups):
                _, off = window(g, per)
                wpad[j, g] = pad_rows(pad_cols(w_ref[g], off), off)

    for j, (out, b_ref) in enumerate(((q_ref, qb_ref), (k_ref, None), (v_ref, vb_ref))):
        bias = None if b_ref is None else as_row(b_ref)
        parts = []
        for g in range(groups):
            base, _ = window(g, per)
            parts.append(dot(x_ref[0, :, base:base + 256], wpad[j, g]))
        for n, col in enumerate(join_windows(parts)):
            if bias is not None:
                col = col + bias[:, 128 * n:128 * n + 128]
            out[0, :, 128 * n:128 * n + 128] = col.astype(bf16)

    docs = docs_ref[0].astype(f32)
    down = jnp.transpose(jnp.broadcast_to(docs, (128, length)))
    lane = lax.broadcasted_iota(jnp.int32, (1, 128), 1)
    same = down == lane.astype(f32)
    doc_q = jnp.where(same & (lane < DOCS), 1.0, 0.0).astype(bf16)
    doc_k = jnp.where(same | (lane >= DOCS), 0.0, masked_score).astype(bf16)
    low = lane < HEAD
    for pair in range(HEADS // 2):
        lanes = slice(128 * pair, 128 * pair + 128)
        q2 = jnp.concatenate([q_ref[0, :, lanes] * bf16(HEAD ** -0.5), doc_q], axis=1)
        k2 = k_ref[0, :, lanes]
        v2 = v_ref[0, :, lanes]
        acc = None
        for h in range(2):
            half = low if h == 0 else jnp.logical_not(low)
            km = jnp.concatenate([jnp.where(half, k2, bf16(0)), doc_k], axis=1)
            ones = jnp.broadcast_to(jnp.where(half, 1.0, 0.0), (length, 128)).astype(bf16)
            vm = jnp.concatenate([jnp.where(half, v2, bf16(0)), ones], axis=1)
            s = dot(q2, km, NT)
            top = jnp.max(s, axis=-1, keepdims=True)
            pr = jnp.exp(s - top).astype(bf16)
            p_ref[0, 2 * pair + h] = pr
            c = dot(pr, vm)
            acc = c if acc is None else acc + c
        inverse = 1.0 / acc[:, 128:]
        r_ref[0, :, lanes] = inverse
        c_ref[0, :, lanes] = (acc[:, :128] * inverse).astype(bf16)


def full(shape):
    return pl.BlockSpec(shape, lambda *_: (0,) * len(shape))


def row_spec(shape):
    return pl.BlockSpec((1,) + shape, lambda r: (r,) + (0,) * len(shape))


def attend(x, docs, wq, wk, wv, qb, vb):
    rows, length, width = x.shape
    wide = row_spec((length, width))
    low = jax.ShapeDtypeStruct((rows, length, width), bf16)
    return pl.pallas_call(
        attend_kernel,
        grid=(rows,),
        in_specs=[wide, row_spec((1, length)), full(wq.shape), full(wk.shape), full(wv.shape),
                  whole(), whole()],
        out_specs=[wide, wide, wide, wide, wide, row_spec((HEADS, length, length))],
        out_shape=[low, low, low, low, jax.ShapeDtypeStruct((rows, length, width), f32), jax.ShapeDtypeStruct((rows, HEADS, length, length), bf16)],
        scratch_shapes=[pltpu.VMEM((3, wq.shape[0], 256, 256), bf16)],
        compiler_params=pltpu.CompilerParams(vmem_limit_bytes=VMEM_LIMIT),
        cost_estimate=pl.CostEstimate(flops=int(2e10), bytes_accessed=int(5e7), transcendentals=0),
        name="attend",
    )(x, docs, wq, wk, wv, qb, vb)


def gelu_both(u):
    cdf = 0.5 * (1.0 + lax.erf(u * 0.7071067811865476))
    pdf = jnp.exp(-0.5 * u * u) * 0.3989422804014327
    return u * cdf, cdf + u * pdf


def low_half():
    return lax.broadcasted_iota(jnp.int32, (1, 128), 1) < 64


def shard_lanes(pos, part):
    start = pos * part
    if start % 128 == 0:
        return start, start + 128
    return start + 64, start - 64


def both_halves(a, b, odd):
    if odd:
        return jnp.where(low_half(), pltpu.roll(a, 64, 1), b)
    return jnp.where(low_half(), a, pltpu.roll(b, 64, 1))


def feed_kernel(me_ref, x_ref, c_ref, r_ref, e_ref, wo_ref, w0_ref, w1_ref, w2_ref, w3_ref, ob_ref, mg_ref, mb_ref, sb_ref, fg_ref, fb_ref,
                result_ref, dh1_ref, dc_ref, near_e, far_e, send_e, keep_w, send_w, gvec_ref, gbe_ref,
                wepad, wspad, be_s, act, slope, back, xhat1, dh2_s, pre_low, df_low, gwo_ref, gwe_ref, gws_ref):
    step = pl.program_id(0)
    groups, width = w0_ref.shape[0], x_ref.shape[2]
    per = width // groups
    part = w0_ref.shape[2] // 2
    hidden = 4 * part
    mine_y = me_ref[0] // 2
    mine_c = me_ref[0] % 2

    @pl.when(step == 0)
    def _():
        gwo_ref[...] = jnp.zeros(gwo_ref.shape, f32)
        gwe_ref[...] = jnp.zeros(gwe_ref.shape, f32)
        gws_ref[...] = jnp.zeros(gws_ref.shape, f32)
        gbe_ref[...] = jnp.zeros(gbe_ref.shape, f32)
        gvec_ref[...] = jnp.zeros(gvec_ref.shape, f32)
        for g in range(groups):
            _, off = window(g, per)
            wide, tall, bias = [], [], []
            for pos in range(4):
                y, dc = pos % 2, pos // 2
                near, far = ((w0_ref, w2_ref), (w1_ref, w3_ref))[dc]
                own = mine_y == y
                blk = jnp.where(own, near[g], far[g])
                e = blk[:per, :256].astype(f32)[:, :part]
                s_ = dot(blk[:part, 128:], shift_matrix(256, 256, off - 64, off)).astype(bf16)
                b = blk[per:, :256].astype(f32)[:1, :part]
                if pos % 2:
                    wide += [e[:, 128:], e[:, :128]]
                    tall += [s_[128:], s_[:128]]
                    bias += [b[:, 128:], b[:, :128]]
                else:
                    wide.append(e)
                    tall.append(s_)
                    bias.append(b)
            wepad[g] = pad_rows(jnp.concatenate(wide, axis=1).astype(bf16), off)
            wspad[g] = jnp.concatenate(tall, axis=0)
            be_s[g:g + 1] = jnp.concatenate(bias, axis=1)

    out_bias, mixed_gain, mixed_bias = as_row(ob_ref), as_row(mg_ref), as_row(mb_ref)
    shrink_bias, final_gain, final_bias = as_row(sb_ref), as_row(fg_ref), as_row(fb_ref)
    length = x_ref.shape[1]
    chunks = [slice(first, first + CHUNK) for first in range(0, length, CHUNK)]
    keep = {}
    for t in chunks:
        h1 = x_ref[0, t].astype(f32) + dot(c_ref[0, t], wo_ref[...]) + out_bias
        cen = h1 - jnp.mean(h1, axis=-1, keepdims=True)
        rstd1 = lax.rsqrt(jnp.mean(cen * cen, axis=-1, keepdims=True) + epsilon)
        xhat = cen * rstd1
        xhat1[t] = xhat
        a_low = (xhat * mixed_gain + mixed_bias).astype(bf16)
        pre_low[t] = a_low
        keep[t.start] = rstd1

    for t in chunks:
        parts = []
        for g in range(groups):
            base, _ = window(g, per)
            for n in range(hidden // 256):
                cols = slice(256 * n, 256 * n + 256)
                u = dot(pre_low[t, base:base + 256], wepad[g, :, cols]) + be_s[g:g + 1, cols]
                val, slp = gelu_both(u)
                act[g, t, cols] = val.astype(bf16)
                slope[g, t, cols] = slp
            parts.append(dot(act[g, t], wspad[g]))
        f = jnp.concatenate(join_windows(parts), axis=1)
        h2 = (xhat1[t] * mixed_gain + mixed_bias) + f + shrink_bias
        cen = h2 - jnp.mean(h2, axis=-1, keepdims=True)
        rstd2 = lax.rsqrt(jnp.mean(cen * cen, axis=-1, keepdims=True) + epsilon)
        xhat2 = cen * rstd2
        result_ref[0, t] = (xhat2 * final_gain + final_bias).astype(bf16)

        up = e_ref[0, t].astype(f32)
        gvec_ref[4:5] += jnp.sum(up * xhat2, axis=0, keepdims=True)
        gvec_ref[5:6] += jnp.sum(up, axis=0, keepdims=True)
        dx = up * final_gain
        dh2 = rstd2 * (dx - jnp.mean(dx, axis=-1, keepdims=True) - xhat2 * jnp.mean(dx * xhat2, axis=-1, keepdims=True))
        gvec_ref[3:4] += jnp.sum(dh2, axis=0, keepdims=True)
        dh2_s[t] = dh2
        df_low[t] = dh2.astype(bf16)

    for t in chunks:
        parts = []
        for g in range(groups):
            base, _ = window(g, per)
            acc = None
            for n in range(hidden // 256):
                cols = slice(256 * n, 256 * n + 256)
                dg = dot(df_low[t, base:base + 256], wspad[g, cols, :], NT)
                du = (dg * slope[g, t, cols]).astype(bf16)
                back[g, t, cols] = du
                gbe_ref[g:g + 1, cols] += jnp.sum(du.astype(f32), axis=0, keepdims=True)
                da = dot(du, wepad[g, :, cols], NT)
                acc = da if acc is None else acc + da
            parts.append(acc)
        dh2_s[t] += jnp.concatenate(join_windows(parts), axis=1)

    a_t = jnp.transpose(pre_low[...])
    df_t = jnp.transpose(df_low[...])
    for g in range(groups):
        rows = slice(per * g, per * g + per)
        gws_ref[g] += dot(df_t[rows], act[g])
        gwe_ref[g] += dot(a_t[rows], back[g])

    for t in chunks:
        da = dh2_s[t]
        xhat = xhat1[t]
        gvec_ref[1:2] += jnp.sum(da * xhat, axis=0, keepdims=True)
        gvec_ref[2:3] += jnp.sum(da, axis=0, keepdims=True)
        dx = da * mixed_gain
        dh1 = keep[t.start] * (dx - jnp.mean(dx, axis=-1, keepdims=True) - xhat * jnp.mean(dx * xhat, axis=-1, keepdims=True))
        gvec_ref[0:1] += jnp.sum(dh1, axis=0, keepdims=True)
        dh1_ref[0, t] = dh1
        dy = dh1.astype(bf16)
        df_low[t] = dy
        dc_ref[0, t] = (dot(dy, wo_ref[...], NT) * r_ref[0, t]).astype(bf16)
    gwo_ref[...] += dot(jnp.transpose(c_ref[0]), df_low[...])

    @pl.when(step == pl.num_programs(0) - 1)
    def _():
        half = width // 2
        for n in range(3):
            a = gwo_ref[:, 128 * n:128 * n + 128].astype(bf16)
            b = gwo_ref[:, half + 128 * n:half + 128 * n + 128].astype(bf16)
            first = mine_c == 0
            keep_w[width * n:width * n + width] = jnp.where(first, a, b)
            send_w[width * n:width * n + width] = jnp.where(first, b, a)
        for pos in range(4):
            near = mine_y == pos % 2
            base = jnp.where(near, 0, send_e.shape[0] // 2)
            most, rest = shard_lanes(pos, part)
            for i in range(groups):
                acc, g = ((gwe_ref, 2 * i) if 2 * i < groups else (gws_ref, 2 * i - groups))
                tiles = (acc[g, :, most:most + 128], acc[g + 1, :, most:most + 128], both_halves(
                    acc[g, :, rest:rest + 128], acc[g + 1, :, rest:rest + 128], pos % 2))
                for n, tile in enumerate(tiles):
                    first = per * (3 * i + n)
                    tile = tile.astype(bf16)
                    if pos // 2:
                        send_e[pl.ds(pl.multiple_of(base + first, 16), per)] = tile
                    else:
                        @pl.when(near)
                        def _():
                            near_e[first:first + per] = tile

                        @pl.when(jnp.logical_not(near))
                        def _():
                            far_e[first:first + per] = tile


def whole():
    return pl.BlockSpec(memory_space=pltpu.VMEM)


def feed(me, x, c, r, e, wo, shards, vectors):
    rows, length, width = x.shape
    groups = shards[0].shape[0]
    part = shards[0].shape[2] // 2
    hidden = 4 * part
    per = width // groups
    wide = row_spec((length, width))
    low = jax.ShapeDtypeStruct((rows, length, width), bf16)
    half_e = jax.ShapeDtypeStruct((groups * 3 * per, 128), bf16)
    flat_e = jax.ShapeDtypeStruct((2 * groups * 3 * per, 128), bf16)
    flat_w = jax.ShapeDtypeStruct((3 * width, 128), bf16)
    return pl.pallas_call(
        feed_kernel,
        grid=(rows,),
        in_specs=[pl.BlockSpec(memory_space=pltpu.SMEM), wide, wide, wide, wide] + [whole()] * 11,
        out_specs=[wide, wide, wide] + [whole()] * 7,
        out_shape=[low, jax.ShapeDtypeStruct((rows, length, width), f32), low, half_e, half_e, flat_e, flat_w, flat_w,
                   jax.ShapeDtypeStruct((8, width), f32), jax.ShapeDtypeStruct((8, hidden), f32)],
        scratch_shapes=[
            pltpu.VMEM((groups, 256, hidden), bf16),
            pltpu.VMEM((groups, hidden, 256), bf16),
            pltpu.VMEM((8, hidden), f32),
            pltpu.VMEM((groups, length, hidden), bf16),
            pltpu.VMEM((groups, length, hidden), f32),
            pltpu.VMEM((groups, length, hidden), bf16),
            pltpu.VMEM((length, width), f32),
            pltpu.VMEM((length, width), f32),
            pltpu.VMEM((length, width), bf16),
            pltpu.VMEM((length, width), bf16),
            pltpu.VMEM((width, width), f32),
            pltpu.VMEM((groups, per, hidden), f32),
            pltpu.VMEM((groups, per, hidden), f32),
        ],
        compiler_params=pltpu.CompilerParams(vmem_limit_bytes=VMEM_LIMIT),
        cost_estimate=pl.CostEstimate(flops=int(4e10), bytes_accessed=int(5e7), transcendentals=0),
        name="feed",
    )(me, x, c, r, e, wo, *shards, *vectors)


def attend_back_kernel(lanes_in, per, x_ref, q_ref, k_ref, v_ref, c_ref, dc_ref, p_ref, me_ref, vec_ref, gbe_ref,
                       prev_ref, dqkv_ref, out_ref, send_ref, gacc, gvec_ref, flat_ref):
    step = pl.program_id(0)
    groups = lanes_in // per

    @pl.when(step == 0)
    def _():
        gacc[...] = jnp.zeros(gacc.shape, f32)
        gvec_ref[...] = jnp.zeros(gvec_ref.shape, f32)

    low = lax.broadcasted_iota(jnp.int32, (1, 128), 1) < HEAD
    for pair in range(lanes_in // 128):
        lanes = slice(128 * pair, 128 * pair + 128)
        q2 = q_ref[0, :, lanes] * bf16(HEAD ** -0.5)
        k2 = k_ref[0, :, lanes]
        v2 = v_ref[0, :, lanes]
        dc2 = dc_ref[0, :, lanes]
        prod = dc2.astype(f32) * c_ref[0, :, lanes].astype(f32)
        q_t = jnp.transpose(q2)
        dc_t = jnp.transpose(dc2)
        dq = None
        dk, dv = [], []
        for h in range(2):
            half = low if h == 0 else jnp.logical_not(low)
            rows = slice(64 * h, 64 * h + 64)
            km = jnp.where(half, k2, bf16(0))
            vm = jnp.where(half, v2, bf16(0))
            delta = jnp.sum(jnp.where(half, prod, 0.0), axis=-1, keepdims=True)
            pr = p_ref[0, 2 * pair + h]
            dp = dot(dc2, vm, NT)
            ds = (pr.astype(f32) * (dp - delta)).astype(bf16)
            a = dot(ds, km)
            dq = a if dq is None else dq + a
            dk.append(dot(q_t[rows], ds))
            dv.append(dot(dc_t[rows], pr))
        dq = (dq * (HEAD ** -0.5)).astype(bf16)
        dk = jnp.transpose(jnp.concatenate(dk, axis=0)).astype(bf16)
        dv = jnp.transpose(jnp.concatenate(dv, axis=0)).astype(bf16)
        dqkv_ref[0, 0, :, lanes] = dq
        dqkv_ref[0, 1, :, lanes] = dk
        dqkv_ref[0, 2, :, lanes] = dv
        gvec_ref[0:1, lanes] += jnp.sum(dq.astype(f32), axis=0, keepdims=True)
        gvec_ref[1:2, lanes] += jnp.sum(dv.astype(f32), axis=0, keepdims=True)

    x_t = jnp.transpose(x_ref[0])
    for g in range(groups):
        base, _ = window(g, per)
        for j in range(3):
            gacc[j, g] += dot(x_t[per * g:per * g + per], dqkv_ref[0, j, :, base:base + 256])

    @pl.when(step == pl.num_programs(0) - 1)
    def _():
        base = 0
        if prev_ref is not None:
            base = prev_ref.shape[0]
            flat_ref[:base] = prev_ref[...]
        for j in range(3):
            a, b = gacc[j, 0], gacc[j, 1]
            cols = (a[:, :128], jnp.where(low, a[:, 128:], b[:, :128]), b[:, 128:])
            for n, col in enumerate(cols):
                first = base + per * (3 * j + n)
                flat_ref[first:first + per] = col.astype(bf16)
        first = base + 9 * per
        bits = [gvec_ref[:, 128 * n:128 * n + 128] for n in range(3)] + [jnp.zeros((8, 128), f32)]
        if vec_ref is not None:
            bits += [vec_ref[:, 128 * n:128 * n + 128] for n in range(vec_ref.shape[1] // 128)]
            part = gbe_ref.shape[1] // 4
            same = me_ref[0] % 2 == 0
            for f in range(4):
                y, core = f // 2, f % 2
                near = [gbe_ref[:, lane:lane + 128] for lane in shard_lanes(y + 2 * core, part)]
                far = [gbe_ref[:, lane:lane + 128] for lane in shard_lanes(y + 2 * (1 - core), part)]
                most, rest = (jnp.where(same, a, b) for a, b in zip(near, far))
                bits += [most, pltpu.roll(rest, 64, 1) if y else rest]
        left = flat_ref.shape[0] - first - 8 * len(bits)
        if left:
            bits.append(jnp.zeros((left, 128), f32))
        flat_ref[first:] = jnp.concatenate(bits, axis=0).astype(bf16)
        if send_ref is None:
            out_ref[...] = flat_ref[...]
        else:
            half = out_ref.shape[0]
            core = me_ref[0] % 2
            out_ref[...] = flat_ref[pl.ds(pl.multiple_of(core * half, 16), half)]
            send_ref[...] = flat_ref[pl.ds(pl.multiple_of((1 - core) * half, 16), half)]


def unused():
    return pl.BlockSpec(memory_space=pl.ANY)


def call_sum(kernel, args, shape, after):
    count = len(args)
    return pl.pallas_call(
        lambda *refs: kernel(*refs[:count], *refs[count + len(after):]),
        in_specs=[whole()] * count + [unused()] * len(after),
        out_specs=whole(),
        out_shape=jax.ShapeDtypeStruct(shape, bf16),
        compiler_params=pltpu.CompilerParams(vmem_limit_bytes=VMEM_LIMIT),
        name="add_up",
    )(*args, *after)


def add(arrays, halves=None, after=()):
    shape = arrays[0].shape
    starts = [(n or 0) * shape[0] for n in halves or [0] * len(arrays)]

    def kernel(*refs):
        acc = None
        for first, ref in zip(starts, refs):
            term = ref[first:first + shape[0]].astype(f32)
            acc = term if acc is None else acc + term
        refs[-1][...] = acc.astype(bf16)

    return call_sum(kernel, arrays, shape, after)


def total(x, after=(), copies=0):
    shape = x.shape[1:]

    def kernel(x_ref, o_ref):
        acc = x_ref[0].astype(f32)
        for n in range(1, x_ref.shape[0]):
            acc = acc + x_ref[n].astype(f32)
        acc = acc.astype(bf16)
        if copies:
            for n in range(copies):
                o_ref[n] = acc
        else:
            o_ref[...] = acc

    return call_sum(kernel, (x,), (copies,) + shape if copies else shape, after)


def attend_back(x, q, k, v, c, dc, p, part, me, per, vec=None, gbe=None, prev=None, devices=1, after=()):
    rows, length, width = x.shape
    lanes = width // 2
    heads = HEADS // 2
    wide = pl.BlockSpec((1, length, lanes), lambda r: (r, 0, part))
    args = [x, q, k, v, c, dc, p, me]
    specs = [wide] * 6 + [pl.BlockSpec((1, heads, length, length), lambda r: (r, part, 0, 0)),
                          pl.BlockSpec(memory_space=pltpu.SMEM)]
    flat = 9 * per + 32
    dqkv = jax.ShapeDtypeStruct((rows, 3, length, lanes), bf16)
    if prev is None:
        args += [vec, gbe]
        specs += [whole(), whole()]
        flat += 8 * (width // 128) + 64
        outs = [jax.ShapeDtypeStruct((flat, 128), bf16)]
        pick = lambda refs: (refs[8], refs[9], None) + refs[10:12] + (None,) + refs[12:]
    else:
        args.append(prev)
        specs.append(whole())
        flat = -(-(prev.shape[0] + flat) // (8 * devices)) * 8 * devices
        outs = [jax.ShapeDtypeStruct((flat // 2, 128), bf16)] * 2
        pick = lambda refs: (None, None, refs[8]) + refs[9:]
    return pl.pallas_call(
        lambda *refs: attend_back_kernel(lanes, per, *refs[:8], *pick(refs[:len(args)] + refs[len(args) + len(after):])),
        grid=(rows,),
        in_specs=specs + [unused()] * len(after),
        out_specs=[pl.BlockSpec((1, 3, length, lanes), lambda r: (r, 0, 0, 0))] + [whole()] * len(outs),
        out_shape=[dqkv] + outs,
        scratch_shapes=[
            pltpu.VMEM((3, lanes // per, per, 256), f32),
            pltpu.VMEM((8, lanes), f32),
            pltpu.VMEM((flat, 128), bf16),
        ],
        compiler_params=pltpu.CompilerParams(vmem_limit_bytes=VMEM_LIMIT),
        cost_estimate=pl.CostEstimate(flops=int(2e10), bytes_accessed=int(3e7), transcendentals=0),
        name="attend_back",
    )(*args, *after)


def input_grad_kernel(dh1_ref, d0_ref, d1_ref, wq_ref, wk_ref, wv_ref, dx_ref, wpad):
    groups, per = wq_ref.shape[0], wq_ref.shape[1]

    @pl.when(pl.program_id(0) == 0)
    def _():
        for j, w_ref in enumerate((wq_ref, wk_ref, wv_ref)):
            for g in range(groups):
                _, off = window(g, per)
                wpad[j, g] = pad_rows(pad_cols(w_ref[g], off), off)

    half = d0_ref.shape[3]
    parts = []
    for g in range(groups):
        base, _ = window(g, per)
        d_ref = (d0_ref, d1_ref)[base // half]
        acc = None
        for j in range(3):
            t = dot(d_ref[0, j, :, base % half:base % half + 256], wpad[j, g], NT)
            acc = t if acc is None else acc + t
        parts.append(acc)
    for n, col in enumerate(join_windows(parts)):
        lanes = slice(128 * n, 128 * n + 128)
        dx_ref[0, :, lanes] = (col + dh1_ref[0, :, lanes]).astype(bf16)


def input_grad(dh1, d0, d1, wq, wk, wv, after=()):
    rows, length, width = dh1.shape
    wide = row_spec((length, width))
    back = pl.BlockSpec((1, 3, length, width // 2), lambda r: (r, 0, 0, 0))
    count = 6
    return pl.pallas_call(
        lambda *refs: input_grad_kernel(*refs[:count], *refs[count + len(after):]),
        grid=(rows,),
        in_specs=[wide, back, back] + [full(wq.shape)] * 3 + [unused()] * len(after),
        out_specs=wide,
        out_shape=jax.ShapeDtypeStruct((rows, length, width), bf16),
        scratch_shapes=[pltpu.VMEM((3, wq.shape[0], 256, 256), bf16)],
        compiler_params=pltpu.CompilerParams(vmem_limit_bytes=VMEM_LIMIT),
        cost_estimate=pl.CostEstimate(flops=int(1e10), bytes_accessed=int(2e7), transcendentals=0),
        name="input_grad",
    )(dh1, d0, d1, wq, wk, wv, *after)


def unpack_kernel(order, me_ref, *refs):
    count = len(order)
    pieces, w_ref, own_ref, other_ref = refs[:count], *refs[count:count + 3]
    refs = refs[1:]
    gexp_ref, gshr_ref, gout_ref, gq_ref, gk_ref, gv_ref, gbe_ref = refs[count + 2:count + 9]
    vecs, (e_ref, flat_w, q_ref) = refs[count + 9:count + 17], refs[count + 17:]
    groups, per = gq_ref.shape[0], gq_ref.shape[1]
    width = gout_ref.shape[0]
    part = gexp_ref.shape[2]
    size = pieces[0].shape[0]
    for bit, piece in zip(order, pieces):
        place = pl.multiple_of((me_ref[1] ^ bit) * size, 8)
        e_ref[pl.ds(place, size)] = piece[...].astype(f32)
    size = w_ref.shape[1]
    for i in range(w_ref.shape[0]):
        place = i % 2 * (flat_w.shape[0] // 2) + i // 2 * size
        flat_w[place:place + size] = w_ref[i].astype(f32)
    for i in range(groups):
        first = 3 * per * i
        a = e_ref[first:first + per]
        b = e_ref[first + per:first + 2 * per]
        mix = e_ref[first + 2 * per:first + 3 * per]
        one = jnp.concatenate([a, mix], axis=1)
        two = jnp.concatenate([b, pltpu.roll(mix, 64, 1)], axis=1)
        if 2 * i < groups:
            gexp_ref[2 * i] = one[:, :part]
            gexp_ref[2 * i + 1] = two[:, :part]
        else:
            gshr_ref[2 * i - groups] = jnp.transpose(one)[:part]
            gshr_ref[2 * i - groups + 1] = jnp.transpose(two)[:part]
    half = own_ref.shape[0]
    core = me_ref[0] % 2
    q_ref[pl.ds(pl.multiple_of(core * half, 16), half)] = own_ref[...]
    q_ref[pl.ds(pl.multiple_of((1 - core) * half, 16), half)] = other_ref[...]
    for n in range(width // 128):
        gout_ref[:, 128 * n:128 * n + 128] = flat_w[width * n:width * n + width]
    tiles = width // 128
    used = 9 * per + 32
    start = used + 8 * tiles + 64
    got = {n: [] for n in range(8)}
    for half, flat in enumerate((q_ref[:start], q_ref[start:start + used])):
        for j, out in enumerate((gq_ref, gk_ref, gv_ref)):
            cols = [flat[per * (3 * j + n):per * (3 * j + n) + per].astype(f32) for n in range(3)]
            out[2 * half] = jnp.concatenate(cols[:2], axis=1)[:, :per]
            out[2 * half + 1] = pltpu.roll(jnp.concatenate(cols[1:], axis=1), 192, 1)[:, :per]
        ends = flat[9 * per:9 * per + 32].astype(f32)
        for m, bias in enumerate((QUERY_BIAS, VALUE_BIAS)):
            got[bias] += [ends[8 * n + m:8 * n + m + 1] for n in range(3)]
    rows = q_ref[used:used + 8 * tiles].astype(f32)
    for m in range(6):
        got[m] = [rows[8 * n + m:8 * n + m + 1] for n in range(tiles)]
    for m, vec in enumerate(vecs):
        vec[...] = jnp.concatenate(got[m], axis=1).reshape(width)
    blocks = q_ref[used + 8 * tiles:start].astype(f32)
    pick = blocks[:16]
    for f in range(1, 4):
        pick = jnp.where(me_ref[0] == f, blocks[16 * f:16 * f + 16], pick)
    gbe_ref[...] = jnp.concatenate([pick[:8], pick[8:]], axis=1)[:groups, :part]


def unpack(place, order, pieces, w, own, other, groups, per, width, part):
    shapes = [(groups, per, part), (groups, part, per), (width, width)] + [(groups, per, per)] * 3 + [
        (groups, part)] + [(width,)] * 8
    return pl.pallas_call(
        functools.partial(unpack_kernel, order),
        in_specs=[pl.BlockSpec(memory_space=pltpu.SMEM)] + [whole()] * (len(pieces) + 3),
        out_specs=[whole()] * len(shapes),
        out_shape=[jax.ShapeDtypeStruct(t, f32) for t in shapes],
        scratch_shapes=[pltpu.VMEM((len(pieces) * pieces[0].shape[0], 128), f32),
                        pltpu.VMEM((w.shape[0] * w.shape[1], 128), f32),
                        pltpu.VMEM((2 * own.shape[0], 128), bf16)],
        compiler_params=pltpu.CompilerParams(vmem_limit_bytes=VMEM_LIMIT),
        name="unpack",
    )(place, *pieces, w, own, other)


def exchange(x, axes, groups=None):
    return lax.all_to_all(x, axes, 0, 0, axis_index_groups=groups, tiled=True)


def on_device(
    inputs,
    doc_ids,
    cotangent,
    query_weight,
    query_bias,
    key_weight,
    value_weight,
    value_bias,
    out_weight,
    out_bias,
    mixed_gain,
    mixed_bias,
    expand_weight,
    expand_bias,
    shrink_weight,
    shrink_bias,
    final_gain,
    final_bias,
):
    micro, rows_dev, length, width = inputs.shape
    rows = micro * rows_dev
    groups, per, part = expand_weight.shape
    x = inputs.reshape(rows, length, width)
    docs = doc_ids.reshape(rows, 1, length)
    cot = cotangent.reshape(rows, length, width)
    dp = lax.axis_size("dp")
    everyone = ("dp", "ffn")
    count = 4 * dp
    me = lax.axis_index("ffn").astype(jnp.int32).reshape(1)
    like = [[4 * d + 2 * y + core for d in range(dp) for y in range(2)] for core in range(2)]

    def swap(array, bit):
        return lax.ppermute(array, "ffn", [(f, f ^ bit) for f in range(4)])

    bias = jnp.pad(expand_bias[:, None], ((0, 0), (0, 15), (0, part)))
    shard = jnp.concatenate([jnp.concatenate([expand_weight, shrink_weight], axis=2), bias], axis=1)
    shards = [shard] + [swap(shard, bit) for bit in (1, 2, 3)]
    q, k, v, c, r, p = attend(x, docs, query_weight, key_weight, value_weight, query_bias, value_bias)
    result, dh1, dc, near_e, far_e, send_e, keep_w, send_w, gvec, gbe = feed(
        me, x, c, r, cot, out_weight, shards, (out_bias, mixed_gain, mixed_bias, shrink_bias, final_gain, final_bias)
    )

    core_w = swap(send_w, 1)
    core_e = swap(send_e, 1)
    sum_w = add((keep_w, core_w))
    far = add((far_e, core_e), (None, 1))
    got_w = exchange(sum_w.reshape(2 * dp, -1, 128), everyone, like)
    far_got = swap(far, 2)
    back = functools.partial(attend_back, x, q, k, v, c, dc, p, me=me, per=per)
    d0, flat0 = back(part=0, vec=gvec, gbe=gbe, after=(far, sum_w))
    piece_w = total(got_w, after=(flat0,))
    sum_e = add((near_e, core_e, far_got), (None, 0, None), after=(flat0,))
    got_e = exchange(sum_e.reshape(dp, -1, 128), "dp")
    all_w = lax.all_gather(piece_w, everyone)
    d1, keep_q, send_q = back(part=1, prev=flat0, devices=count, after=(sum_e, piece_w))
    piece_e = total(got_e, after=(d1,))
    order, pieces = [0], [piece_e]
    bit = dp // 2
    while bit:
        pieces = pieces + [lax.ppermute(t, "dp", [(d, d ^ bit) for d in range(dp)]) for t in pieces]
        order = order + [n ^ bit for n in order]
        bit //= 2
    sum_q = add((keep_q, swap(send_q, 1)), after=(piece_e, pieces[1]))
    got_q = exchange(sum_q.reshape(2 * dp, -1, 128), everyone, like)
    dx = input_grad(dh1, d0, d1, query_weight, key_weight, value_weight, after=(sum_q,))
    piece_q = total(got_q, after=(dx, all_w, *pieces[2:]), copies=2 * dp)
    own_q = exchange(piece_q, everyone, like).reshape(-1, 128)
    other_q = swap(own_q, 1)
    place = jnp.stack([lax.axis_index("ffn"), lax.axis_index("dp")]).astype(jnp.int32)
    gexp, gshr, gout, gq, gk, gv, gbe, *vecs = unpack(
        place, order, pieces, all_w, own_q, other_q, groups, per, width, part
    )
    return (
        result.reshape(inputs.shape),
        dx.reshape(inputs.shape),
        gq,
        vecs[QUERY_BIAS],
        gk,
        gv,
        vecs[VALUE_BIAS],
        gout,
        vecs[OUT_BIAS],
        vecs[MIXED_GAIN],
        vecs[MIXED_BIAS],
        gexp,
        gbe,
        gshr,
        vecs[SHRINK_BIAS],
        vecs[FINAL_GAIN],
        vecs[FINAL_BIAS],
    )


def solution(mesh):
    in_specs = (
        P(None, ("dp", "ffn"), None, None),
        P(None, ("dp", "ffn"), None),
        P(None, ("dp", "ffn"), None, None),
        P(),
        P(),
        P(),
        P(),
        P(),
        P(),
        P(),
        P(),
        P(),
        P(None, None, "ffn"),
        P(None, "ffn"),
        P(None, "ffn", None),
        P(),
        P(),
        P(),
    )
    out_specs = (
        P(None, ("dp", "ffn"), None, None),
        P(None, ("dp", "ffn"), None, None),
        P(),
        P(),
        P(),
        P(),
        P(),
        P(),
        P(),
        P(),
        P(),
        P(None, None, "ffn"),
        P(None, "ffn"),
        P(None, "ffn", None),
        P(),
        P(),
        P(),
    )
    return jax.shard_map(
        on_device, mesh=mesh, in_specs=in_specs, out_specs=out_specs, check_vma=False
    )
```

```python
import functools

import jax
import jax.numpy as jnp
from jax import lax
from jax.experimental import pallas as pl
from jax.experimental.pallas import tpu as pltpu
from jax.sharding import PartitionSpec as P

HEADS = 12
HEAD = 64
DOCS = 4
CHUNK = 256
epsilon = 1e-05
masked_score = -1e30
bf16 = jnp.bfloat16
f32 = jnp.float32
VMEM_LIMIT = 60 * 1024 * 1024
SMALL_LIMIT = 30 * 1024 * 1024

OUT_BIAS, MIXED_GAIN, MIXED_BIAS, SHRINK_BIAS, FINAL_GAIN, FINAL_BIAS, QUERY_BIAS, VALUE_BIAS = range(8)

NN = (((1,), (0,)), ((), ()))
NT = (((1,), (1,)), ((), ()))
TN = (((0,), (0,)), ((), ()))


def dot(a, b, dims=NN):
    return lax.dot_general(a, b, dims, preferred_element_type=f32)


def window(group, width):
    start = group * width
    base = start // 128 * 128
    return base, start - base


def shift_matrix(rows, cols, offset, low=0):
    r = lax.broadcasted_iota(jnp.int32, (rows, cols), 0) + offset
    c = lax.broadcasted_iota(jnp.int32, (rows, cols), 1)
    return jnp.where((c == r) & (c >= low), 1.0, 0.0).astype(bf16)


def as_row(ref):
    return ref[...].astype(f32).reshape(1, ref.shape[0])


def pad_cols(w, offset):
    return dot(w, shift_matrix(w.shape[1], 256, offset)).astype(bf16)


def pad_rows(w, offset):
    rows = w.shape[0]
    parts = []
    if offset:
        parts.append(jnp.zeros((offset, w.shape[1]), bf16))
    parts.append(w)
    if 256 - offset - rows:
        parts.append(jnp.zeros((256 - offset - rows, w.shape[1]), bf16))
    return jnp.concatenate(parts, axis=0)


def join_windows(parts):
    out = []
    for i in range(0, len(parts), 2):
        a, b = parts[i], parts[i + 1]
        out += [a[:, :128], a[:, 128:] + b[:, :128], b[:, 128:]]
    return out


def attend_kernel(x_ref, docs_ref, wq_ref, wk_ref, wv_ref, qb_ref, vb_ref,
                  q_ref, k_ref, v_ref, c_ref, r_ref, p_ref, wpad):
    length = x_ref.shape[1]
    width = x_ref.shape[2]
    groups = wq_ref.shape[0]
    per = width // groups

    @pl.when(pl.program_id(0) == 0)
    def _():
        for j, w_ref in enumerate((wq_ref, wk_ref, wv_ref)):
            for g in range(groups):
                _, off = window(g, per)
                wpad[j, g] = pad_rows(pad_cols(w_ref[g], off), off)

    for j, (out, b_ref) in enumerate(((q_ref, qb_ref), (k_ref, None), (v_ref, vb_ref))):
        bias = None if b_ref is None else as_row(b_ref)
        parts = []
        for g in range(groups):
            base, _ = window(g, per)
            parts.append(dot(x_ref[0, :, base:base + 256], wpad[j, g]))
        for n, col in enumerate(join_windows(parts)):
            if bias is not None:
                col = col + bias[:, 128 * n:128 * n + 128]
            out[0, :, 128 * n:128 * n + 128] = col.astype(bf16)

    docs = docs_ref[0].astype(f32)
    down = jnp.transpose(jnp.broadcast_to(docs, (128, length)))
    lane = lax.broadcasted_iota(jnp.int32, (1, 128), 1)
    same = down == lane.astype(f32)
    doc_q = jnp.where(same & (lane < DOCS), 1.0, 0.0).astype(bf16)
    doc_k = jnp.where(same | (lane >= DOCS), 0.0, masked_score).astype(bf16)
    low = lane < HEAD
    for pair in range(HEADS // 2):
        lanes = slice(128 * pair, 128 * pair + 128)
        q2 = jnp.concatenate([q_ref[0, :, lanes] * bf16(HEAD ** -0.5), doc_q], axis=1)
        k2 = k_ref[0, :, lanes]
        v2 = v_ref[0, :, lanes]
        acc = None
        for h in range(2):
            half = low if h == 0 else jnp.logical_not(low)
            km = jnp.concatenate([jnp.where(half, k2, bf16(0)), doc_k], axis=1)
            ones = jnp.broadcast_to(jnp.where(half, 1.0, 0.0), (length, 128)).astype(bf16)
            vm = jnp.concatenate([jnp.where(half, v2, bf16(0)), ones], axis=1)
            s = dot(q2, km, NT)
            top = jnp.max(s, axis=-1, keepdims=True)
            pr = jnp.exp(s - top).astype(bf16)
            p_ref[0, 2 * pair + h] = pr
            c = dot(pr, vm)
            acc = c if acc is None else acc + c
        inverse = 1.0 / acc[:, 128:]
        r_ref[0, :, lanes] = inverse
        c_ref[0, :, lanes] = (acc[:, :128] * inverse).astype(bf16)


def full(shape):
    return pl.BlockSpec(shape, lambda *_: (0,) * len(shape))


def row_spec(shape):
    return pl.BlockSpec((1,) + shape, lambda r: (r,) + (0,) * len(shape))


def attend(x, docs, wq, wk, wv, qb, vb):
    rows, length, width = x.shape
    wide = row_spec((length, width))
    low = jax.ShapeDtypeStruct((rows, length, width), bf16)
    return pl.pallas_call(
        attend_kernel,
        grid=(rows,),
        in_specs=[wide, row_spec((1, length)), full(wq.shape), full(wk.shape), full(wv.shape),
                  whole(), whole()],
        out_specs=[wide, wide, wide, wide, wide, row_spec((HEADS, length, length))],
        out_shape=[low, low, low, low, jax.ShapeDtypeStruct((rows, length, width), f32), jax.ShapeDtypeStruct((rows, HEADS, length, length), bf16)],
        scratch_shapes=[pltpu.VMEM((3, wq.shape[0], 256, 256), bf16)],
        compiler_params=pltpu.CompilerParams(vmem_limit_bytes=VMEM_LIMIT),
        cost_estimate=pl.CostEstimate(flops=int(2e10), bytes_accessed=int(5e7), transcendentals=0),
        name="attend",
    )(x, docs, wq, wk, wv, qb, vb)


def gelu_both(u):
    cdf = 0.5 * (1.0 + lax.erf(u * 0.7071067811865476))
    pdf = jnp.exp(-0.5 * u * u) * 0.3989422804014327
    return u * cdf, cdf + u * pdf


def low_half():
    return lax.broadcasted_iota(jnp.int32, (1, 128), 1) < 64


def shard_lanes(pos, part):
    start = pos * part
    if start % 128 == 0:
        return start, start + 128
    return start + 64, start - 64


def both_halves(a, b, odd):
    if odd:
        return jnp.where(low_half(), pltpu.roll(a, 64, 1), b)
    return jnp.where(low_half(), a, pltpu.roll(b, 64, 1))


def feed_kernel(me_ref, x_ref, c_ref, r_ref, e_ref, wo_ref, w0_ref, w1_ref, w2_ref, w3_ref, ob_ref, mg_ref, mb_ref, sb_ref, fg_ref, fb_ref,
                result_ref, dh1_ref, dc_ref, near_e, far_e, send_e, keep_w, send_w, gvec_ref, gbe_ref,
                wepad, wspad, be_s, act, slope, back, xhat1, dh2_s, pre_low, df_low, gwo_ref, gwe_ref, gws_ref):
    step = pl.program_id(0)
    groups, width = w0_ref.shape[0], x_ref.shape[2]
    per = width // groups
    part = w0_ref.shape[2] // 2
    hidden = 4 * part
    mine_y = me_ref[0] // 2
    mine_c = me_ref[0] % 2

    @pl.when(step == 0)
    def _():
        gwo_ref[...] = jnp.zeros(gwo_ref.shape, f32)
        gwe_ref[...] = jnp.zeros(gwe_ref.shape, f32)
        gws_ref[...] = jnp.zeros(gws_ref.shape, f32)
        gbe_ref[...] = jnp.zeros(gbe_ref.shape, f32)
        gvec_ref[...] = jnp.zeros(gvec_ref.shape, f32)
        for g in range(groups):
            _, off = window(g, per)
            wide, tall, bias = [], [], []
            for pos in range(4):
                y, dc = pos % 2, pos // 2
                near, far = ((w0_ref, w2_ref), (w1_ref, w3_ref))[dc]
                own = mine_y == y
                blk = jnp.where(own, near[g], far[g])
                e = blk[:per, :256].astype(f32)[:, :part]
                s_ = dot(blk[:part, 128:], shift_matrix(256, 256, off - 64, off)).astype(bf16)
                b = blk[per:, :256].astype(f32)[:1, :part]
                if pos % 2:
                    wide += [e[:, 128:], e[:, :128]]
                    tall += [s_[128:], s_[:128]]
                    bias += [b[:, 128:], b[:, :128]]
                else:
                    wide.append(e)
                    tall.append(s_)
                    bias.append(b)
            wepad[g] = pad_rows(jnp.concatenate(wide, axis=1).astype(bf16), off)
            wspad[g] = jnp.concatenate(tall, axis=0)
            be_s[g:g + 1] = jnp.concatenate(bias, axis=1)

    out_bias, mixed_gain, mixed_bias = as_row(ob_ref), as_row(mg_ref), as_row(mb_ref)
    shrink_bias, final_gain, final_bias = as_row(sb_ref), as_row(fg_ref), as_row(fb_ref)
    length = x_ref.shape[1]
    chunks = [slice(first, first + CHUNK) for first in range(0, length, CHUNK)]
    keep = {}
    for t in chunks:
        h1 = x_ref[0, t].astype(f32) + dot(c_ref[0, t], wo_ref[...]) + out_bias
        cen = h1 - jnp.mean(h1, axis=-1, keepdims=True)
        rstd1 = lax.rsqrt(jnp.mean(cen * cen, axis=-1, keepdims=True) + epsilon)
        xhat = cen * rstd1
        xhat1[t] = xhat
        a_low = (xhat * mixed_gain + mixed_bias).astype(bf16)
        pre_low[t] = a_low
        keep[t.start] = rstd1

    for t in chunks:
        parts = []
        for g in range(groups):
            base, _ = window(g, per)
            for n in range(hidden // 256):
                cols = slice(256 * n, 256 * n + 256)
                u = dot(pre_low[t, base:base + 256], wepad[g, :, cols]) + be_s[g:g + 1, cols]
                val, slp = gelu_both(u)
                act[g, t, cols] = val.astype(bf16)
                slope[g, t, cols] = slp
            parts.append(dot(act[g, t], wspad[g]))
        f = jnp.concatenate(join_windows(parts), axis=1)
        h2 = (xhat1[t] * mixed_gain + mixed_bias) + f + shrink_bias
        cen = h2 - jnp.mean(h2, axis=-1, keepdims=True)
        rstd2 = lax.rsqrt(jnp.mean(cen * cen, axis=-1, keepdims=True) + epsilon)
        xhat2 = cen * rstd2
        result_ref[0, t] = (xhat2 * final_gain + final_bias).astype(bf16)

        up = e_ref[0, t].astype(f32)
        gvec_ref[4:5] += jnp.sum(up * xhat2, axis=0, keepdims=True)
        gvec_ref[5:6] += jnp.sum(up, axis=0, keepdims=True)
        dx = up * final_gain
        dh2 = rstd2 * (dx - jnp.mean(dx, axis=-1, keepdims=True) - xhat2 * jnp.mean(dx * xhat2, axis=-1, keepdims=True))
        gvec_ref[3:4] += jnp.sum(dh2, axis=0, keepdims=True)
        dh2_s[t] = dh2
        df_low[t] = dh2.astype(bf16)

    for t in chunks:
        parts = []
        for g in range(groups):
            base, _ = window(g, per)
            acc = None
            for n in range(hidden // 256):
                cols = slice(256 * n, 256 * n + 256)
                dg = dot(df_low[t, base:base + 256], wspad[g, cols, :], NT)
                du = (dg * slope[g, t, cols]).astype(bf16)
                back[g, t, cols] = du
                gbe_ref[g:g + 1, cols] += jnp.sum(du.astype(f32), axis=0, keepdims=True)
                da = dot(du, wepad[g, :, cols], NT)
                acc = da if acc is None else acc + da
            parts.append(acc)
        dh2_s[t] += jnp.concatenate(join_windows(parts), axis=1)

    a_t = jnp.transpose(pre_low[...])
    df_t = jnp.transpose(df_low[...])
    for g in range(groups):
        rows = slice(per * g, per * g + per)
        gws_ref[g] += dot(df_t[rows], act[g])
        gwe_ref[g] += dot(a_t[rows], back[g])

    for t in chunks:
        da = dh2_s[t]
        xhat = xhat1[t]
        gvec_ref[1:2] += jnp.sum(da * xhat, axis=0, keepdims=True)
        gvec_ref[2:3] += jnp.sum(da, axis=0, keepdims=True)
        dx = da * mixed_gain
        dh1 = keep[t.start] * (dx - jnp.mean(dx, axis=-1, keepdims=True) - xhat * jnp.mean(dx * xhat, axis=-1, keepdims=True))
        gvec_ref[0:1] += jnp.sum(dh1, axis=0, keepdims=True)
        dh1_ref[0, t] = dh1
        dy = dh1.astype(bf16)
        df_low[t] = dy
        dc_ref[0, t] = (dot(dy, wo_ref[...], NT) * r_ref[0, t]).astype(bf16)
    gwo_ref[...] += dot(jnp.transpose(c_ref[0]), df_low[...])

    @pl.when(step == pl.num_programs(0) - 1)
    def _():
        half = width // 2
        for n in range(3):
            a = gwo_ref[:, 128 * n:128 * n + 128].astype(bf16)
            b = gwo_ref[:, half + 128 * n:half + 128 * n + 128].astype(bf16)
            first = mine_c == 0
            keep_w[width * n:width * n + width] = jnp.where(first, a, b)
            send_w[width * n:width * n + width] = jnp.where(first, b, a)
        for pos in range(4):
            near = mine_y == pos % 2
            base = jnp.where(near, 0, send_e.shape[0] // 2)
            most, rest = shard_lanes(pos, part)
            for i in range(groups):
                acc, g = ((gwe_ref, 2 * i) if 2 * i < groups else (gws_ref, 2 * i - groups))
                tiles = (acc[g, :, most:most + 128], acc[g + 1, :, most:most + 128], both_halves(
                    acc[g, :, rest:rest + 128], acc[g + 1, :, rest:rest + 128], pos % 2))
                for n, tile in enumerate(tiles):
                    first = per * (3 * i + n)
                    tile = tile.astype(bf16)
                    if pos // 2:
                        send_e[pl.ds(pl.multiple_of(base + first, 16), per)] = tile
                    else:
                        @pl.when(near)
                        def _():
                            near_e[first:first + per] = tile

                        @pl.when(jnp.logical_not(near))
                        def _():
                            far_e[first:first + per] = tile


def whole():
    return pl.BlockSpec(memory_space=pltpu.VMEM)


def feed(me, x, c, r, e, wo, shards, vectors):
    rows, length, width = x.shape
    groups = shards[0].shape[0]
    part = shards[0].shape[2] // 2
    hidden = 4 * part
    per = width // groups
    wide = row_spec((length, width))
    low = jax.ShapeDtypeStruct((rows, length, width), bf16)
    half_e = jax.ShapeDtypeStruct((groups * 3 * per, 128), bf16)
    flat_e = jax.ShapeDtypeStruct((2 * groups * 3 * per, 128), bf16)
    flat_w = jax.ShapeDtypeStruct((3 * width, 128), bf16)
    return pl.pallas_call(
        feed_kernel,
        grid=(rows,),
        in_specs=[pl.BlockSpec(memory_space=pltpu.SMEM), wide, wide, wide, wide] + [whole()] * 11,
        out_specs=[wide, wide, wide] + [whole()] * 7,
        out_shape=[low, jax.ShapeDtypeStruct((rows, length, width), f32), low, half_e, half_e, flat_e, flat_w, flat_w,
                   jax.ShapeDtypeStruct((8, width), f32), jax.ShapeDtypeStruct((8, hidden), f32)],
        scratch_shapes=[
            pltpu.VMEM((groups, 256, hidden), bf16),
            pltpu.VMEM((groups, hidden, 256), bf16),
            pltpu.VMEM((8, hidden), f32),
            pltpu.VMEM((groups, length, hidden), bf16),
            pltpu.VMEM((groups, length, hidden), f32),
            pltpu.VMEM((groups, length, hidden), bf16),
            pltpu.VMEM((length, width), f32),
            pltpu.VMEM((length, width), f32),
            pltpu.VMEM((length, width), bf16),
            pltpu.VMEM((length, width), bf16),
            pltpu.VMEM((width, width), f32),
            pltpu.VMEM((groups, per, hidden), f32),
            pltpu.VMEM((groups, per, hidden), f32),
        ],
        compiler_params=pltpu.CompilerParams(vmem_limit_bytes=VMEM_LIMIT),
        cost_estimate=pl.CostEstimate(flops=int(4e10), bytes_accessed=int(5e7), transcendentals=0),
        name="feed",
    )(me, x, c, r, e, wo, *shards, *vectors)


def attend_back_kernel(lanes_in, per, x_ref, q_ref, k_ref, v_ref, c_ref, dc_ref, p_ref, me_ref, vec_ref, gbe_ref,
                       prev_ref, dqkv_ref, out_ref, send_ref, gacc, gvec_ref, flat_ref):
    step = pl.program_id(0)
    groups = lanes_in // per

    @pl.when(step == 0)
    def _():
        gacc[...] = jnp.zeros(gacc.shape, f32)
        gvec_ref[...] = jnp.zeros(gvec_ref.shape, f32)

    low = lax.broadcasted_iota(jnp.int32, (1, 128), 1) < HEAD
    for pair in range(lanes_in // 128):
        lanes = slice(128 * pair, 128 * pair + 128)
        q2 = q_ref[0, :, lanes] * bf16(HEAD ** -0.5)
        k2 = k_ref[0, :, lanes]
        v2 = v_ref[0, :, lanes]
        dc2 = dc_ref[0, :, lanes]
        prod = dc2.astype(f32) * c_ref[0, :, lanes].astype(f32)
        q_t = jnp.transpose(q2)
        dc_t = jnp.transpose(dc2)
        dq = None
        dk, dv = [], []
        for h in range(2):
            half = low if h == 0 else jnp.logical_not(low)
            rows = slice(64 * h, 64 * h + 64)
            km = jnp.where(half, k2, bf16(0))
            vm = jnp.where(half, v2, bf16(0))
            delta = jnp.sum(jnp.where(half, prod, 0.0), axis=-1, keepdims=True)
            pr = p_ref[0, 2 * pair + h]
            dp = dot(dc2, vm, NT)
            ds = (pr.astype(f32) * (dp - delta)).astype(bf16)
            a = dot(ds, km)
            dq = a if dq is None else dq + a
            dk.append(dot(q_t[rows], ds))
            dv.append(dot(dc_t[rows], pr))
        dq = (dq * (HEAD ** -0.5)).astype(bf16)
        dk = jnp.transpose(jnp.concatenate(dk, axis=0)).astype(bf16)
        dv = jnp.transpose(jnp.concatenate(dv, axis=0)).astype(bf16)
        dqkv_ref[0, 0, :, lanes] = dq
        dqkv_ref[0, 1, :, lanes] = dk
        dqkv_ref[0, 2, :, lanes] = dv
        gvec_ref[0:1, lanes] += jnp.sum(dq.astype(f32), axis=0, keepdims=True)
        gvec_ref[1:2, lanes] += jnp.sum(dv.astype(f32), axis=0, keepdims=True)

    x_t = jnp.transpose(x_ref[0])
    for g in range(groups):
        base, _ = window(g, per)
        for j in range(3):
            gacc[j, g] += dot(x_t[per * g:per * g + per], dqkv_ref[0, j, :, base:base + 256])

    @pl.when(step == pl.num_programs(0) - 1)
    def _():
        base = 0
        if prev_ref is not None:
            base = prev_ref.shape[0]
            flat_ref[:base] = prev_ref[...]
        for j in range(3):
            a, b = gacc[j, 0], gacc[j, 1]
            cols = (a[:, :128], jnp.where(low, a[:, 128:], b[:, :128]), b[:, 128:])
            for n, col in enumerate(cols):
                first = base + per * (3 * j + n)
                flat_ref[first:first + per] = col.astype(bf16)
        first = base + 9 * per
        bits = [gvec_ref[:, 128 * n:128 * n + 128] for n in range(3)] + [jnp.zeros((8, 128), f32)]
        if vec_ref is not None:
            bits += [vec_ref[:, 128 * n:128 * n + 128] for n in range(vec_ref.shape[1] // 128)]
            part = gbe_ref.shape[1] // 4
            same = me_ref[0] % 2 == 0
            for f in range(4):
                y, core = f // 2, f % 2
                near = [gbe_ref[:, lane:lane + 128] for lane in shard_lanes(y + 2 * core, part)]
                far = [gbe_ref[:, lane:lane + 128] for lane in shard_lanes(y + 2 * (1 - core), part)]
                most, rest = (jnp.where(same, a, b) for a, b in zip(near, far))
                bits += [most, pltpu.roll(rest, 64, 1) if y else rest]
        left = flat_ref.shape[0] - first - 8 * len(bits)
        if left:
            bits.append(jnp.zeros((left, 128), f32))
        flat_ref[first:] = jnp.concatenate(bits, axis=0).astype(bf16)
        if send_ref is None:
            out_ref[...] = flat_ref[...]
        else:
            half = out_ref.shape[0]
            core = me_ref[0] % 2
            out_ref[...] = flat_ref[pl.ds(pl.multiple_of(core * half, 16), half)]
            send_ref[...] = flat_ref[pl.ds(pl.multiple_of((1 - core) * half, 16), half)]


def unused():
    return pl.BlockSpec(memory_space=pl.ANY)


def call_sum(kernel, args, shape, after):
    count = len(args)
    return pl.pallas_call(
        lambda *refs: kernel(*refs[:count], *refs[count + len(after):]),
        in_specs=[whole()] * count + [unused()] * len(after),
        out_specs=whole(),
        out_shape=jax.ShapeDtypeStruct(shape, bf16),
        compiler_params=pltpu.CompilerParams(vmem_limit_bytes=SMALL_LIMIT),
        name="add_up",
    )(*args, *after)


def add(arrays, halves=None, after=()):
    shape = arrays[0].shape
    starts = [(n or 0) * shape[0] for n in halves or [0] * len(arrays)]

    def kernel(*refs):
        acc = None
        for first, ref in zip(starts, refs):
            term = ref[first:first + shape[0]].astype(f32)
            acc = term if acc is None else acc + term
        refs[-1][...] = acc.astype(bf16)

    return call_sum(kernel, arrays, shape, after)


def add_both(keep_w, core_w, far_e, core_e):
    def kernel(kw_ref, cw_ref, fe_ref, ce_ref, w_ref, e_ref):
        w_ref[...] = (kw_ref[...].astype(f32) + cw_ref[...].astype(f32)).astype(bf16)
        half = fe_ref.shape[0]
        e_ref[...] = (fe_ref[...].astype(f32) + ce_ref[half:].astype(f32)).astype(bf16)

    return pl.pallas_call(
        kernel,
        in_specs=[whole()] * 4,
        out_specs=[whole()] * 2,
        out_shape=[jax.ShapeDtypeStruct(t.shape, bf16) for t in (keep_w, far_e)],
        compiler_params=pltpu.CompilerParams(vmem_limit_bytes=SMALL_LIMIT),
        name="add_up",
    )(keep_w, core_w, far_e, core_e)


def total(x, after=(), copies=0):
    shape = x.shape[1:]

    def kernel(x_ref, o_ref):
        acc = x_ref[0].astype(f32)
        for n in range(1, x_ref.shape[0]):
            acc = acc + x_ref[n].astype(f32)
        acc = acc.astype(bf16)
        if copies:
            for n in range(copies):
                o_ref[n] = acc
        else:
            o_ref[...] = acc

    return call_sum(kernel, (x,), (copies,) + shape if copies else shape, after)


def attend_back(x, q, k, v, c, dc, p, part, me, per, vec=None, gbe=None, prev=None, devices=1, after=()):
    rows, length, width = x.shape
    lanes = width // 2
    heads = HEADS // 2
    wide = pl.BlockSpec((1, length, lanes), lambda r: (r, 0, part))
    args = [x, q, k, v, c, dc, p, me]
    specs = [wide] * 6 + [pl.BlockSpec((1, heads, length, length), lambda r: (r, part, 0, 0)),
                          pl.BlockSpec(memory_space=pltpu.SMEM)]
    flat = 9 * per + 32
    dqkv = jax.ShapeDtypeStruct((rows, 3, length, lanes), bf16)
    if prev is None:
        args += [vec, gbe]
        specs += [whole(), whole()]
        flat += 8 * (width // 128) + 64
        outs = [jax.ShapeDtypeStruct((flat, 128), bf16)]
        pick = lambda refs: (refs[8], refs[9], None) + refs[10:12] + (None,) + refs[12:]
    else:
        args.append(prev)
        specs.append(whole())
        flat = -(-(prev.shape[0] + flat) // (8 * devices)) * 8 * devices
        outs = [jax.ShapeDtypeStruct((flat // 2, 128), bf16)] * 2
        pick = lambda refs: (None, None, refs[8]) + refs[9:]
    return pl.pallas_call(
        lambda *refs: attend_back_kernel(lanes, per, *refs[:8], *pick(refs[:len(args)] + refs[len(args) + len(after):])),
        grid=(rows,),
        in_specs=specs + [unused()] * len(after),
        out_specs=[pl.BlockSpec((1, 3, length, lanes), lambda r: (r, 0, 0, 0))] + [whole()] * len(outs),
        out_shape=[dqkv] + outs,
        scratch_shapes=[
            pltpu.VMEM((3, lanes // per, per, 256), f32),
            pltpu.VMEM((8, lanes), f32),
            pltpu.VMEM((flat, 128), bf16),
        ],
        compiler_params=pltpu.CompilerParams(vmem_limit_bytes=VMEM_LIMIT),
        cost_estimate=pl.CostEstimate(flops=int(2e10), bytes_accessed=int(3e7), transcendentals=0),
        name="attend_back",
    )(*args, *after)


def input_grad_kernel(dh1_ref, d0_ref, d1_ref, wq_ref, wk_ref, wv_ref, dx_ref, wpad):
    groups, per = wq_ref.shape[0], wq_ref.shape[1]

    @pl.when(pl.program_id(0) == 0)
    def _():
        for j, w_ref in enumerate((wq_ref, wk_ref, wv_ref)):
            for g in range(groups):
                _, off = window(g, per)
                wpad[j, g] = pad_rows(pad_cols(w_ref[g], off), off)

    half = d0_ref.shape[3]
    parts = []
    for g in range(groups):
        base, _ = window(g, per)
        d_ref = (d0_ref, d1_ref)[base // half]
        acc = None
        for j in range(3):
            t = dot(d_ref[0, j, :, base % half:base % half + 256], wpad[j, g], NT)
            acc = t if acc is None else acc + t
        parts.append(acc)
    for n, col in enumerate(join_windows(parts)):
        lanes = slice(128 * n, 128 * n + 128)
        dx_ref[0, :, lanes] = (col + dh1_ref[0, :, lanes]).astype(bf16)


def input_grad(dh1, d0, d1, wq, wk, wv, half, prev=None, after=()):
    rows, length, width = dh1.shape
    count = rows // 2 if half == 0 else rows - rows // 2
    first = half * (rows // 2)
    wide = pl.BlockSpec((1, length, width), lambda r: (r + first, 0, 0))
    back = pl.BlockSpec((1, 3, length, width // 2), lambda r: (r + first, 0, 0, 0))
    args = [dh1, d0, d1, wq, wk, wv]
    extra = list(after)
    aliases = {}
    if prev is not None:
        aliases = {len(args) + len(extra): 0}
        extra.append(prev)
    return pl.pallas_call(
        lambda *refs: input_grad_kernel(*refs[:len(args)], *refs[len(args) + len(extra):]),
        grid=(count,),
        in_specs=[wide, back, back] + [full(wq.shape)] * 3 + [unused()] * len(extra),
        out_specs=wide,
        out_shape=jax.ShapeDtypeStruct((rows, length, width), bf16),
        input_output_aliases=aliases,
        scratch_shapes=[pltpu.VMEM((3, wq.shape[0], 256, 256), bf16)],
        compiler_params=pltpu.CompilerParams(vmem_limit_bytes=SMALL_LIMIT),
        cost_estimate=pl.CostEstimate(flops=int(5e9), bytes_accessed=int(1e7), transcendentals=0),
        name="input_grad",
    )(*args, *extra)


def unpack_kernel(order, me_ref, *refs):
    count = len(order)
    pieces, w_ref, own_ref, other_ref = refs[:count], *refs[count:count + 3]
    refs = refs[1:]
    gexp_ref, gshr_ref, gout_ref, gq_ref, gk_ref, gv_ref, gbe_ref = refs[count + 2:count + 9]
    vecs, (e_ref, flat_w, q_ref) = refs[count + 9:count + 17], refs[count + 17:]
    groups, per = gq_ref.shape[0], gq_ref.shape[1]
    width = gout_ref.shape[0]
    part = gexp_ref.shape[2]
    size = pieces[0].shape[0]
    for bit, piece in zip(order, pieces):
        place = pl.multiple_of((me_ref[1] ^ bit) * size, 8)
        e_ref[pl.ds(place, size)] = piece[...].astype(f32)
    size = w_ref.shape[1]
    for i in range(w_ref.shape[0]):
        place = i % 2 * (flat_w.shape[0] // 2) + i // 2 * size
        flat_w[place:place + size] = w_ref[i].astype(f32)
    for i in range(groups):
        first = 3 * per * i
        a = e_ref[first:first + per]
        b = e_ref[first + per:first + 2 * per]
        mix = e_ref[first + 2 * per:first + 3 * per]
        one = jnp.concatenate([a, mix], axis=1)
        two = jnp.concatenate([b, pltpu.roll(mix, 64, 1)], axis=1)
        if 2 * i < groups:
            gexp_ref[2 * i] = one[:, :part]
            gexp_ref[2 * i + 1] = two[:, :part]
        else:
            gshr_ref[2 * i - groups] = jnp.transpose(one)[:part]
            gshr_ref[2 * i - groups + 1] = jnp.transpose(two)[:part]
    half = own_ref.shape[0]
    core = me_ref[0] % 2
    q_ref[pl.ds(pl.multiple_of(core * half, 16), half)] = own_ref[...]
    q_ref[pl.ds(pl.multiple_of((1 - core) * half, 16), half)] = other_ref[...]
    for n in range(width // 128):
        gout_ref[:, 128 * n:128 * n + 128] = flat_w[width * n:width * n + width]
    tiles = width // 128
    used = 9 * per + 32
    start = used + 8 * tiles + 64
    got = {n: [] for n in range(8)}
    for half, flat in enumerate((q_ref[:start], q_ref[start:start + used])):
        for j, out in enumerate((gq_ref, gk_ref, gv_ref)):
            cols = [flat[per * (3 * j + n):per * (3 * j + n) + per].astype(f32) for n in range(3)]
            out[2 * half] = jnp.concatenate(cols[:2], axis=1)[:, :per]
            out[2 * half + 1] = pltpu.roll(jnp.concatenate(cols[1:], axis=1), 192, 1)[:, :per]
        ends = flat[9 * per:9 * per + 32].astype(f32)
        for m, bias in enumerate((QUERY_BIAS, VALUE_BIAS)):
            got[bias] += [ends[8 * n + m:8 * n + m + 1] for n in range(3)]
    rows = q_ref[used:used + 8 * tiles].astype(f32)
    for m in range(6):
        got[m] = [rows[8 * n + m:8 * n + m + 1] for n in range(tiles)]
    for m, vec in enumerate(vecs):
        vec[...] = jnp.concatenate(got[m], axis=1).reshape(width)
    blocks = q_ref[used + 8 * tiles:start].astype(f32)
    pick = blocks[:16]
    for f in range(1, 4):
        pick = jnp.where(me_ref[0] == f, blocks[16 * f:16 * f + 16], pick)
    gbe_ref[...] = jnp.concatenate([pick[:8], pick[8:]], axis=1)[:groups, :part]


def unpack(place, order, pieces, w, own, other, groups, per, width, part):
    shapes = [(groups, per, part), (groups, part, per), (width, width)] + [(groups, per, per)] * 3 + [
        (groups, part)] + [(width,)] * 8
    return pl.pallas_call(
        functools.partial(unpack_kernel, order),
        in_specs=[pl.BlockSpec(memory_space=pltpu.SMEM)] + [whole()] * (len(pieces) + 3),
        out_specs=[whole()] * len(shapes),
        out_shape=[jax.ShapeDtypeStruct(t, f32) for t in shapes],
        scratch_shapes=[pltpu.VMEM((len(pieces) * pieces[0].shape[0], 128), f32),
                        pltpu.VMEM((w.shape[0] * w.shape[1], 128), f32),
                        pltpu.VMEM((2 * own.shape[0], 128), bf16)],
        compiler_params=pltpu.CompilerParams(vmem_limit_bytes=SMALL_LIMIT),
        name="unpack",
    )(place, *pieces, w, own, other)


def exchange(x, axes, groups=None):
    return lax.all_to_all(x, axes, 0, 0, axis_index_groups=groups, tiled=True)


def on_device(
    inputs,
    doc_ids,
    cotangent,
    query_weight,
    query_bias,
    key_weight,
    value_weight,
    value_bias,
    out_weight,
    out_bias,
    mixed_gain,
    mixed_bias,
    expand_weight,
    expand_bias,
    shrink_weight,
    shrink_bias,
    final_gain,
    final_bias,
):
    micro, rows_dev, length, width = inputs.shape
    rows = micro * rows_dev
    groups, per, part = expand_weight.shape
    x = inputs.reshape(rows, length, width)
    docs = doc_ids.reshape(rows, 1, length)
    cot = cotangent.reshape(rows, length, width)
    dp = lax.axis_size("dp")
    everyone = ("dp", "ffn")
    count = 4 * dp
    me = lax.axis_index("ffn").astype(jnp.int32).reshape(1)
    like = [[4 * d + 2 * y + core for d in range(dp) for y in range(2)] for core in range(2)]

    def swap(array, bit):
        return lax.ppermute(array, "ffn", [(f, f ^ bit) for f in range(4)])

    bias = jnp.pad(expand_bias[:, None], ((0, 0), (0, 15), (0, part)))
    shard = jnp.concatenate([jnp.concatenate([expand_weight, shrink_weight], axis=2), bias], axis=1)
    shards = [shard] + [swap(shard, bit) for bit in (1, 2, 3)]
    q, k, v, c, r, p = attend(x, docs, query_weight, key_weight, value_weight, query_bias, value_bias)
    result, dh1, dc, near_e, far_e, send_e, keep_w, send_w, gvec, gbe = feed(
        me, x, c, r, cot, out_weight, shards, (out_bias, mixed_gain, mixed_bias, shrink_bias, final_gain, final_bias)
    )

    core_w = swap(send_w, 1)
    core_e = swap(send_e, 1)
    sum_w, far = add_both(keep_w, core_w, far_e, core_e)
    got_w = exchange(sum_w.reshape(2 * dp, -1, 128), everyone, like)
    far_got = swap(far, 2)
    back = functools.partial(attend_back, x, q, k, v, c, dc, p, me=me, per=per)
    d0, flat0 = back(part=0, vec=gvec, gbe=gbe, after=(far, sum_w))
    piece_w = total(got_w, after=(flat0,))
    sum_e = add((near_e, core_e, far_got), (None, 0, None), after=(piece_w,))
    got_e = exchange(sum_e.reshape(dp, -1, 128), "dp")
    all_w = lax.all_gather(piece_w, everyone)
    d1, keep_q, send_q = back(part=1, prev=flat0, devices=count, after=(sum_e, piece_w))
    piece_e = total(got_e, after=(d1,))
    order, pieces = [0], [piece_e]
    bit = dp // 2
    while bit:
        pieces = pieces + [lax.ppermute(t, "dp", [(d, d ^ bit) for d in range(dp)]) for t in pieces]
        order = order + [n ^ bit for n in order]
        bit //= 2
    sum_q = add((keep_q, swap(send_q, 1)))
    got_q = exchange(sum_q.reshape(2 * dp, -1, 128), everyone, like)
    back_weights = (query_weight, key_weight, value_weight)
    dx = input_grad(dh1, d0, d1, *back_weights, half=0, after=(sum_q, pieces[1]))
    dx = input_grad(dh1, d0, d1, *back_weights, half=1, prev=dx, after=pieces[2:4])
    piece_q = total(got_q, after=(dx, all_w, *pieces[4:]), copies=2 * dp)
    own_q = exchange(piece_q, everyone, like).reshape(-1, 128)
    other_q = swap(own_q, 1)
    place = jnp.stack([lax.axis_index("ffn"), lax.axis_index("dp")]).astype(jnp.int32)
    gexp, gshr, gout, gq, gk, gv, gbe, *vecs = unpack(
        place, order, pieces, all_w, own_q, other_q, groups, per, width, part
    )
    return (
        result.reshape(inputs.shape),
        dx.reshape(inputs.shape),
        gq,
        vecs[QUERY_BIAS],
        gk,
        gv,
        vecs[VALUE_BIAS],
        gout,
        vecs[OUT_BIAS],
        vecs[MIXED_GAIN],
        vecs[MIXED_BIAS],
        gexp,
        gbe,
        gshr,
        vecs[SHRINK_BIAS],
        vecs[FINAL_GAIN],
        vecs[FINAL_BIAS],
    )


def solution(mesh):
    in_specs = (
        P(None, ("dp", "ffn"), None, None),
        P(None, ("dp", "ffn"), None),
        P(None, ("dp", "ffn"), None, None),
        P(),
        P(),
        P(),
        P(),
        P(),
        P(),
        P(),
        P(),
        P(),
        P(None, None, "ffn"),
        P(None, "ffn"),
        P(None, "ffn", None),
        P(),
        P(),
        P(),
    )
    out_specs = (
        P(None, ("dp", "ffn"), None, None),
        P(None, ("dp", "ffn"), None, None),
        P(),
        P(),
        P(),
        P(),
        P(),
        P(),
        P(),
        P(),
        P(),
        P(None, None, "ffn"),
        P(None, "ffn"),
        P(None, "ffn", None),
        P(),
        P(),
        P(),
    )
    return jax.shard_map(
        on_device, mesh=mesh, in_specs=in_specs, out_specs=out_specs, check_vma=False
    )
```

```python
import functools

import jax
import jax.numpy as jnp
from jax import lax
from jax.experimental import pallas as pl
from jax.experimental.pallas import tpu as pltpu
from jax.sharding import PartitionSpec as P

HEADS = 12
HEAD = 64
DOCS = 4
CHUNK = 256
epsilon = 1e-05
masked_score = -1e30
bf16 = jnp.bfloat16
f32 = jnp.float32
VMEM_LIMIT = 60 * 1024 * 1024
SMALL_LIMIT = 30 * 1024 * 1024
GRAD_LIMIT = 30 * 1024 * 1024

OUT_BIAS, MIXED_GAIN, MIXED_BIAS, SHRINK_BIAS, FINAL_GAIN, FINAL_BIAS, QUERY_BIAS, VALUE_BIAS = range(8)

NN = (((1,), (0,)), ((), ()))
NT = (((1,), (1,)), ((), ()))
TN = (((0,), (0,)), ((), ()))


def dot(a, b, dims=NN):
    return lax.dot_general(a, b, dims, preferred_element_type=f32)


def window(group, width):
    start = group * width
    base = start // 128 * 128
    return base, start - base


def shift_matrix(rows, cols, offset, low=0):
    r = lax.broadcasted_iota(jnp.int32, (rows, cols), 0) + offset
    c = lax.broadcasted_iota(jnp.int32, (rows, cols), 1)
    return jnp.where((c == r) & (c >= low), 1.0, 0.0).astype(bf16)


def as_row(ref):
    return ref[...].astype(f32).reshape(1, ref.shape[0])


def pad_cols(w, offset):
    return dot(w, shift_matrix(w.shape[1], 256, offset)).astype(bf16)


def pad_rows(w, offset):
    rows = w.shape[0]
    parts = []
    if offset:
        parts.append(jnp.zeros((offset, w.shape[1]), bf16))
    parts.append(w)
    if 256 - offset - rows:
        parts.append(jnp.zeros((256 - offset - rows, w.shape[1]), bf16))
    return jnp.concatenate(parts, axis=0)


def join_windows(parts):
    out = []
    for i in range(0, len(parts), 2):
        a, b = parts[i], parts[i + 1]
        out += [a[:, :128], a[:, 128:] + b[:, :128], b[:, 128:]]
    return out


def attend_kernel(x_ref, docs_ref, wq_ref, wk_ref, wv_ref, qb_ref, vb_ref,
                  q_ref, k_ref, v_ref, c_ref, r_ref, p_ref, wpad):
    length = x_ref.shape[1]
    width = x_ref.shape[2]
    groups = wq_ref.shape[0]
    per = width // groups

    @pl.when(pl.program_id(0) == 0)
    def _():
        for j, w_ref in enumerate((wq_ref, wk_ref, wv_ref)):
            for g in range(groups):
                _, off = window(g, per)
                wpad[j, g] = pad_rows(pad_cols(w_ref[g], off), off)

    for j, (out, b_ref) in enumerate(((q_ref, qb_ref), (k_ref, None), (v_ref, vb_ref))):
        bias = None if b_ref is None else as_row(b_ref)
        parts = []
        for g in range(groups):
            base, _ = window(g, per)
            parts.append(dot(x_ref[0, :, base:base + 256], wpad[j, g]))
        for n, col in enumerate(join_windows(parts)):
            if bias is not None:
                col = col + bias[:, 128 * n:128 * n + 128]
            out[0, :, 128 * n:128 * n + 128] = col.astype(bf16)

    docs = docs_ref[0].astype(f32)
    down = jnp.transpose(jnp.broadcast_to(docs, (128, length)))
    lane = lax.broadcasted_iota(jnp.int32, (1, 128), 1)
    same = down == lane.astype(f32)
    doc_q = jnp.where(same & (lane < DOCS), 1.0, 0.0).astype(bf16)
    doc_k = jnp.where(same | (lane >= DOCS), 0.0, masked_score).astype(bf16)
    low = lane < HEAD
    for pair in range(HEADS // 2):
        lanes = slice(128 * pair, 128 * pair + 128)
        q2 = jnp.concatenate([q_ref[0, :, lanes] * bf16(HEAD ** -0.5), doc_q], axis=1)
        k2 = k_ref[0, :, lanes]
        v2 = v_ref[0, :, lanes]
        acc = None
        for h in range(2):
            half = low if h == 0 else jnp.logical_not(low)
            km = jnp.concatenate([jnp.where(half, k2, bf16(0)), doc_k], axis=1)
            ones = jnp.broadcast_to(jnp.where(half, 1.0, 0.0), (length, 128)).astype(bf16)
            vm = jnp.concatenate([jnp.where(half, v2, bf16(0)), ones], axis=1)
            s = dot(q2, km, NT)
            top = jnp.max(s, axis=-1, keepdims=True)
            pr = jnp.exp(s - top).astype(bf16)
            p_ref[0, 2 * pair + h] = pr
            c = dot(pr, vm)
            acc = c if acc is None else acc + c
        inverse = 1.0 / acc[:, 128:]
        r_ref[0, :, lanes] = inverse
        c_ref[0, :, lanes] = (acc[:, :128] * inverse).astype(bf16)


def full(shape):
    return pl.BlockSpec(shape, lambda *_: (0,) * len(shape))


def row_spec(shape):
    return pl.BlockSpec((1,) + shape, lambda r: (r,) + (0,) * len(shape))


def attend(x, docs, wq, wk, wv, qb, vb):
    rows, length, width = x.shape
    wide = row_spec((length, width))
    low = jax.ShapeDtypeStruct((rows, length, width), bf16)
    return pl.pallas_call(
        attend_kernel,
        grid=(rows,),
        in_specs=[wide, row_spec((1, length)), full(wq.shape), full(wk.shape), full(wv.shape),
                  whole(), whole()],
        out_specs=[wide, wide, wide, wide, wide, row_spec((HEADS, length, length))],
        out_shape=[low, low, low, low, jax.ShapeDtypeStruct((rows, length, width), f32), jax.ShapeDtypeStruct((rows, HEADS, length, length), bf16)],
        scratch_shapes=[pltpu.VMEM((3, wq.shape[0], 256, 256), bf16)],
        compiler_params=pltpu.CompilerParams(vmem_limit_bytes=VMEM_LIMIT),
        cost_estimate=pl.CostEstimate(flops=int(2e10), bytes_accessed=int(5e7), transcendentals=0),
        name="attend",
    )(x, docs, wq, wk, wv, qb, vb)


def gelu_both(u):
    cdf = 0.5 * (1.0 + lax.erf(u * 0.7071067811865476))
    pdf = jnp.exp(-0.5 * u * u) * 0.3989422804014327
    return u * cdf, cdf + u * pdf


def low_half():
    return lax.broadcasted_iota(jnp.int32, (1, 128), 1) < 64


def shard_lanes(pos, part):
    start = pos * part
    if start % 128 == 0:
        return start, start + 128
    return start + 64, start - 64


def both_halves(a, b, odd):
    if odd:
        return jnp.where(low_half(), pltpu.roll(a, 64, 1), b)
    return jnp.where(low_half(), a, pltpu.roll(b, 64, 1))


def feed_kernel(me_ref, x_ref, c_ref, r_ref, e_ref, wo_ref, w0_ref, w1_ref, w2_ref, w3_ref, ob_ref, mg_ref, mb_ref, sb_ref, fg_ref, fb_ref,
                result_ref, dh1_ref, dc_ref, near_e, far_e, send_e, keep_w, send_w, gvec_ref, gbe_ref,
                wepad, wspad, be_s, act, slope, back, xhat1, dh2_s, pre_low, df_low, gwo_ref, gwe_ref, gws_ref):
    step = pl.program_id(0)
    groups, width = w0_ref.shape[0], x_ref.shape[2]
    per = width // groups
    part = w0_ref.shape[2] // 2
    hidden = 4 * part
    mine_y = me_ref[0] // 2
    mine_c = me_ref[0] % 2

    @pl.when(step == 0)
    def _():
        gwo_ref[...] = jnp.zeros(gwo_ref.shape, f32)
        gwe_ref[...] = jnp.zeros(gwe_ref.shape, f32)
        gws_ref[...] = jnp.zeros(gws_ref.shape, f32)
        gbe_ref[...] = jnp.zeros(gbe_ref.shape, f32)
        gvec_ref[...] = jnp.zeros(gvec_ref.shape, f32)
        for g in range(groups):
            _, off = window(g, per)
            wide, tall, bias = [], [], []
            for pos in range(4):
                y, dc = pos % 2, pos // 2
                near, far = ((w0_ref, w2_ref), (w1_ref, w3_ref))[dc]
                own = mine_y == y
                blk = jnp.where(own, near[g], far[g])
                e = blk[:per, :256].astype(f32)[:, :part]
                s_ = dot(blk[:part, 128:], shift_matrix(256, 256, off - 64, off)).astype(bf16)
                b = blk[per:, :256].astype(f32)[:1, :part]
                if pos % 2:
                    wide += [e[:, 128:], e[:, :128]]
                    tall += [s_[128:], s_[:128]]
                    bias += [b[:, 128:], b[:, :128]]
                else:
                    wide.append(e)
                    tall.append(s_)
                    bias.append(b)
            wepad[g] = pad_rows(jnp.concatenate(wide, axis=1).astype(bf16), off)
            wspad[g] = jnp.concatenate(tall, axis=0)
            be_s[g:g + 1] = jnp.concatenate(bias, axis=1)

    out_bias, mixed_gain, mixed_bias = as_row(ob_ref), as_row(mg_ref), as_row(mb_ref)
    shrink_bias, final_gain, final_bias = as_row(sb_ref), as_row(fg_ref), as_row(fb_ref)
    length = x_ref.shape[1]
    chunks = [slice(first, first + CHUNK) for first in range(0, length, CHUNK)]
    keep = {}
    for t in chunks:
        h1 = x_ref[0, t].astype(f32) + dot(c_ref[0, t], wo_ref[...]) + out_bias
        cen = h1 - jnp.mean(h1, axis=-1, keepdims=True)
        rstd1 = lax.rsqrt(jnp.mean(cen * cen, axis=-1, keepdims=True) + epsilon)
        xhat = cen * rstd1
        xhat1[t] = xhat
        a_low = (xhat * mixed_gain + mixed_bias).astype(bf16)
        pre_low[t] = a_low
        keep[t.start] = rstd1

    for t in chunks:
        parts = []
        for g in range(groups):
            base, _ = window(g, per)
            for n in range(hidden // 256):
                cols = slice(256 * n, 256 * n + 256)
                u = dot(pre_low[t, base:base + 256], wepad[g, :, cols]) + be_s[g:g + 1, cols]
                val, slp = gelu_both(u)
                act[g, t, cols] = val.astype(bf16)
                slope[g, t, cols] = slp
            parts.append(dot(act[g, t], wspad[g]))
        f = jnp.concatenate(join_windows(parts), axis=1)
        h2 = (xhat1[t] * mixed_gain + mixed_bias) + f + shrink_bias
        cen = h2 - jnp.mean(h2, axis=-1, keepdims=True)
        rstd2 = lax.rsqrt(jnp.mean(cen * cen, axis=-1, keepdims=True) + epsilon)
        xhat2 = cen * rstd2
        result_ref[0, t] = (xhat2 * final_gain + final_bias).astype(bf16)

        up = e_ref[0, t].astype(f32)
        gvec_ref[4:5] += jnp.sum(up * xhat2, axis=0, keepdims=True)
        gvec_ref[5:6] += jnp.sum(up, axis=0, keepdims=True)
        dx = up * final_gain
        dh2 = rstd2 * (dx - jnp.mean(dx, axis=-1, keepdims=True) - xhat2 * jnp.mean(dx * xhat2, axis=-1, keepdims=True))
        gvec_ref[3:4] += jnp.sum(dh2, axis=0, keepdims=True)
        dh2_s[t] = dh2
        df_low[t] = dh2.astype(bf16)

    for t in chunks:
        parts = []
        for g in range(groups):
            base, _ = window(g, per)
            acc = None
            for n in range(hidden // 256):
                cols = slice(256 * n, 256 * n + 256)
                dg = dot(df_low[t, base:base + 256], wspad[g, cols, :], NT)
                du = (dg * slope[g, t, cols]).astype(bf16)
                back[g, t, cols] = du
                gbe_ref[g:g + 1, cols] += jnp.sum(du.astype(f32), axis=0, keepdims=True)
                da = dot(du, wepad[g, :, cols], NT)
                acc = da if acc is None else acc + da
            parts.append(acc)
        dh2_s[t] += jnp.concatenate(join_windows(parts), axis=1)

    a_t = jnp.transpose(pre_low[...])
    df_t = jnp.transpose(df_low[...])
    for g in range(groups):
        rows = slice(per * g, per * g + per)
        gws_ref[g] += dot(df_t[rows], act[g])
        gwe_ref[g] += dot(a_t[rows], back[g])

    for t in chunks:
        da = dh2_s[t]
        xhat = xhat1[t]
        gvec_ref[1:2] += jnp.sum(da * xhat, axis=0, keepdims=True)
        gvec_ref[2:3] += jnp.sum(da, axis=0, keepdims=True)
        dx = da * mixed_gain
        dh1 = keep[t.start] * (dx - jnp.mean(dx, axis=-1, keepdims=True) - xhat * jnp.mean(dx * xhat, axis=-1, keepdims=True))
        gvec_ref[0:1] += jnp.sum(dh1, axis=0, keepdims=True)
        dh1_ref[0, t] = dh1
        dy = dh1.astype(bf16)
        df_low[t] = dy
        dc_ref[0, t] = (dot(dy, wo_ref[...], NT) * r_ref[0, t]).astype(bf16)
    gwo_ref[...] += dot(jnp.transpose(c_ref[0]), df_low[...])

    @pl.when(step == pl.num_programs(0) - 1)
    def _():
        half = width // 2
        for n in range(3):
            a = gwo_ref[:, 128 * n:128 * n + 128].astype(bf16)
            b = gwo_ref[:, half + 128 * n:half + 128 * n + 128].astype(bf16)
            first = mine_c == 0
            keep_w[width * n:width * n + width] = jnp.where(first, a, b)
            send_w[width * n:width * n + width] = jnp.where(first, b, a)
        for pos in range(4):
            near = mine_y == pos % 2
            base = jnp.where(near, 0, send_e.shape[0] // 2)
            most, rest = shard_lanes(pos, part)
            for i in range(groups):
                acc, g = ((gwe_ref, 2 * i) if 2 * i < groups else (gws_ref, 2 * i - groups))
                tiles = (acc[g, :, most:most + 128], acc[g + 1, :, most:most + 128], both_halves(
                    acc[g, :, rest:rest + 128], acc[g + 1, :, rest:rest + 128], pos % 2))
                for n, tile in enumerate(tiles):
                    first = per * (3 * i + n)
                    tile = tile.astype(bf16)
                    if pos // 2:
                        send_e[pl.ds(pl.multiple_of(base + first, 16), per)] = tile
                    else:
                        @pl.when(near)
                        def _():
                            near_e[first:first + per] = tile

                        @pl.when(jnp.logical_not(near))
                        def _():
                            far_e[first:first + per] = tile


def whole():
    return pl.BlockSpec(memory_space=pltpu.VMEM)


def feed(me, x, c, r, e, wo, shards, vectors):
    rows, length, width = x.shape
    groups = shards[0].shape[0]
    part = shards[0].shape[2] // 2
    hidden = 4 * part
    per = width // groups
    wide = row_spec((length, width))
    low = jax.ShapeDtypeStruct((rows, length, width), bf16)
    half_e = jax.ShapeDtypeStruct((groups * 3 * per, 128), bf16)
    flat_e = jax.ShapeDtypeStruct((2 * groups * 3 * per, 128), bf16)
    flat_w = jax.ShapeDtypeStruct((3 * width, 128), bf16)
    return pl.pallas_call(
        feed_kernel,
        grid=(rows,),
        in_specs=[pl.BlockSpec(memory_space=pltpu.SMEM), wide, wide, wide, wide] + [whole()] * 11,
        out_specs=[wide, wide, wide] + [whole()] * 7,
        out_shape=[low, jax.ShapeDtypeStruct((rows, length, width), f32), low, half_e, half_e, flat_e, flat_w, flat_w,
                   jax.ShapeDtypeStruct((8, width), f32), jax.ShapeDtypeStruct((8, hidden), f32)],
        scratch_shapes=[
            pltpu.VMEM((groups, 256, hidden), bf16),
            pltpu.VMEM((groups, hidden, 256), bf16),
            pltpu.VMEM((8, hidden), f32),
            pltpu.VMEM((groups, length, hidden), bf16),
            pltpu.VMEM((groups, length, hidden), f32),
            pltpu.VMEM((groups, length, hidden), bf16),
            pltpu.VMEM((length, width), f32),
            pltpu.VMEM((length, width), f32),
            pltpu.VMEM((length, width), bf16),
            pltpu.VMEM((length, width), bf16),
            pltpu.VMEM((width, width), f32),
            pltpu.VMEM((groups, per, hidden), f32),
            pltpu.VMEM((groups, per, hidden), f32),
        ],
        compiler_params=pltpu.CompilerParams(vmem_limit_bytes=VMEM_LIMIT),
        cost_estimate=pl.CostEstimate(flops=int(4e10), bytes_accessed=int(5e7), transcendentals=0),
        name="feed",
    )(me, x, c, r, e, wo, *shards, *vectors)


def attend_back_kernel(lanes_in, per, x_ref, q_ref, k_ref, v_ref, c_ref, dc_ref, p_ref, me_ref, vec_ref, gbe_ref,
                       prev_ref, dqkv_ref, out_ref, send_ref, token_ref, gacc, gvec_ref, flat_ref):
    step = pl.program_id(0)
    token_ref[...] = jnp.zeros(token_ref.shape, f32)
    groups = lanes_in // per

    @pl.when(step == 0)
    def _():
        gacc[...] = jnp.zeros(gacc.shape, f32)
        gvec_ref[...] = jnp.zeros(gvec_ref.shape, f32)

    low = lax.broadcasted_iota(jnp.int32, (1, 128), 1) < HEAD
    for pair in range(lanes_in // 128):
        lanes = slice(128 * pair, 128 * pair + 128)
        q2 = q_ref[0, :, lanes] * bf16(HEAD ** -0.5)
        k2 = k_ref[0, :, lanes]
        v_t = jnp.transpose(v_ref[0, :, lanes])
        zeros = jnp.zeros((HEAD, v_t.shape[1]), bf16)
        dc2 = dc_ref[0, :, lanes]
        prod = dc2.astype(f32) * c_ref[0, :, lanes].astype(f32)
        q_t = jnp.transpose(q2)
        dc_t = jnp.transpose(dc2)
        dq = None
        dk, dv = [], []
        for h in range(2):
            half = low if h == 0 else jnp.logical_not(low)
            rows = slice(64 * h, 64 * h + 64)
            km = jnp.where(half, k2, bf16(0))
            vm = jnp.concatenate([v_t[:HEAD], zeros] if h == 0 else [zeros, v_t[HEAD:]], axis=0)
            delta = jnp.sum(jnp.where(half, prod, 0.0), axis=-1, keepdims=True)
            pr = p_ref[0, 2 * pair + h]
            dp = dot(dc2, vm)
            ds = (pr.astype(f32) * (dp - delta)).astype(bf16)
            a = dot(ds, km)
            dq = a if dq is None else dq + a
            dk.append(dot(q_t[rows], ds))
            dv.append(dot(dc_t[rows], pr))
        dq = (dq * (HEAD ** -0.5)).astype(bf16)
        dk = jnp.transpose(jnp.concatenate(dk, axis=0)).astype(bf16)
        dv = jnp.transpose(jnp.concatenate(dv, axis=0)).astype(bf16)
        dqkv_ref[0, 0, :, lanes] = dq
        dqkv_ref[0, 1, :, lanes] = dk
        dqkv_ref[0, 2, :, lanes] = dv
        gvec_ref[0:1, lanes] += jnp.sum(dq.astype(f32), axis=0, keepdims=True)
        gvec_ref[1:2, lanes] += jnp.sum(dv.astype(f32), axis=0, keepdims=True)

    x_t = jnp.transpose(x_ref[0])
    for g in range(groups):
        base, _ = window(g, per)
        for j in range(3):
            gacc[j, g] += dot(x_t[per * g:per * g + per], dqkv_ref[0, j, :, base:base + 256])

    @pl.when(step == pl.num_programs(0) - 1)
    def _():
        base = 0
        if prev_ref is not None:
            base = prev_ref.shape[0]
            flat_ref[:base] = prev_ref[...]
        for j in range(3):
            a, b = gacc[j, 0], gacc[j, 1]
            cols = (a[:, :128], jnp.where(low, a[:, 128:], b[:, :128]), b[:, 128:])
            for n, col in enumerate(cols):
                first = base + per * (3 * j + n)
                flat_ref[first:first + per] = col.astype(bf16)
        first = base + 9 * per
        bits = [gvec_ref[:, 128 * n:128 * n + 128] for n in range(3)] + [jnp.zeros((8, 128), f32)]
        if vec_ref is not None:
            bits += [vec_ref[:, 128 * n:128 * n + 128] for n in range(vec_ref.shape[1] // 128)]
            part = gbe_ref.shape[1] // 4
            same = me_ref[0] % 2 == 0
            for f in range(4):
                y, core = f // 2, f % 2
                near = [gbe_ref[:, lane:lane + 128] for lane in shard_lanes(y + 2 * core, part)]
                far = [gbe_ref[:, lane:lane + 128] for lane in shard_lanes(y + 2 * (1 - core), part)]
                most, rest = (jnp.where(same, a, b) for a, b in zip(near, far))
                bits += [most, pltpu.roll(rest, 64, 1) if y else rest]
        left = flat_ref.shape[0] - first - 8 * len(bits)
        if left:
            bits.append(jnp.zeros((left, 128), f32))
        flat_ref[first:] = jnp.concatenate(bits, axis=0).astype(bf16)
        if send_ref is None:
            out_ref[...] = flat_ref[...]
        else:
            half = out_ref.shape[0]
            core = me_ref[0] % 2
            out_ref[...] = flat_ref[pl.ds(pl.multiple_of(core * half, 16), half)]
            send_ref[...] = flat_ref[pl.ds(pl.multiple_of((1 - core) * half, 16), half)]


TOKEN = jax.ShapeDtypeStruct((8, 128), f32)


def unused():
    return pl.BlockSpec(memory_space=pl.ANY)


def call_sum(kernel, args, shape, after):
    count = len(args)
    return pl.pallas_call(
        lambda *refs: kernel(*refs[:count], *refs[count + len(after):]),
        in_specs=[whole()] * count + [unused()] * len(after),
        out_specs=whole(),
        out_shape=jax.ShapeDtypeStruct(shape, bf16),
        compiler_params=pltpu.CompilerParams(vmem_limit_bytes=SMALL_LIMIT),
        name="add_up",
    )(*args, *after)


def add(arrays, halves=None, after=()):
    shape = arrays[0].shape
    starts = [(n or 0) * shape[0] for n in halves or [0] * len(arrays)]

    def kernel(*refs):
        acc = None
        for first, ref in zip(starts, refs):
            term = ref[first:first + shape[0]].astype(f32)
            acc = term if acc is None else acc + term
        refs[-1][...] = acc.astype(bf16)

    return call_sum(kernel, arrays, shape, after)


def add_both(keep_w, core_w, far_e, core_e):
    def kernel(kw_ref, cw_ref, fe_ref, ce_ref, w_ref, e_ref):
        w_ref[...] = (kw_ref[...].astype(f32) + cw_ref[...].astype(f32)).astype(bf16)
        half = fe_ref.shape[0]
        e_ref[...] = (fe_ref[...].astype(f32) + ce_ref[half:].astype(f32)).astype(bf16)

    return pl.pallas_call(
        kernel,
        in_specs=[whole()] * 4,
        out_specs=[whole()] * 2,
        out_shape=[jax.ShapeDtypeStruct(t.shape, bf16) for t in (keep_w, far_e)],
        compiler_params=pltpu.CompilerParams(vmem_limit_bytes=SMALL_LIMIT),
        name="add_up",
    )(keep_w, core_w, far_e, core_e)


def total(x, after=(), copies=0):
    shape = x.shape[1:]

    def kernel(x_ref, o_ref):
        acc = x_ref[0].astype(f32)
        for n in range(1, x_ref.shape[0]):
            acc = acc + x_ref[n].astype(f32)
        acc = acc.astype(bf16)
        if copies:
            for n in range(copies):
                o_ref[n] = acc
        else:
            o_ref[...] = acc

    return call_sum(kernel, (x,), (copies,) + shape if copies else shape, after)


def attend_back(x, q, k, v, c, dc, p, part, me, per, vec=None, gbe=None, prev=None, devices=1, after=()):
    rows, length, width = x.shape
    lanes = width // 2
    heads = HEADS // 2
    wide = pl.BlockSpec((1, length, lanes), lambda r: (r, 0, part))
    args = [x, q, k, v, c, dc, p, me]
    specs = [wide] * 6 + [pl.BlockSpec((1, heads, length, length), lambda r: (r, part, 0, 0)),
                          pl.BlockSpec(memory_space=pltpu.SMEM)]
    flat = 9 * per + 32
    dqkv = jax.ShapeDtypeStruct((rows, 3, length, lanes), bf16)
    if prev is None:
        args += [vec, gbe]
        specs += [whole(), whole()]
        flat += 8 * (width // 128) + 64
        outs = [jax.ShapeDtypeStruct((flat, 128), bf16)]
        pick = lambda refs: (refs[8], refs[9], None) + refs[10:12] + (None,) + refs[12:]
    else:
        args.append(prev)
        specs.append(whole())
        flat = -(-(prev.shape[0] + flat) // (8 * devices)) * 8 * devices
        outs = [jax.ShapeDtypeStruct((flat // 2, 128), bf16)] * 2
        pick = lambda refs: (None, None, refs[8]) + refs[9:]
    return pl.pallas_call(
        lambda *refs: attend_back_kernel(lanes, per, *refs[:8], *pick(refs[:len(args)] + refs[len(args) + len(after):])),
        grid=(rows,),
        in_specs=specs + [unused()] * len(after),
        out_specs=[pl.BlockSpec((1, 3, length, lanes), lambda r: (r, 0, 0, 0))] + [whole()] * (len(outs) + 1),
        out_shape=[dqkv] + outs + [TOKEN],
        scratch_shapes=[
            pltpu.VMEM((3, lanes // per, per, 256), f32),
            pltpu.VMEM((8, lanes), f32),
            pltpu.VMEM((flat, 128), bf16),
        ],
        compiler_params=pltpu.CompilerParams(vmem_limit_bytes=VMEM_LIMIT),
        cost_estimate=pl.CostEstimate(flops=int(2e10), bytes_accessed=int(3e7), transcendentals=0),
        name="attend_back",
    )(*args, *after)


def input_grad_kernel(dh1_ref, d0_ref, d1_ref, wq_ref, wk_ref, wv_ref, dx_ref, token_ref, wpad):
    token_ref[...] = jnp.zeros(token_ref.shape, f32)
    groups, per = wq_ref.shape[0], wq_ref.shape[1]

    @pl.when(pl.program_id(0) == 0)
    def _():
        for j, w_ref in enumerate((wq_ref, wk_ref, wv_ref)):
            for g in range(groups):
                _, off = window(g, per)
                wpad[j, g] = pad_rows(pad_cols(w_ref[g], off), off)

    half = d0_ref.shape[3]
    parts = []
    for g in range(groups):
        base, _ = window(g, per)
        d_ref = (d0_ref, d1_ref)[base // half]
        acc = None
        for j in range(3):
            t = dot(d_ref[0, j, :, base % half:base % half + 256], wpad[j, g], NT)
            acc = t if acc is None else acc + t
        parts.append(acc)
    for n, col in enumerate(join_windows(parts)):
        lanes = slice(128 * n, 128 * n + 128)
        dx_ref[0, :, lanes] = (col + dh1_ref[0, :, lanes]).astype(bf16)


def input_grad(dh1, d0, d1, wq, wk, wv, half, prev=None, after=()):
    rows, length, width = dh1.shape
    count = rows // 2 if half == 0 else rows - rows // 2
    first = half * (rows // 2)
    wide = pl.BlockSpec((1, length, width), lambda r: (r + first, 0, 0))
    back = pl.BlockSpec((1, 3, length, width // 2), lambda r: (r + first, 0, 0, 0))
    args = [dh1, d0, d1, wq, wk, wv]
    extra = list(after)
    aliases = {}
    if prev is not None:
        aliases = {len(args) + len(extra): 0}
        extra.append(prev)
    return pl.pallas_call(
        lambda *refs: input_grad_kernel(*refs[:len(args)], *refs[len(args) + len(extra):]),
        grid=(count,),
        in_specs=[wide, back, back] + [full(wq.shape)] * 3 + [unused()] * len(extra),
        out_specs=[wide, whole()],
        out_shape=[jax.ShapeDtypeStruct((rows, length, width), bf16), TOKEN],
        input_output_aliases=aliases,
        scratch_shapes=[pltpu.VMEM((3, wq.shape[0], 256, 256), bf16)],
        compiler_params=pltpu.CompilerParams(vmem_limit_bytes=GRAD_LIMIT),
        cost_estimate=pl.CostEstimate(flops=int(5e9), bytes_accessed=int(1e7), transcendentals=0),
        name="input_grad",
    )(*args, *extra)


def unpack_kernel(order, me_ref, *refs):
    count = len(order)
    pieces, w_ref, own_ref, other_ref = refs[:count], *refs[count:count + 3]
    refs = refs[1:]
    gexp_ref, gshr_ref, gout_ref, gq_ref, gk_ref, gv_ref, gbe_ref = refs[count + 2:count + 9]
    vecs, (e_ref, flat_w, q_ref) = refs[count + 9:count + 17], refs[count + 17:]
    groups, per = gq_ref.shape[0], gq_ref.shape[1]
    width = gout_ref.shape[0]
    part = gexp_ref.shape[2]
    size = pieces[0].shape[0]
    for bit, piece in zip(order, pieces):
        place = pl.multiple_of((me_ref[1] ^ bit) * size, 8)
        e_ref[pl.ds(place, size)] = piece[...].astype(f32)
    size = w_ref.shape[1]
    for i in range(w_ref.shape[0]):
        place = i % 2 * (flat_w.shape[0] // 2) + i // 2 * size
        flat_w[place:place + size] = w_ref[i].astype(f32)
    for i in range(groups):
        first = 3 * per * i
        a = e_ref[first:first + per]
        b = e_ref[first + per:first + 2 * per]
        mix = e_ref[first + 2 * per:first + 3 * per]
        one = jnp.concatenate([a, mix], axis=1)
        two = jnp.concatenate([b, pltpu.roll(mix, 64, 1)], axis=1)
        if 2 * i < groups:
            gexp_ref[2 * i] = one[:, :part]
            gexp_ref[2 * i + 1] = two[:, :part]
        else:
            gshr_ref[2 * i - groups] = jnp.transpose(one)[:part]
            gshr_ref[2 * i - groups + 1] = jnp.transpose(two)[:part]
    half = own_ref.shape[0]
    core = me_ref[0] % 2
    q_ref[pl.ds(pl.multiple_of(core * half, 16), half)] = own_ref[...]
    q_ref[pl.ds(pl.multiple_of((1 - core) * half, 16), half)] = other_ref[...]
    for n in range(width // 128):
        gout_ref[:, 128 * n:128 * n + 128] = flat_w[width * n:width * n + width]
    tiles = width // 128
    used = 9 * per + 32
    start = used + 8 * tiles + 64
    got = {n: [] for n in range(8)}
    for half, flat in enumerate((q_ref[:start], q_ref[start:start + used])):
        for j, out in enumerate((gq_ref, gk_ref, gv_ref)):
            cols = [flat[per * (3 * j + n):per * (3 * j + n) + per].astype(f32) for n in range(3)]
            out[2 * half] = jnp.concatenate(cols[:2], axis=1)[:, :per]
            out[2 * half + 1] = pltpu.roll(jnp.concatenate(cols[1:], axis=1), 192, 1)[:, :per]
        ends = flat[9 * per:9 * per + 32].astype(f32)
        for m, bias in enumerate((QUERY_BIAS, VALUE_BIAS)):
            got[bias] += [ends[8 * n + m:8 * n + m + 1] for n in range(3)]
    rows = q_ref[used:used + 8 * tiles].astype(f32)
    for m in range(6):
        got[m] = [rows[8 * n + m:8 * n + m + 1] for n in range(tiles)]
    for m, vec in enumerate(vecs):
        vec[...] = jnp.concatenate(got[m], axis=1).reshape(width)
    blocks = q_ref[used + 8 * tiles:start].astype(f32)
    pick = blocks[:16]
    for f in range(1, 4):
        pick = jnp.where(me_ref[0] == f, blocks[16 * f:16 * f + 16], pick)
    gbe_ref[...] = jnp.concatenate([pick[:8], pick[8:]], axis=1)[:groups, :part]


def unpack(place, order, pieces, w, own, other, groups, per, width, part):
    shapes = [(groups, per, part), (groups, part, per), (width, width)] + [(groups, per, per)] * 3 + [
        (groups, part)] + [(width,)] * 8
    return pl.pallas_call(
        functools.partial(unpack_kernel, order),
        in_specs=[pl.BlockSpec(memory_space=pltpu.SMEM)] + [whole()] * (len(pieces) + 3),
        out_specs=[whole()] * len(shapes),
        out_shape=[jax.ShapeDtypeStruct(t, f32) for t in shapes],
        scratch_shapes=[pltpu.VMEM((len(pieces) * pieces[0].shape[0], 128), f32),
                        pltpu.VMEM((w.shape[0] * w.shape[1], 128), f32),
                        pltpu.VMEM((2 * own.shape[0], 128), bf16)],
        compiler_params=pltpu.CompilerParams(vmem_limit_bytes=SMALL_LIMIT),
        name="unpack",
    )(place, *pieces, w, own, other)


def exchange(x, axes, groups=None):
    return lax.all_to_all(x, axes, 0, 0, axis_index_groups=groups, tiled=True)


def on_device(
    inputs,
    doc_ids,
    cotangent,
    query_weight,
    query_bias,
    key_weight,
    value_weight,
    value_bias,
    out_weight,
    out_bias,
    mixed_gain,
    mixed_bias,
    expand_weight,
    expand_bias,
    shrink_weight,
    shrink_bias,
    final_gain,
    final_bias,
):
    micro, rows_dev, length, width = inputs.shape
    rows = micro * rows_dev
    groups, per, part = expand_weight.shape
    x = inputs.reshape(rows, length, width)
    docs = doc_ids.reshape(rows, 1, length)
    cot = cotangent.reshape(rows, length, width)
    dp = lax.axis_size("dp")
    everyone = ("dp", "ffn")
    count = 4 * dp
    me = lax.axis_index("ffn").astype(jnp.int32).reshape(1)
    like = [[4 * d + 2 * y + core for d in range(dp) for y in range(2)] for core in range(2)]

    def swap(array, bit):
        return lax.ppermute(array, "ffn", [(f, f ^ bit) for f in range(4)])

    bias = jnp.pad(expand_bias[:, None], ((0, 0), (0, 15), (0, part)))
    shard = jnp.concatenate([jnp.concatenate([expand_weight, shrink_weight], axis=2), bias], axis=1)
    shards = [shard] + [swap(shard, bit) for bit in (1, 2, 3)]
    q, k, v, c, r, p = attend(x, docs, query_weight, key_weight, value_weight, query_bias, value_bias)
    result, dh1, dc, near_e, far_e, send_e, keep_w, send_w, gvec, gbe = feed(
        me, x, c, r, cot, out_weight, shards, (out_bias, mixed_gain, mixed_bias, shrink_bias, final_gain, final_bias)
    )

    core_w = swap(send_w, 1)
    core_e = swap(send_e, 1)
    sum_w, far = add_both(keep_w, core_w, far_e, core_e)
    got_w = exchange(sum_w.reshape(2 * dp, -1, 128), everyone, like)
    far_got = swap(far, 2)
    back = functools.partial(attend_back, x, q, k, v, c, dc, p, me=me, per=per)
    d0, flat0, done_0 = back(part=0, vec=gvec, gbe=gbe, after=(far, sum_w))
    piece_w = total(got_w, after=(done_0,))
    sum_e = add((near_e, core_e, far_got), (None, 0, None), after=(piece_w,))
    got_e = exchange(sum_e.reshape(dp, -1, 128), "dp")
    all_w = lax.all_gather(piece_w, everyone)
    d1, keep_q, send_q, done_1 = back(part=1, prev=flat0, devices=count, after=(sum_e, piece_w))
    piece_e = total(got_e, after=(done_1,))
    order, pieces = [0], [piece_e]
    bit = dp // 2
    while bit:
        pieces = pieces + [lax.ppermute(t, "dp", [(d, d ^ bit) for d in range(dp)]) for t in pieces]
        order = order + [n ^ bit for n in order]
        bit //= 2
    sum_q = add((keep_q, swap(send_q, 1)))
    got_q = exchange(sum_q.reshape(2 * dp, -1, 128), everyone, like)
    back_weights = (query_weight, key_weight, value_weight)
    dx, _ = input_grad(dh1, d0, d1, *back_weights, half=0, after=(sum_q, pieces[1]))
    dx, done_2 = input_grad(dh1, d0, d1, *back_weights, half=1, prev=dx, after=pieces[2:4])
    piece_q = total(got_q, after=(done_2, all_w[0, :8], *pieces[4:]), copies=2 * dp)
    own_q = exchange(piece_q, everyone, like).reshape(-1, 128)
    other_q = swap(own_q, 1)
    place = jnp.stack([lax.axis_index("ffn"), lax.axis_index("dp")]).astype(jnp.int32)
    gexp, gshr, gout, gq, gk, gv, gbe, *vecs = unpack(
        place, order, pieces, all_w, own_q, other_q, groups, per, width, part
    )
    return (
        result.reshape(inputs.shape),
        dx.reshape(inputs.shape),
        gq,
        vecs[QUERY_BIAS],
        gk,
        gv,
        vecs[VALUE_BIAS],
        gout,
        vecs[OUT_BIAS],
        vecs[MIXED_GAIN],
        vecs[MIXED_BIAS],
        gexp,
        gbe,
        gshr,
        vecs[SHRINK_BIAS],
        vecs[FINAL_GAIN],
        vecs[FINAL_BIAS],
    )


def solution(mesh):
    in_specs = (
        P(None, ("dp", "ffn"), None, None),
        P(None, ("dp", "ffn"), None),
        P(None, ("dp", "ffn"), None, None),
        P(),
        P(),
        P(),
        P(),
        P(),
        P(),
        P(),
        P(),
        P(),
        P(None, None, "ffn"),
        P(None, "ffn"),
        P(None, "ffn", None),
        P(),
        P(),
        P(),
    )
    out_specs = (
        P(None, ("dp", "ffn"), None, None),
        P(None, ("dp", "ffn"), None, None),
        P(),
        P(),
        P(),
        P(),
        P(),
        P(),
        P(),
        P(),
        P(),
        P(None, None, "ffn"),
        P(None, "ffn"),
        P(None, "ffn", None),
        P(),
        P(),
        P(),
    )
    return jax.shard_map(
        on_device, mesh=mesh, in_specs=in_specs, out_specs=out_specs, check_vma=False
    )
```

```python
import functools

import jax
import jax.numpy as jnp
from jax import lax
from jax.experimental import pallas as pl
from jax.experimental.pallas import tpu as pltpu
from jax.sharding import PartitionSpec as P

HEADS = 12
HEAD = 64
DOCS = 4
CHUNK = 256
epsilon = 1e-05
masked_score = -1e30
bf16 = jnp.bfloat16
f32 = jnp.float32
VMEM_LIMIT = 60 * 1024 * 1024
SMALL_LIMIT = 30 * 1024 * 1024
GRAD_LIMIT = 30 * 1024 * 1024

OUT_BIAS, MIXED_GAIN, MIXED_BIAS, SHRINK_BIAS, FINAL_GAIN, FINAL_BIAS, QUERY_BIAS, VALUE_BIAS = range(8)

NN = (((1,), (0,)), ((), ()))
NT = (((1,), (1,)), ((), ()))
TN = (((0,), (0,)), ((), ()))


def dot(a, b, dims=NN):
    return lax.dot_general(a, b, dims, preferred_element_type=f32)


def window(group, width):
    start = group * width
    base = start // 128 * 128
    return base, start - base


def shift_matrix(rows, cols, offset, low=0):
    r = lax.broadcasted_iota(jnp.int32, (rows, cols), 0) + offset
    c = lax.broadcasted_iota(jnp.int32, (rows, cols), 1)
    return jnp.where((c == r) & (c >= low), 1.0, 0.0).astype(bf16)


def as_row(ref):
    return ref[...].astype(f32).reshape(1, ref.shape[0])


def pad_cols(w, offset):
    return dot(w, shift_matrix(w.shape[1], 256, offset)).astype(bf16)


def pad_rows(w, offset):
    rows = w.shape[0]
    parts = []
    if offset:
        parts.append(jnp.zeros((offset, w.shape[1]), bf16))
    parts.append(w)
    if 256 - offset - rows:
        parts.append(jnp.zeros((256 - offset - rows, w.shape[1]), bf16))
    return jnp.concatenate(parts, axis=0)


def join_windows(parts):
    out = []
    for i in range(0, len(parts), 2):
        a, b = parts[i], parts[i + 1]
        out += [a[:, :128], a[:, 128:] + b[:, :128], b[:, 128:]]
    return out


def attend_kernel(x_ref, docs_ref, wq_ref, wk_ref, wv_ref, qb_ref, vb_ref,
                  q_ref, k_ref, v_ref, c_ref, r_ref, p_ref, wpad):
    length = x_ref.shape[1]
    width = x_ref.shape[2]
    groups = wq_ref.shape[0]
    per = width // groups

    @pl.when(pl.program_id(0) == 0)
    def _():
        for j, w_ref in enumerate((wq_ref, wk_ref, wv_ref)):
            for g in range(groups):
                _, off = window(g, per)
                wpad[j, g] = pad_rows(pad_cols(w_ref[g], off), off)

    for j, (out, b_ref) in enumerate(((q_ref, qb_ref), (k_ref, None), (v_ref, vb_ref))):
        bias = None if b_ref is None else as_row(b_ref)
        parts = []
        for g in range(groups):
            base, _ = window(g, per)
            parts.append(dot(x_ref[0, :, base:base + 256], wpad[j, g]))
        for n, col in enumerate(join_windows(parts)):
            if bias is not None:
                col = col + bias[:, 128 * n:128 * n + 128]
            out[0, :, 128 * n:128 * n + 128] = col.astype(bf16)

    docs = docs_ref[0].astype(f32)
    down = jnp.transpose(jnp.broadcast_to(docs, (128, length)))
    lane = lax.broadcasted_iota(jnp.int32, (1, 128), 1)
    same = down == lane.astype(f32)
    doc_q = jnp.where(same & (lane < DOCS), 1.0, 0.0).astype(bf16)
    doc_k = jnp.where(same | (lane >= DOCS), 0.0, masked_score).astype(bf16)
    low = lane < HEAD
    for pair in range(HEADS // 2):
        lanes = slice(128 * pair, 128 * pair + 128)
        q2 = jnp.concatenate([q_ref[0, :, lanes] * bf16(HEAD ** -0.5), doc_q], axis=1)
        k2 = k_ref[0, :, lanes]
        v2 = v_ref[0, :, lanes]
        acc = None
        for h in range(2):
            half = low if h == 0 else jnp.logical_not(low)
            km = jnp.concatenate([jnp.where(half, k2, bf16(0)), doc_k], axis=1)
            ones = jnp.broadcast_to(jnp.where(half, 1.0, 0.0), (length, 128)).astype(bf16)
            vm = jnp.concatenate([jnp.where(half, v2, bf16(0)), ones], axis=1)
            s = dot(q2, km, NT)
            top = jnp.max(s, axis=-1, keepdims=True)
            pr = jnp.exp(s - top).astype(bf16)
            p_ref[0, 2 * pair + h] = pr
            c = dot(pr, vm)
            acc = c if acc is None else acc + c
        inverse = 1.0 / acc[:, 128:]
        r_ref[0, :, lanes] = inverse
        c_ref[0, :, lanes] = (acc[:, :128] * inverse).astype(bf16)


def full(shape):
    return pl.BlockSpec(shape, lambda *_: (0,) * len(shape))


def row_spec(shape):
    return pl.BlockSpec((1,) + shape, lambda r: (r,) + (0,) * len(shape))


def attend(x, docs, wq, wk, wv, qb, vb):
    rows, length, width = x.shape
    wide = row_spec((length, width))
    low = jax.ShapeDtypeStruct((rows, length, width), bf16)
    return pl.pallas_call(
        attend_kernel,
        grid=(rows,),
        in_specs=[wide, row_spec((1, length)), full(wq.shape), full(wk.shape), full(wv.shape),
                  whole(), whole()],
        out_specs=[wide, wide, wide, wide, wide, row_spec((HEADS, length, length))],
        out_shape=[low, low, low, low, jax.ShapeDtypeStruct((rows, length, width), f32), jax.ShapeDtypeStruct((rows, HEADS, length, length), bf16)],
        scratch_shapes=[pltpu.VMEM((3, wq.shape[0], 256, 256), bf16)],
        compiler_params=pltpu.CompilerParams(vmem_limit_bytes=VMEM_LIMIT),
        cost_estimate=pl.CostEstimate(flops=int(2e10), bytes_accessed=int(5e7), transcendentals=0),
        name="attend",
    )(x, docs, wq, wk, wv, qb, vb)


def gelu_both(u):
    cdf = 0.5 * (1.0 + lax.erf(u * 0.7071067811865476))
    pdf = jnp.exp(-0.5 * u * u) * 0.3989422804014327
    return u * cdf, cdf + u * pdf


def low_half():
    return lax.broadcasted_iota(jnp.int32, (1, 128), 1) < 64


def shard_lanes(pos, part):
    start = pos * part
    if start % 128 == 0:
        return start, start + 128
    return start + 64, start - 64


def both_halves(a, b, odd):
    if odd:
        return jnp.where(low_half(), pltpu.roll(a, 64, 1), b)
    return jnp.where(low_half(), a, pltpu.roll(b, 64, 1))


def feed_kernel(me_ref, x_ref, c_ref, r_ref, e_ref, wo_ref, w0_ref, w1_ref, w2_ref, w3_ref, ob_ref, mg_ref, mb_ref, sb_ref, fg_ref, fb_ref,
                result_ref, dh1_ref, dc_ref, near_e, far_e, send_e, keep_w, send_w, gvec_ref, gbe_ref,
                wepad, wspad, be_s, act, slope, back, xhat1, dh2_s, pre_low, df_low, gwo_ref, gwe_ref, gws_ref):
    step = pl.program_id(0)
    groups, width = w0_ref.shape[0], x_ref.shape[2]
    per = width // groups
    part = w0_ref.shape[2] // 2
    hidden = 4 * part
    mine_y = me_ref[0] // 2
    mine_c = me_ref[0] % 2

    @pl.when(step == 0)
    def _():
        gwo_ref[...] = jnp.zeros(gwo_ref.shape, f32)
        gwe_ref[...] = jnp.zeros(gwe_ref.shape, f32)
        gws_ref[...] = jnp.zeros(gws_ref.shape, f32)
        gbe_ref[...] = jnp.zeros(gbe_ref.shape, f32)
        gvec_ref[...] = jnp.zeros(gvec_ref.shape, f32)
        for g in range(groups):
            _, off = window(g, per)
            wide, tall, bias = [], [], []
            for pos in range(4):
                y, dc = pos % 2, pos // 2
                near, far = ((w0_ref, w2_ref), (w1_ref, w3_ref))[dc]
                own = mine_y == y
                blk = jnp.where(own, near[g], far[g])
                e = blk[:per, :256].astype(f32)[:, :part]
                s_ = dot(blk[:part, 128:], shift_matrix(256, 256, off - 64, off)).astype(bf16)
                b = blk[per:, :256].astype(f32)[:1, :part]
                if pos % 2:
                    wide += [e[:, 128:], e[:, :128]]
                    tall += [s_[128:], s_[:128]]
                    bias += [b[:, 128:], b[:, :128]]
                else:
                    wide.append(e)
                    tall.append(s_)
                    bias.append(b)
            wepad[g] = pad_rows(jnp.concatenate(wide, axis=1).astype(bf16), off)
            wspad[g] = jnp.concatenate(tall, axis=0)
            be_s[g:g + 1] = jnp.concatenate(bias, axis=1)

    out_bias, mixed_gain, mixed_bias = as_row(ob_ref), as_row(mg_ref), as_row(mb_ref)
    shrink_bias, final_gain, final_bias = as_row(sb_ref), as_row(fg_ref), as_row(fb_ref)
    length = x_ref.shape[1]
    chunks = [slice(first, first + CHUNK) for first in range(0, length, CHUNK)]
    keep = {}
    for t in chunks:
        h1 = x_ref[0, t].astype(f32) + dot(c_ref[0, t], wo_ref[...]) + out_bias
        cen = h1 - jnp.mean(h1, axis=-1, keepdims=True)
        rstd1 = lax.rsqrt(jnp.mean(cen * cen, axis=-1, keepdims=True) + epsilon)
        xhat = cen * rstd1
        xhat1[t] = xhat
        a_low = (xhat * mixed_gain + mixed_bias).astype(bf16)
        pre_low[t] = a_low
        keep[t.start] = rstd1

    for t in chunks:
        parts = []
        for g in range(groups):
            base, _ = window(g, per)
            for n in range(hidden // 256):
                cols = slice(256 * n, 256 * n + 256)
                u = dot(pre_low[t, base:base + 256], wepad[g, :, cols]) + be_s[g:g + 1, cols]
                val, slp = gelu_both(u)
                act[g, t, cols] = val.astype(bf16)
                slope[g, t, cols] = slp
            parts.append(dot(act[g, t], wspad[g]))
        f = jnp.concatenate(join_windows(parts), axis=1)
        h2 = (xhat1[t] * mixed_gain + mixed_bias) + f + shrink_bias
        cen = h2 - jnp.mean(h2, axis=-1, keepdims=True)
        rstd2 = lax.rsqrt(jnp.mean(cen * cen, axis=-1, keepdims=True) + epsilon)
        xhat2 = cen * rstd2
        result_ref[0, t] = (xhat2 * final_gain + final_bias).astype(bf16)

        up = e_ref[0, t].astype(f32)
        gvec_ref[4:5] += jnp.sum(up * xhat2, axis=0, keepdims=True)
        gvec_ref[5:6] += jnp.sum(up, axis=0, keepdims=True)
        dx = up * final_gain
        dh2 = rstd2 * (dx - jnp.mean(dx, axis=-1, keepdims=True) - xhat2 * jnp.mean(dx * xhat2, axis=-1, keepdims=True))
        gvec_ref[3:4] += jnp.sum(dh2, axis=0, keepdims=True)
        dh2_s[t] = dh2
        df_low[t] = dh2.astype(bf16)

    for t in chunks:
        parts = []
        for g in range(groups):
            base, _ = window(g, per)
            acc = None
            for n in range(hidden // 256):
                cols = slice(256 * n, 256 * n + 256)
                dg = dot(df_low[t, base:base + 256], wspad[g, cols, :], NT)
                du = (dg * slope[g, t, cols]).astype(bf16)
                back[g, t, cols] = du
                gbe_ref[g:g + 1, cols] += jnp.sum(du.astype(f32), axis=0, keepdims=True)
                da = dot(du, wepad[g, :, cols], NT)
                acc = da if acc is None else acc + da
            parts.append(acc)
        dh2_s[t] += jnp.concatenate(join_windows(parts), axis=1)

    a_t = jnp.transpose(pre_low[...])
    df_t = jnp.transpose(df_low[...])
    for g in range(groups):
        rows = slice(per * g, per * g + per)
        gws_ref[g] += dot(df_t[rows], act[g])
        gwe_ref[g] += dot(a_t[rows], back[g])

    for t in chunks:
        da = dh2_s[t]
        xhat = xhat1[t]
        gvec_ref[1:2] += jnp.sum(da * xhat, axis=0, keepdims=True)
        gvec_ref[2:3] += jnp.sum(da, axis=0, keepdims=True)
        dx = da * mixed_gain
        dh1 = keep[t.start] * (dx - jnp.mean(dx, axis=-1, keepdims=True) - xhat * jnp.mean(dx * xhat, axis=-1, keepdims=True))
        gvec_ref[0:1] += jnp.sum(dh1, axis=0, keepdims=True)
        dh1_ref[0, t] = dh1
        dy = dh1.astype(bf16)
        df_low[t] = dy
        dc_ref[0, t] = (dot(dy, wo_ref[...], NT) * r_ref[0, t]).astype(bf16)
    gwo_ref[...] += dot(jnp.transpose(c_ref[0]), df_low[...])

    @pl.when(step == pl.num_programs(0) - 1)
    def _():
        half = width // 2
        for n in range(3):
            a = gwo_ref[:, 128 * n:128 * n + 128].astype(bf16)
            b = gwo_ref[:, half + 128 * n:half + 128 * n + 128].astype(bf16)
            first = mine_c == 0
            keep_w[width * n:width * n + width] = jnp.where(first, a, b)
            send_w[width * n:width * n + width] = jnp.where(first, b, a)
        for pos in range(4):
            near = mine_y == pos % 2
            base = jnp.where(near, 0, send_e.shape[0] // 2)
            most, rest = shard_lanes(pos, part)
            for i in range(groups):
                acc, g = ((gwe_ref, 2 * i) if 2 * i < groups else (gws_ref, 2 * i - groups))
                tiles = (acc[g, :, most:most + 128], acc[g + 1, :, most:most + 128], both_halves(
                    acc[g, :, rest:rest + 128], acc[g + 1, :, rest:rest + 128], pos % 2))
                for n, tile in enumerate(tiles):
                    first = per * (3 * i + n)
                    tile = tile.astype(bf16)
                    if pos // 2:
                        send_e[pl.ds(pl.multiple_of(base + first, 16), per)] = tile
                    else:
                        @pl.when(near)
                        def _():
                            near_e[first:first + per] = tile

                        @pl.when(jnp.logical_not(near))
                        def _():
                            far_e[first:first + per] = tile


def whole():
    return pl.BlockSpec(memory_space=pltpu.VMEM)


def feed(me, x, c, r, e, wo, shards, vectors):
    rows, length, width = x.shape
    groups = shards[0].shape[0]
    part = shards[0].shape[2] // 2
    hidden = 4 * part
    per = width // groups
    wide = row_spec((length, width))
    low = jax.ShapeDtypeStruct((rows, length, width), bf16)
    half_e = jax.ShapeDtypeStruct((groups * 3 * per, 128), bf16)
    flat_e = jax.ShapeDtypeStruct((2 * groups * 3 * per, 128), bf16)
    flat_w = jax.ShapeDtypeStruct((3 * width, 128), bf16)
    return pl.pallas_call(
        feed_kernel,
        grid=(rows,),
        in_specs=[pl.BlockSpec(memory_space=pltpu.SMEM), wide, wide, wide, wide] + [whole()] * 11,
        out_specs=[wide, wide, wide] + [whole()] * 7,
        out_shape=[low, jax.ShapeDtypeStruct((rows, length, width), f32), low, half_e, half_e, flat_e, flat_w, flat_w,
                   jax.ShapeDtypeStruct((8, width), f32), jax.ShapeDtypeStruct((8, hidden), f32)],
        scratch_shapes=[
            pltpu.VMEM((groups, 256, hidden), bf16),
            pltpu.VMEM((groups, hidden, 256), bf16),
            pltpu.VMEM((8, hidden), f32),
            pltpu.VMEM((groups, length, hidden), bf16),
            pltpu.VMEM((groups, length, hidden), f32),
            pltpu.VMEM((groups, length, hidden), bf16),
            pltpu.VMEM((length, width), f32),
            pltpu.VMEM((length, width), f32),
            pltpu.VMEM((length, width), bf16),
            pltpu.VMEM((length, width), bf16),
            pltpu.VMEM((width, width), f32),
            pltpu.VMEM((groups, per, hidden), f32),
            pltpu.VMEM((groups, per, hidden), f32),
        ],
        compiler_params=pltpu.CompilerParams(vmem_limit_bytes=VMEM_LIMIT),
        cost_estimate=pl.CostEstimate(flops=int(4e10), bytes_accessed=int(5e7), transcendentals=0),
        name="feed",
    )(me, x, c, r, e, wo, *shards, *vectors)


def attend_back_kernel(lanes_in, per, x_ref, q_ref, k_ref, v_ref, c_ref, dc_ref, p_ref, me_ref, vec_ref, gbe_ref,
                       prev_ref, dqkv_ref, out_ref, send_ref, token_ref, gacc, gvec_ref, flat_ref):
    step = pl.program_id(0)
    token_ref[...] = jnp.zeros(token_ref.shape, f32)
    groups = lanes_in // per

    @pl.when(step == 0)
    def _():
        gacc[...] = jnp.zeros(gacc.shape, f32)
        gvec_ref[...] = jnp.zeros(gvec_ref.shape, f32)

    low = lax.broadcasted_iota(jnp.int32, (1, 128), 1) < HEAD
    for pair in range(lanes_in // 128):
        lanes = slice(128 * pair, 128 * pair + 128)
        q2 = q_ref[0, :, lanes] * bf16(HEAD ** -0.5)
        k2 = k_ref[0, :, lanes]
        v_t = jnp.transpose(v_ref[0, :, lanes])
        zeros = jnp.zeros((HEAD, v_t.shape[1]), bf16)
        dc2 = dc_ref[0, :, lanes]
        prod = dc2.astype(f32) * c_ref[0, :, lanes].astype(f32)
        q_t = jnp.transpose(q2)
        dc_t = jnp.transpose(dc2)
        dq = None
        dk, dv = [], []
        for h in range(2):
            half = low if h == 0 else jnp.logical_not(low)
            rows = slice(64 * h, 64 * h + 64)
            km = jnp.where(half, k2, bf16(0))
            vm = jnp.concatenate([v_t[:HEAD], zeros] if h == 0 else [zeros, v_t[HEAD:]], axis=0)
            delta = jnp.sum(jnp.where(half, prod, 0.0), axis=-1, keepdims=True)
            pr = p_ref[0, 2 * pair + h]
            dp = dot(dc2, vm)
            ds = (pr.astype(f32) * (dp - delta)).astype(bf16)
            a = dot(ds, km)
            dq = a if dq is None else dq + a
            dk.append(dot(q_t[rows], ds))
            dv.append(dot(dc_t[rows], pr))
        dq = (dq * (HEAD ** -0.5)).astype(bf16)
        dk = jnp.transpose(jnp.concatenate(dk, axis=0)).astype(bf16)
        dv = jnp.transpose(jnp.concatenate(dv, axis=0)).astype(bf16)
        dqkv_ref[0, 0, :, lanes] = dq
        dqkv_ref[0, 1, :, lanes] = dk
        dqkv_ref[0, 2, :, lanes] = dv
        gvec_ref[0:1, lanes] += jnp.sum(dq.astype(f32), axis=0, keepdims=True)
        gvec_ref[1:2, lanes] += jnp.sum(dv.astype(f32), axis=0, keepdims=True)

    x_t = jnp.transpose(x_ref[0])
    for g in range(groups):
        base, _ = window(g, per)
        for j in range(3):
            gacc[j, g] += dot(x_t[per * g:per * g + per], dqkv_ref[0, j, :, base:base + 256])

    @pl.when(step == pl.num_programs(0) - 1)
    def _():
        base = 0
        if prev_ref is not None:
            base = prev_ref.shape[0]
            flat_ref[:base] = prev_ref[...]
        for j in range(3):
            a, b = gacc[j, 0], gacc[j, 1]
            cols = (a[:, :128], jnp.where(low, a[:, 128:], b[:, :128]), b[:, 128:])
            for n, col in enumerate(cols):
                first = base + per * (3 * j + n)
                flat_ref[first:first + per] = col.astype(bf16)
        first = base + 9 * per
        bits = [gvec_ref[:, 128 * n:128 * n + 128] for n in range(3)] + [jnp.zeros((8, 128), f32)]
        if vec_ref is not None:
            bits += [vec_ref[:, 128 * n:128 * n + 128] for n in range(vec_ref.shape[1] // 128)]
            part = gbe_ref.shape[1] // 4
            same = me_ref[0] % 2 == 0
            for f in range(4):
                y, core = f // 2, f % 2
                near = [gbe_ref[:, lane:lane + 128] for lane in shard_lanes(y + 2 * core, part)]
                far = [gbe_ref[:, lane:lane + 128] for lane in shard_lanes(y + 2 * (1 - core), part)]
                most, rest = (jnp.where(same, a, b) for a, b in zip(near, far))
                bits += [most, pltpu.roll(rest, 64, 1) if y else rest]
        left = flat_ref.shape[0] - first - 8 * len(bits)
        if left:
            bits.append(jnp.zeros((left, 128), f32))
        flat_ref[first:] = jnp.concatenate(bits, axis=0).astype(bf16)
        if send_ref is None:
            out_ref[...] = flat_ref[...]
        else:
            half = out_ref.shape[0]
            core = me_ref[0] % 2
            out_ref[...] = flat_ref[pl.ds(pl.multiple_of(core * half, 16), half)]
            send_ref[...] = flat_ref[pl.ds(pl.multiple_of((1 - core) * half, 16), half)]


TOKEN = jax.ShapeDtypeStruct((8, 128), f32)


def unused():
    return pl.BlockSpec(memory_space=pl.ANY)


def call_sum(kernel, args, shape, after):
    count = len(args)
    return pl.pallas_call(
        lambda *refs: kernel(*refs[:count], *refs[count + len(after):]),
        in_specs=[whole()] * count + [unused()] * len(after),
        out_specs=whole(),
        out_shape=jax.ShapeDtypeStruct(shape, bf16),
        compiler_params=pltpu.CompilerParams(vmem_limit_bytes=SMALL_LIMIT),
        name="add_up",
    )(*args, *after)


def add(arrays, halves=None, after=()):
    shape = arrays[0].shape
    starts = [(n or 0) * shape[0] for n in halves or [0] * len(arrays)]

    def kernel(*refs):
        acc = None
        for first, ref in zip(starts, refs):
            term = ref[first:first + shape[0]].astype(f32)
            acc = term if acc is None else acc + term
        refs[-1][...] = acc.astype(bf16)

    return call_sum(kernel, arrays, shape, after)


def add_both(keep_w, core_w, far_e, core_e):
    def kernel(kw_ref, cw_ref, fe_ref, ce_ref, w_ref, e_ref):
        w_ref[...] = (kw_ref[...].astype(f32) + cw_ref[...].astype(f32)).astype(bf16)
        half = fe_ref.shape[0]
        e_ref[...] = (fe_ref[...].astype(f32) + ce_ref[half:].astype(f32)).astype(bf16)

    return pl.pallas_call(
        kernel,
        in_specs=[whole()] * 4,
        out_specs=[whole()] * 2,
        out_shape=[jax.ShapeDtypeStruct(t.shape, bf16) for t in (keep_w, far_e)],
        compiler_params=pltpu.CompilerParams(vmem_limit_bytes=SMALL_LIMIT),
        name="add_up",
    )(keep_w, core_w, far_e, core_e)


def total(x, after=(), copies=0):
    shape = x.shape[1:]

    def kernel(x_ref, o_ref):
        acc = x_ref[0].astype(f32)
        for n in range(1, x_ref.shape[0]):
            acc = acc + x_ref[n].astype(f32)
        acc = acc.astype(bf16)
        if copies:
            for n in range(copies):
                o_ref[n] = acc
        else:
            o_ref[...] = acc

    return call_sum(kernel, (x,), (copies,) + shape if copies else shape, after)


def attend_back(x, q, k, v, c, dc, p, part, me, per, vec=None, gbe=None, prev=None, devices=1, after=()):
    rows, length, width = x.shape
    lanes = width // 2
    heads = HEADS // 2
    wide = pl.BlockSpec((1, length, lanes), lambda r: (r, 0, part))
    args = [x, q, k, v, c, dc, p, me]
    specs = [wide] * 6 + [pl.BlockSpec((1, heads, length, length), lambda r: (r, part, 0, 0)),
                          pl.BlockSpec(memory_space=pltpu.SMEM)]
    flat = 9 * per + 32
    dqkv = jax.ShapeDtypeStruct((rows, 3, length, lanes), bf16)
    if prev is None:
        args += [vec, gbe]
        specs += [whole(), whole()]
        flat += 8 * (width // 128) + 64
        outs = [jax.ShapeDtypeStruct((flat, 128), bf16)]
        pick = lambda refs: (refs[8], refs[9], None) + refs[10:12] + (None,) + refs[12:]
    else:
        args.append(prev)
        specs.append(whole())
        flat = -(-(prev.shape[0] + flat) // (8 * devices)) * 8 * devices
        outs = [jax.ShapeDtypeStruct((flat // 2, 128), bf16)] * 2
        pick = lambda refs: (None, None, refs[8]) + refs[9:]
    return pl.pallas_call(
        lambda *refs: attend_back_kernel(lanes, per, *refs[:8], *pick(refs[:len(args)] + refs[len(args) + len(after):])),
        grid=(rows,),
        in_specs=specs + [unused()] * len(after),
        out_specs=[pl.BlockSpec((1, 3, length, lanes), lambda r: (r, 0, 0, 0))] + [whole()] * (len(outs) + 1),
        out_shape=[dqkv] + outs + [TOKEN],
        scratch_shapes=[
            pltpu.VMEM((3, lanes // per, per, 256), f32),
            pltpu.VMEM((8, lanes), f32),
            pltpu.VMEM((flat, 128), bf16),
        ],
        compiler_params=pltpu.CompilerParams(vmem_limit_bytes=VMEM_LIMIT),
        cost_estimate=pl.CostEstimate(flops=int(2e10), bytes_accessed=int(3e7), transcendentals=0),
        name="attend_back",
    )(*args, *after)


def input_grad_kernel(dh1_ref, d0_ref, d1_ref, wq_ref, wk_ref, wv_ref, dx_ref, token_ref, wpad):
    token_ref[...] = jnp.zeros(token_ref.shape, f32)
    groups, per = wq_ref.shape[0], wq_ref.shape[1]

    @pl.when(pl.program_id(0) == 0)
    def _():
        for j, w_ref in enumerate((wq_ref, wk_ref, wv_ref)):
            for g in range(groups):
                _, off = window(g, per)
                wpad[j, g] = pad_rows(pad_cols(w_ref[g], off), off)

    half = d0_ref.shape[3]
    parts = []
    for g in range(groups):
        base, _ = window(g, per)
        d_ref = (d0_ref, d1_ref)[base // half]
        acc = None
        for j in range(3):
            t = dot(d_ref[0, j, :, base % half:base % half + 256], wpad[j, g], NT)
            acc = t if acc is None else acc + t
        parts.append(acc)
    for n, col in enumerate(join_windows(parts)):
        lanes = slice(128 * n, 128 * n + 128)
        dx_ref[0, :, lanes] = (col + dh1_ref[0, :, lanes]).astype(bf16)


def input_grad(dh1, d0, d1, wq, wk, wv, half, prev=None, after=()):
    rows, length, width = dh1.shape
    count = rows // 2 if half == 0 else rows - rows // 2
    first = half * (rows // 2)
    wide = pl.BlockSpec((1, length, width), lambda r: (r + first, 0, 0))
    back = pl.BlockSpec((1, 3, length, width // 2), lambda r: (r + first, 0, 0, 0))
    args = [dh1, d0, d1, wq, wk, wv]
    extra = list(after)
    aliases = {}
    if prev is not None:
        aliases = {len(args) + len(extra): 0}
        extra.append(prev)
    return pl.pallas_call(
        lambda *refs: input_grad_kernel(*refs[:len(args)], *refs[len(args) + len(extra):]),
        grid=(count,),
        in_specs=[wide, back, back] + [full(wq.shape)] * 3 + [unused()] * len(extra),
        out_specs=[wide, whole()],
        out_shape=[jax.ShapeDtypeStruct((rows, length, width), bf16), TOKEN],
        input_output_aliases=aliases,
        scratch_shapes=[pltpu.VMEM((3, wq.shape[0], 256, 256), bf16)],
        compiler_params=pltpu.CompilerParams(vmem_limit_bytes=GRAD_LIMIT),
        cost_estimate=pl.CostEstimate(flops=int(5e9), bytes_accessed=int(1e7), transcendentals=0),
        name="input_grad",
    )(*args, *extra)


def unpack_kernel(order, me_ref, *refs):
    count = len(order)
    pieces, w_ref, own_ref, other_ref = refs[:count], *refs[count:count + 3]
    refs = refs[1:]
    gexp_ref, gshr_ref, gout_ref, gq_ref, gk_ref, gv_ref, gbe_ref = refs[count + 2:count + 9]
    vecs, (e_ref, flat_w, q_ref) = refs[count + 9:count + 17], refs[count + 17:]
    groups, per = gq_ref.shape[0], gq_ref.shape[1]
    width = gout_ref.shape[0]
    part = gexp_ref.shape[2]
    size = pieces[0].shape[0]
    for bit, piece in zip(order, pieces):
        place = pl.multiple_of((me_ref[1] ^ bit) * size, 8)
        e_ref[pl.ds(place, size)] = piece[...].astype(f32)
    size = w_ref.shape[1]
    for i in range(w_ref.shape[0]):
        place = i % 2 * (flat_w.shape[0] // 2) + i // 2 * size
        flat_w[place:place + size] = w_ref[i].astype(f32)
    for i in range(groups):
        first = 3 * per * i
        a = e_ref[first:first + per]
        b = e_ref[first + per:first + 2 * per]
        mix = e_ref[first + 2 * per:first + 3 * per]
        one = jnp.concatenate([a, mix], axis=1)
        two = jnp.concatenate([b, pltpu.roll(mix, 64, 1)], axis=1)
        if 2 * i < groups:
            gexp_ref[2 * i] = one[:, :part]
            gexp_ref[2 * i + 1] = two[:, :part]
        else:
            gshr_ref[2 * i - groups] = jnp.transpose(one)[:part]
            gshr_ref[2 * i - groups + 1] = jnp.transpose(two)[:part]
    half = own_ref.shape[0]
    core = me_ref[0] % 2
    q_ref[pl.ds(pl.multiple_of(core * half, 16), half)] = own_ref[...]
    q_ref[pl.ds(pl.multiple_of((1 - core) * half, 16), half)] = other_ref[...]
    for n in range(width // 128):
        gout_ref[:, 128 * n:128 * n + 128] = flat_w[width * n:width * n + width]
    tiles = width // 128
    used = 9 * per + 32
    start = used + 8 * tiles + 64
    got = {n: [] for n in range(8)}
    for half, flat in enumerate((q_ref[:start], q_ref[start:start + used])):
        for j, out in enumerate((gq_ref, gk_ref, gv_ref)):
            cols = [flat[per * (3 * j + n):per * (3 * j + n) + per].astype(f32) for n in range(3)]
            out[2 * half] = jnp.concatenate(cols[:2], axis=1)[:, :per]
            out[2 * half + 1] = pltpu.roll(jnp.concatenate(cols[1:], axis=1), 192, 1)[:, :per]
        ends = flat[9 * per:9 * per + 32].astype(f32)
        for m, bias in enumerate((QUERY_BIAS, VALUE_BIAS)):
            got[bias] += [ends[8 * n + m:8 * n + m + 1] for n in range(3)]
    rows = q_ref[used:used + 8 * tiles].astype(f32)
    for m in range(6):
        got[m] = [rows[8 * n + m:8 * n + m + 1] for n in range(tiles)]
    for m, vec in enumerate(vecs):
        vec[...] = jnp.concatenate(got[m], axis=1).reshape(width)
    blocks = q_ref[used + 8 * tiles:start].astype(f32)
    pick = blocks[:16]
    for f in range(1, 4):
        pick = jnp.where(me_ref[0] == f, blocks[16 * f:16 * f + 16], pick)
    gbe_ref[...] = jnp.concatenate([pick[:8], pick[8:]], axis=1)[:groups, :part]


def unpack(place, order, pieces, w, own, other, groups, per, width, part):
    shapes = [(groups, per, part), (groups, part, per), (width, width)] + [(groups, per, per)] * 3 + [
        (groups, part)] + [(width,)] * 8
    return pl.pallas_call(
        functools.partial(unpack_kernel, order),
        in_specs=[pl.BlockSpec(memory_space=pltpu.SMEM)] + [whole()] * (len(pieces) + 3),
        out_specs=[whole()] * len(shapes),
        out_shape=[jax.ShapeDtypeStruct(t, f32) for t in shapes],
        scratch_shapes=[pltpu.VMEM((len(pieces) * pieces[0].shape[0], 128), f32),
                        pltpu.VMEM((w.shape[0] * w.shape[1], 128), f32),
                        pltpu.VMEM((2 * own.shape[0], 128), bf16)],
        compiler_params=pltpu.CompilerParams(vmem_limit_bytes=SMALL_LIMIT),
        name="unpack",
    )(place, *pieces, w, own, other)


def exchange(x, axes, groups=None):
    return lax.all_to_all(x, axes, 0, 0, axis_index_groups=groups, tiled=True)


def on_device(
    inputs,
    doc_ids,
    cotangent,
    query_weight,
    query_bias,
    key_weight,
    value_weight,
    value_bias,
    out_weight,
    out_bias,
    mixed_gain,
    mixed_bias,
    expand_weight,
    expand_bias,
    shrink_weight,
    shrink_bias,
    final_gain,
    final_bias,
):
    micro, rows_dev, length, width = inputs.shape
    rows = micro * rows_dev
    groups, per, part = expand_weight.shape
    x = inputs.reshape(rows, length, width)
    docs = doc_ids.reshape(rows, 1, length)
    cot = cotangent.reshape(rows, length, width)
    dp = lax.axis_size("dp")
    everyone = ("dp", "ffn")
    count = 4 * dp
    me = lax.axis_index("ffn").astype(jnp.int32).reshape(1)
    like = [[4 * d + 2 * y + core for d in range(dp) for y in range(2)] for core in range(2)]

    def swap(array, bit):
        return lax.ppermute(array, "ffn", [(f, f ^ bit) for f in range(4)])

    bias = jnp.pad(expand_bias[:, None], ((0, 0), (0, 15), (0, part)))
    shard = jnp.concatenate([jnp.concatenate([expand_weight, shrink_weight], axis=2), bias], axis=1)
    shards = [shard] + [swap(shard, bit) for bit in (1, 2, 3)]
    q, k, v, c, r, p = attend(x, docs, query_weight, key_weight, value_weight, query_bias, value_bias)
    result, dh1, dc, near_e, far_e, send_e, keep_w, send_w, gvec, gbe = feed(
        me, x, c, r, cot, out_weight, shards, (out_bias, mixed_gain, mixed_bias, shrink_bias, final_gain, final_bias)
    )

    core_w = swap(send_w, 1)
    core_e = swap(send_e, 1)
    sum_w, far = add_both(keep_w, core_w, far_e, core_e)
    got_w = exchange(sum_w.reshape(2 * dp, -1, 128), everyone, like)
    far_got = swap(far, 2)
    back = functools.partial(attend_back, x, q, k, v, c, dc, p, me=me, per=per)
    d0, flat0, done_0 = back(part=0, vec=gvec, gbe=gbe, after=(far, sum_w))
    piece_w = total(got_w, after=(done_0,))
    sum_e = add((near_e, core_e, far_got), (None, 0, None), after=(piece_w,))
    got_e = exchange(sum_e.reshape(dp, -1, 128), "dp")
    all_w = lax.all_gather(piece_w, everyone)
    d1, keep_q, send_q, done_1 = back(part=1, prev=flat0, devices=count, after=(sum_e, piece_w))
    sum_q = add((keep_q, swap(send_q, 1)))
    piece_e = total(got_e, after=(done_1, sum_q))
    order, pieces = [0], [piece_e]
    bit = dp // 2
    while bit:
        pieces = pieces + [lax.ppermute(t, "dp", [(d, d ^ bit) for d in range(dp)]) for t in pieces]
        order = order + [n ^ bit for n in order]
        bit //= 2
    got_q = exchange(sum_q.reshape(2 * dp, -1, 128), everyone, like)
    back_weights = (query_weight, key_weight, value_weight)
    dx, _ = input_grad(dh1, d0, d1, *back_weights, half=0, after=(sum_q, pieces[1]))
    dx, done_2 = input_grad(dh1, d0, d1, *back_weights, half=1, prev=dx, after=pieces[2:4])
    piece_q = total(got_q, after=(done_2, all_w[0, :8], *pieces[4:]), copies=2 * dp)
    own_q = exchange(piece_q, everyone, like).reshape(-1, 128)
    other_q = swap(own_q, 1)
    place = jnp.stack([lax.axis_index("ffn"), lax.axis_index("dp")]).astype(jnp.int32)
    gexp, gshr, gout, gq, gk, gv, gbe, *vecs = unpack(
        place, order, pieces, all_w, own_q, other_q, groups, per, width, part
    )
    return (
        result.reshape(inputs.shape),
        dx.reshape(inputs.shape),
        gq,
        vecs[QUERY_BIAS],
        gk,
        gv,
        vecs[VALUE_BIAS],
        gout,
        vecs[OUT_BIAS],
        vecs[MIXED_GAIN],
        vecs[MIXED_BIAS],
        gexp,
        gbe,
        gshr,
        vecs[SHRINK_BIAS],
        vecs[FINAL_GAIN],
        vecs[FINAL_BIAS],
    )


def solution(mesh):
    in_specs = (
        P(None, ("dp", "ffn"), None, None),
        P(None, ("dp", "ffn"), None),
        P(None, ("dp", "ffn"), None, None),
        P(),
        P(),
        P(),
        P(),
        P(),
        P(),
        P(),
        P(),
        P(),
        P(None, None, "ffn"),
        P(None, "ffn"),
        P(None, "ffn", None),
        P(),
        P(),
        P(),
    )
    out_specs = (
        P(None, ("dp", "ffn"), None, None),
        P(None, ("dp", "ffn"), None, None),
        P(),
        P(),
        P(),
        P(),
        P(),
        P(),
        P(),
        P(),
        P(),
        P(None, None, "ffn"),
        P(None, "ffn"),
        P(None, "ffn", None),
        P(),
        P(),
        P(),
    )
    return jax.shard_map(
        on_device, mesh=mesh, in_specs=in_specs, out_specs=out_specs, check_vma=False
    )
```
